256 devices in a mesh: ctx: 32 (over x, y, core), head: 8 (over z).
Axes of the slice: x: 4, y: 4, z: 8, core: 2. Of those that a mesh axis runs over, the one named last changes fastest.
Arguments:
- queries: bfloat16 [4096, 16384], P(('ctx', 'head')), may hold values from -12 to 12
- keys: bfloat16 [4096, 1024], P(('ctx', 'head')), may hold values from -4.5 to 4.5
- values: bfloat16 [4096, 1024], P(('ctx', 'head')), may hold values from -5 to 5
- grad_out: bfloat16 [4096, 16384], P(('ctx', 'head')), may hold values from -5 to 5
- doc_lengths: int32 [8], replicated, may hold values from 1 to 2048, 4096 in all
- block_pairs: int32 [248, 2], replicated, may hold values from 0 to 31, as said below
- scale_index: int32 [2, 32, 8], replicated, may hold values from 0 to 15
- scale_table: float32 [2, 16], replicated, may hold values from 0.5 to 1.5
Outputs:
- attn_out: bfloat16 [4096, 16384], P(('ctx', 'head'))
- grad_queries: bfloat16 [4096, 16384], P(('ctx', 'head'))
- grad_keys: bfloat16 [4096, 1024], P(('ctx', 'head'))
- grad_values: bfloat16 [4096, 1024], P(('ctx', 'head'))
The draws below stay inside these ranges and needn't reach their ends.
Inputs may be any that keep to these rules, and one draw needn't show every extreme that they name: `doc_lengths`: the 8 lengths sum to 4096; the longest is exactly 2048. `block_pairs`: each row is a pair (query block, key block) of blocks of 128 tokens with the key block below the query block; the 248 rows are distinct.
All inputs are finite; a program needn't handle non-finite values.
Results may differ from the reference program's by a relative error of at most 0.014.
Values may be sent and summed in bfloat16 or wider, within the bound.
A program may use at most 64 MiB of HBM per device.

```python
import math
import jax
import jax.numpy as jnp
import numpy as np
from jax import lax

QH = 128
KVH = 8
HD = 128
SEQ = 4096
BLK = 128
NBLK = 32
NDOC = 8
MAXDOC = 2048
NPAIR = 248
NSCALE = 16


def draw_queries(key, part):
    key = jax.random.fold_in(key, 21)
    samples = jnp.clip(jax.random.normal(key, (SEQ, QH * HD), jnp.float32), -4.0, 4.0)
    return samples.astype(jnp.bfloat16)


def draw_keys(key, part):
    key = jax.random.fold_in(key, 22)
    samples = jnp.clip(jax.random.normal(key, (SEQ, KVH * HD), jnp.float32), -4.0, 4.0)
    return samples.astype(jnp.bfloat16)


def draw_block_pairs(key, part):
    key = jax.random.fold_in(key, 23)
    lower_q, lower_k = jnp.tril_indices(NBLK, -1)
    chosen = jax.random.permutation(key, lower_q.shape[0])[:NPAIR]
    return jnp.stack([lower_q[chosen], lower_k[chosen]], axis=1).astype(jnp.int32)


def plant(values, key, low, top_value):
    spot = [jax.random.randint(jax.random.fold_in(key, axis), (), 0, length) for axis, length in enumerate(values.shape)]
    widest = values.shape.index(max(values.shape))
    neighbour = spot[:widest] + [(spot[widest] + 1) % values.shape[widest]] + spot[widest + 1:]
    return values.at[tuple(spot)].set(low).at[tuple(neighbour)].set(top_value)


def steps_of(rng, shape, cuts, smallest, top_value):
    gain = 1.0
    for dim, parts in cuts:
        draws = jax.random.uniform(jax.random.fold_in(jax.random.fold_in(rng, 6), dim), (parts,), jnp.float32, smallest / len(cuts), top_value / len(cuts))
        gain = gain * jnp.repeat(jnp.exp(draws), shape[dim] // parts).reshape((-1,) + (1,) * (len(shape) - 1 - dim))
    return gain


def split_up(amount, total, reach, lean):
    weights = [(1 << 20) // math.isqrt(grade ** lean) + 1 for grade in range(2, amount + 1)]
    rest, counts = total - reach - (amount - 1), [1] * (amount - 1)
    while rest > 0:
        candidates = [i for i in range(amount - 1) if counts[i] < reach]
        whole, remaining = sum([weights[i] for i in candidates]), rest
        for i in candidates:
            more = min(reach - counts[i], max(1, remaining * weights[i] // whole), rest)
            counts[i] = counts[i] + more
            rest = rest - more
    return np.array([reach] + counts)


def uneven_parts(own_key, amount, total, reach, skew):
    if amount == 2:
        one = jax.random.randint(own_key, (), max(1, total - reach), min(reach, total - 1) + 1)
        return jnp.stack([one, total - one])
    tallies = jnp.asarray(split_up(amount, total, reach, skew), jnp.int32)
    couples = (amount - 1) // 2
    donor, receiver = tallies[1:1 + 2 * couples:2], tallies[2:2 + 2 * couples:2]
    slack = jnp.minimum(donor - 1, reach - receiver)
    moved = jax.random.randint(jax.random.fold_in(own_key, 1), (couples,), 0, 1 << 20) % (slack + 1)
    tallies = tallies.at[1:1 + 2 * couples:2].set(donor - moved).at[2:2 + 2 * couples:2].set(receiver + moved)
    return tallies[jax.random.permutation(jax.random.fold_in(own_key, 2), amount)]


def normal_values(own_key, extent, scale, limit, cuts=(), held_as=jnp.bfloat16):
    factor_of = steps_of(own_key, extent, cuts, -0.22, 0.18) if cuts else 1.0
    entries = jax.random.normal(own_key, extent, jnp.float32) * scale * factor_of
    return jnp.minimum(jnp.maximum(entries, -limit), limit).astype(held_as)


def setup_inputs(seed: int = 0) -> dict:
    key_of = jax.random.split(jax.random.key(seed), 9)
    return {
        "queries": draw_queries(jax.random.fold_in(key_of[8], 71), 0),
        "keys": draw_keys(jax.random.fold_in(key_of[8], 71), 0),
        "values": normal_values(key_of[2], (SEQ, KVH * HD), 1.0, 5.0, ((0, 256),)),
        "grad_out": normal_values(key_of[3], (SEQ, QH * HD), 1.0, 5.0, ((0, 256),)),
        "doc_lengths": uneven_parts(key_of[4], NDOC, SEQ, MAXDOC, 2).astype(jnp.int32),
        "block_pairs": draw_block_pairs(jax.random.fold_in(key_of[8], 71), 0),
        "scale_index": plant(jax.random.randint(key_of[6], (2, NBLK, KVH), 0, NSCALE), jax.random.fold_in(key_of[6], 1), 0, NSCALE - 1).astype(jnp.int32),
        "scale_table": jnp.clip(jnp.exp(jax.random.uniform(key_of[7], (2, NSCALE), jnp.float32, math.log(0.5), math.log(1.5))), 0.5, 1.5),
    }


neg_big = -1e+30
rope_base = 500000.0

def stored(values_in):
    return lax.optimization_barrier(values_in.astype(jnp.bfloat16))

def rotate(vectors, position, turning):
    half_width = vectors.shape[-1] // 2
    frequency = jnp.exp(jnp.arange(half_width, dtype=jnp.float32) * (-2.0 * math.log(rope_base) / vectors.shape[-1]))
    angles = position.astype(jnp.float32)[:, None] * frequency[None, :]
    cosine = jnp.cos(angles)[:, None, :]
    sine_part = turning * jnp.sin(angles)[:, None, :]
    first_half = vectors[..., :half_width]
    second = vectors[..., half_width:]
    return jnp.concatenate([first_half * cosine - second * sine_part, second * cosine + first_half * sine_part], axis=-1)

def doc_and_pos(token_index, doc_lengths):
    doc_ends = jnp.cumsum(doc_lengths).astype(jnp.int32)
    before = (doc_ends[None, :] <= token_index[:, None]).astype(jnp.int32)
    doc_id = lax.optimization_barrier(jnp.sum(before, axis=1)).astype(jnp.int32)
    doc_start = lax.optimization_barrier(jnp.sum(before * doc_lengths[None, :], axis=1)).astype(jnp.int32)
    return (doc_id, token_index - doc_start)

def block_scales(scale_index, scale_table, table_row):
    options = jnp.arange(scale_table.shape[1], dtype=jnp.int32)
    one_hot = (scale_index[table_row][..., None] == options).astype(jnp.float32)
    return lax.optimization_barrier(jnp.sum(one_hot * scale_table[table_row], axis=-1))

def reference(queries, keys, values, grad_out, doc_lengths, block_pairs, scale_index, scale_table):
    seq_len = queries.shape[0]
    per_group = QH // KVH
    score_scale = 1.0 / math.sqrt(HD)
    highest = lax.Precision.HIGHEST
    token_index = jnp.arange(seq_len, dtype=jnp.int32)
    doc_id, position = doc_and_pos(token_index, doc_lengths)
    block_of = token_index // BLK
    block_count = seq_len // BLK
    listed = jnp.zeros((block_count, block_count), jnp.int32).at[block_pairs[:, 0], block_pairs[:, 1]].set(1)
    key_scale = jnp.repeat(block_scales(scale_index, scale_table, 0), BLK, axis=0)
    value_scale = jnp.repeat(block_scales(scale_index, scale_table, 1), BLK, axis=0)
    q_rot = stored(rotate(queries.reshape(seq_len, QH, HD).astype(jnp.float32), position, 1.0))
    k_rot = stored(rotate(keys.reshape(seq_len, KVH, HD).astype(jnp.float32) * key_scale[:, :, None], position, 1.0))
    v_scaled = stored(values.reshape(seq_len, KVH, HD).astype(jnp.float32) * value_scale[:, :, None])
    grad_rows = grad_out.reshape(seq_len, QH, HD)
    query_rows = math.gcd(seq_len, 512)
    row_count = seq_len // query_rows

    def one_head(kv_head):
        q_head = lax.dynamic_slice_in_dim(q_rot, kv_head * per_group, per_group, 1).astype(jnp.float32)
        go_head = lax.dynamic_slice_in_dim(grad_rows, kv_head * per_group, per_group, 1).astype(jnp.float32)
        k_head = lax.dynamic_index_in_dim(k_rot, kv_head, 1, keepdims=False).astype(jnp.float32)
        v_head = lax.dynamic_index_in_dim(v_scaled, kv_head, 1, keepdims=False).astype(jnp.float32)

        def row_step(running, row_block):
            grad_k, grad_v = running
            first_row = row_block * query_rows
            q_block = lax.dynamic_slice_in_dim(q_head, first_row, query_rows, 0)
            go_block = lax.dynamic_slice_in_dim(go_head, first_row, query_rows, 0)
            q_idx = first_row + jnp.arange(query_rows, dtype=jnp.int32)
            q_doc = lax.dynamic_slice_in_dim(doc_id, first_row, query_rows, 0)
            q_block_of = q_idx // BLK
            allowed = (token_index[None, :] <= q_idx[:, None]) & (doc_id[None, :] == q_doc[:, None])
            allowed = allowed & ((block_of[None, :] == q_block_of[:, None]) | (listed[q_block_of][:, block_of] > 0))
            scores = jnp.einsum('qgd,kd->gqk', q_block, k_head, precision=highest) * score_scale
            scores = jnp.where(allowed[None], scores, neg_big)
            row_max = lax.optimization_barrier(jnp.max(scores, axis=-1, keepdims=True))
            row_sum = lax.optimization_barrier(jnp.sum(jnp.where(allowed[None], jnp.exp(scores - row_max), 0.0), axis=-1, keepdims=True))
            lse = row_max + jnp.log(row_sum)
            probs = jnp.where(allowed[None], jnp.exp(scores - lse), 0.0)
            probs_b = stored(probs).astype(jnp.float32)
            out_block = stored(jnp.einsum('gqk,kd->qgd', probs_b, v_head, precision=highest))
            delta = lax.optimization_barrier(jnp.sum(go_block * out_block.astype(jnp.float32), axis=-1)).T
            grad_probs = jnp.einsum('qgd,kd->gqk', go_block, v_head, precision=highest)
            grad_scores = probs * (grad_probs - delta[:, :, None])
            grad_sb = stored(grad_scores).astype(jnp.float32)
            dq_block = jnp.einsum('gqk,kd->qgd', grad_sb, k_head, precision=highest) * score_scale
            grad_k = grad_k + jnp.einsum('gqk,qgd->kd', grad_sb, q_block, precision=highest) * score_scale
            grad_v = grad_v + jnp.einsum('gqk,qgd->kd', probs_b, go_block, precision=highest)
            return ((grad_k, grad_v), (out_block, dq_block))
        zeros_kv = jnp.zeros((seq_len, HD), jnp.float32)
        (grad_k, grad_v), (out_parts, dq_parts) = lax.scan(row_step, (zeros_kv, zeros_kv), jnp.arange(row_count, dtype=jnp.int32))
        return (out_parts.reshape(seq_len, per_group, HD), dq_parts.reshape(seq_len, per_group, HD), grad_k, grad_v)
    outputs, dq_all, grad_k, grad_v = lax.map(one_head, jnp.arange(KVH, dtype=jnp.int32))
    attn_out = outputs.transpose(1, 0, 2, 3).reshape(seq_len, QH * HD)
    dq_rot = dq_all.transpose(1, 0, 2, 3).reshape(seq_len, QH, HD)
    grad_queries = rotate(dq_rot, position, -1.0).astype(jnp.bfloat16).reshape(seq_len, QH * HD)
    grad_keys = (key_scale[:, :, None] * rotate(grad_k.transpose(1, 0, 2), position, -1.0)).astype(jnp.bfloat16).reshape(seq_len, KVH * HD)
    grad_values = (value_scale[:, :, None] * grad_v.transpose(1, 0, 2)).astype(jnp.bfloat16).reshape(seq_len, KVH * HD)
    return (attn_out, grad_queries, grad_keys, grad_values)
```

```python
import functools
import math

import jax
import jax.numpy as jnp
import numpy as np
from jax import lax
from jax.experimental import pallas as pl
from jax.experimental.pallas import tpu as pltpu
from jax.sharding import PartitionSpec as P

HD = 128
BLK = 128
ROWS = 16
GRP = 16
NX, NY, NC, NZ = 4, 4, 2, 8
NP = NX * NC
NBLK = 32
NDOC = 8
WIDE = GRP * HD
NEG = -1e30
SCALE = 1.0 / math.sqrt(HD)
EXP2_SCALE = SCALE * math.log2(math.e)
MESH = pl.DeviceIdType.MESH
BF = jnp.bfloat16
F32 = jnp.float32
VMEM_LIMIT = 56 * 1024 * 1024


def place():
    ctx = lax.axis_index("ctx")
    return ctx // (NY * NC), (ctx // NC) % NY, ctx % NC, lax.axis_index("head")


def device(xx, yy, cc, zz):
    return {"ctx": xx * (NY * NC) + yy * NC + cc, "head": zz}


def peer(p, y, z):
    return device(p // NC, y, p % NC, z)


def remote(src, dst, send_sem, recv_sem, dev):
    return pltpu.make_async_remote_copy(
        src_ref=src, dst_ref=dst, send_sem=send_sem, recv_sem=recv_sem, device_id=dev, device_id_type=MESH
    )


def enter(me, y, z, x, c):
    barrier = pltpu.get_barrier_semaphore()
    for d in range(1, NP):
        pl.semaphore_signal(barrier, inc=1, device_id=peer((me + d) % NP, y, z), device_id_type=MESH)
    for d in range(1, NY):
        pl.semaphore_signal(barrier, inc=1, device_id=device(x, (y + d) % NY, c, z), device_id_type=MESH)
    for d in (1, NZ - 1):
        pl.semaphore_signal(barrier, inc=1, device_id=device(x, y, c, (z + d) % NZ), device_id_type=MESH)
    return barrier


N_PARTNERS = NP - 1 + NY - 1 + 2


def turn(x, cosine, sine):
    return x * cosine + pltpu.roll(x, HD // 2, 1) * sine


def gather_kernel(
    q_ref, k_ref, v_ref, go_ref, doc_ref, pairs_ref, sidx_ref, stab_ref, freq_ref,
    qx_ref, gox_ref, ka_ref, va_ref, lists_ref, cs_ref,
    qs, ks, vs,
    q_s, q_r, go_s, go_r, k_s, k_r, v_s, v_r, ky_s, ky_r, kzr_s, kzr_r, kzl_s, kzl_r,
    vzr_s, vzr_r, vzl_s, vzl_r, vy_s, vy_r, own_s,
):
    x, y, c, z = place()
    me = NC * x + c
    block = lax.axis_index("ctx")
    barrier = enter(me, y, z, x, c)

    token = BLK * block + ROWS * z + lax.broadcasted_iota(jnp.int32, (ROWS, HD), 0)
    start = jnp.zeros((ROWS, HD), jnp.int32)
    end = 0
    for d in range(NDOC):
        end = end + doc_ref[d]
        start = start + jnp.where(token >= end, doc_ref[d], 0)
    angle = (token - start).astype(F32) * freq_ref[0:1, :]
    cosine = jnp.cos(angle)
    sine = jnp.sin(angle)
    sine = jnp.where(lax.broadcasted_iota(jnp.int32, (ROWS, HD), 1) < HD // 2, -sine, sine)
    cs_ref[0] = cosine
    cs_ref[1] = sine

    for h in range(NP):
        cols = slice(h * HD, (h + 1) * HD)
        key_scale = stab_ref[0, sidx_ref[0, block, h]]
        value_scale = stab_ref[1, sidx_ref[1, block, h]]
        ks[h] = turn(k_ref[:, cols].astype(F32) * key_scale, cosine, sine).astype(BF)
        vs[h] = (v_ref[:, cols].astype(F32) * value_scale).astype(BF)

    pl.semaphore_wait(barrier, N_PARTNERS)

    def kv_copies(p):
        return (
            remote(ks.at[p], ka_ref.at[z, y, me], k_s.at[p], k_r.at[me], peer(p, y, z)),
            remote(vs.at[p], va_ref.at[y, z, me], v_s.at[p], v_r.at[me], peer(p, y, z)),
        )

    def kv_arrivals(p):
        return (
            remote(ks.at[p], ka_ref.at[z, y, p], k_s.at[p], k_r.at[p], peer(p, y, z)),
            remote(vs.at[p], va_ref.at[y, z, p], v_s.at[p], v_r.at[p], peer(p, y, z)),
        )

    def go_cols(p):
        return go_ref.at[:, pl.ds(pl.multiple_of(p * WIDE, WIDE), WIDE)]

    def go_copy(p, slot):
        return remote(go_cols(p), gox_ref.at[slot], go_s.at[p], go_r.at[slot], peer(p, y, z))

    def q_copy(p, slot):
        return remote(qs.at[p], qx_ref.at[slot], q_s.at[p], q_r.at[slot], peer(p, y, z))

    def each_peer(fn):
        def step(d, carry):
            fn((me + d) % NP)
            return carry

        lax.fori_loop(1, NP, step, 0)

    def start_kv(p):
        for copy in kv_copies(p):
            copy.start()

    each_peer(start_kv)
    each_peer(lambda p: go_copy(p, me).start())
    own_go = pltpu.make_async_copy(go_cols(me), gox_ref.at[me], own_s)
    own_go.start()
    ka_ref[z, y, me] = ks[me]
    va_ref[y, z, me] = vs[me]

    def rotate_q(p):
        for h in range(GRP):
            cols = pl.ds(pl.multiple_of(p * WIDE + h * HD, HD), HD)
            qs[p, :, h * HD:(h + 1) * HD] = turn(q_ref[:, cols].astype(F32), cosine, sine).astype(BF)

    def rotate_and_send(p):
        rotate_q(p)
        q_copy(p, me).start()

    each_peer(rotate_and_send)
    rotate_q(me)
    qx_ref[me] = qs[me]

    right, left = (z + 1) % NZ, (z + NZ - 1) % NZ
    to_right, to_left = device(x, y, c, right), device(x, y, c, left)

    def k_ring(s, sending):
        zr, zl = ((z + NZ - s) % NZ, (z + s) % NZ) if sending else ((z + NZ - s - 1) % NZ, (z + s + 1) % NZ)
        if s < 3:
            ref_r, ref_l = ka_ref.at[zr], ka_ref.at[zl]
        else:
            ref_r, ref_l = ka_ref.at[zr, pl.ds(0, NY // 2)], ka_ref.at[zl, pl.ds(NY // 2, NY // 2)]
        return (
            remote(ref_r, ref_r, kzr_s.at[s], kzr_r.at[s], to_right),
            remote(ref_l, ref_l, kzl_s.at[s], kzl_r.at[s], to_left),
        )

    def v_ring(s, sending):
        zr, zl = ((z + NZ - s) % NZ, (z + s) % NZ) if sending else ((z + NZ - s - 1) % NZ, (z + s + 1) % NZ)
        if s < 3:
            ref_r, ref_l = va_ref.at[y, zr], va_ref.at[y, zl]
        else:
            ref_r, ref_l = va_ref.at[y, zr, pl.ds(0, NP // 2)], va_ref.at[y, zl, pl.ds(NP // 2, NP // 2)]
        return (
            remote(ref_r, ref_r, vzr_s.at[s], vzr_r.at[s], to_right),
            remote(ref_l, ref_l, vzl_s.at[s], vzl_r.at[s], to_left),
        )

    def v_spread(zz):
        for d in (2, 1, 3):
            remote(
                va_ref.at[y, zz], va_ref.at[y, zz], vy_s.at[d, zz], vy_r.at[y, zz], device(x, (y + d) % NY, c, z)
            ).start()

    def k_spread(d, yy):
        ref = ka_ref.at[z, yy]
        return remote(ref, ref, ky_s.at[d], ky_r.at[yy], device(x, (y + d) % NY, c, z))

    def begin(pair):
        for copy in pair:
            copy.start()

    def arrive(pair):
        for copy in pair:
            copy.wait_recv()

    each_peer(lambda p: arrive(kv_arrivals(p)))
    begin(v_ring(0, True))
    for d in (2, 1, 3):
        k_spread(d, y).start()
    v_spread(z)

    lane = lax.broadcasted_iota(jnp.int32, (NP, BLK), 1)
    row = lax.broadcasted_iota(jnp.int32, (NP, BLK), 0)
    own_block = NY * NC * (row // NC) + NC * y + row % NC
    first = BLK * own_block + ROWS * z
    doc_start = jnp.zeros((NP, BLK), jnp.int32)
    end = 0
    for d in range(NDOC):
        end = end + doc_ref[d]
        doc_start = doc_start + jnp.where(first >= end, doc_ref[d], 0)
    pairs = pairs_ref[...]
    pair_lane = lax.broadcasted_iota(jnp.int32, (pairs.shape[0], BLK), 1)
    lane_block = jnp.where(pair_lane < NP, NY * NC * (pair_lane // NC) + NC * y + pair_lane % NC, -1)
    pair_q = (pairs[:, 0:1] == lane_block).astype(F32)
    pair_k = (pairs[:, 1:2] == pair_lane).astype(F32)
    listed = lax.dot_general(pair_q, pair_k, (((0,), (0,)), ((), ())), preferred_element_type=F32)[:NP]
    wanted = ((listed > 0.5) | (lane == own_block)) & (BLK * lane + BLK - 1 >= doc_start) & (lane <= own_block)
    wanted_f = wanted.astype(F32)
    upper = (
        lax.broadcasted_iota(jnp.int32, (BLK, BLK), 0) <= lax.broadcasted_iota(jnp.int32, (BLK, BLK), 1)
    ).astype(F32)
    rank = jnp.dot(wanted_f, upper, preferred_element_type=F32)
    lane_f = lane.astype(F32)

    def list_step(r, out):
        hit = wanted & (rank.astype(jnp.int32) == r + 1)
        entry = jnp.sum(jnp.where(hit, lane_f, 0.0), axis=1, keepdims=True)
        return jnp.where(lane == r, entry, out)

    out = lax.fori_loop(0, NBLK, list_step, jnp.zeros((NP, BLK), F32))
    out = jnp.where(lane == BLK - 1, jnp.sum(wanted_f, axis=1, keepdims=True), out)
    lists_ref[...] = out.astype(jnp.int32)

    def v_step(s):
        arrive(v_ring(s - 1, False))
        if s < 4:
            begin(v_ring(s, True))
            v_spread((z + NZ - s) % NZ)
            v_spread((z + s) % NZ)
        else:
            v_spread((z + 4) % NZ)

    def k_step(s):
        arrive(k_ring(s - 1, False))
        if s < 4:
            begin(k_ring(s, True))

    v_step(1)
    for d in range(1, NY):
        k_spread(d, (y + d) % NY).wait_recv()
    begin(k_ring(0, True))
    v_step(2)
    v_step(3)
    k_step(1)
    v_step(4)
    k_step(2)
    k_step(3)
    k_step(4)

    def spread_in(zz, carry):
        for d in range(1, NY):
            yy = (y + d) % NY
            remote(
                va_ref.at[yy, zz], va_ref.at[yy, zz], vy_s.at[d, zz], vy_r.at[yy, zz], device(x, yy, c, z)
            ).wait_recv()
        return carry

    lax.fori_loop(0, NZ, spread_in, 0)

    def qgo_in(p):
        go_copy(p, p).wait_recv()
        q_copy(p, p).wait_recv()

    each_peer(qgo_in)
    own_go.wait()

    def sent(p):
        for copy in kv_copies(p):
            copy.wait_send()
        go_copy(p, me).wait_send()
        q_copy(p, me).wait_send()

    each_peer(sent)
    for d in range(1, NY):
        k_spread(d, y).wait_send()
    for s in range(4):
        for copy in k_ring(s, True) + v_ring(s, True):
            copy.wait_send()

    def spread_sent(zz, carry):
        for d in range(1, NY):
            remote(
                va_ref.at[y, zz], va_ref.at[y, zz], vy_s.at[d, zz], vy_r.at[y, zz], device(x, (y + d) % NY, c, z)
            ).wait_send()
        return carry

    lax.fori_loop(0, NZ, spread_sent, 0)


def heads_to_rows(ref, i):
    return jnp.concatenate([ref[i, :, h * HD:(h + 1) * HD] for h in range(GRP)], axis=0)


def rows_to_heads(ref, i, rows):
    for h in range(GRP):
        ref[i, :, h * HD:(h + 1) * HD] = rows[h * ROWS:(h + 1) * ROWS]


def attend_kernel(
    lists_ref, doc_ref, q_ref, go_ref, k_ref, v_ref, o_ref, dq_ref, dk_ref, dv_ref, s_ref, dk_acc, dv_acc
):
    _, y, _, z = place()
    rows = GRP * ROWS
    dk_acc[...] = jnp.zeros_like(dk_acc)
    dv_acc[...] = jnp.zeros_like(dv_acc)
    key_row = lax.broadcasted_iota(jnp.int32, (BLK, rows), 0)
    lane = lax.broadcasted_iota(jnp.int32, (1, rows), 1)
    nt = (((1,), (1,)), ((), ()))
    tn = (((0,), (0,)), ((), ()))

    def group(i, carry):
        own = NY * NC * (i // NC) + NC * y + i % NC
        count = lists_ref[i, BLK - 1]
        queries = heads_to_rows(q_ref, i)
        grads = heads_to_rows(go_ref, i)
        token = BLK * own + ROWS * z + lane % ROWS
        start = jnp.zeros((1, rows), jnp.int32)
        end = 0
        for d in range(NDOC):
            end = end + doc_ref[d]
            start = start + jnp.where(token >= end, doc_ref[d], 0)

        def spot(t):
            b = lists_ref[i, t]
            return b, (b // NC) % NY, (b // (NY * NC)) * NC + b % NC

        def keys_at(yb, ib):
            return k_ref[:, yb, ib].reshape(BLK, HD)

        def values_at(yb, ib):
            return v_ref[yb, :, ib].reshape(BLK, HD)

        def score_step(t, top):
            b, yb, ib = spot(t)
            scores = lax.dot_general(keys_at(yb, ib), queries, nt, preferred_element_type=F32)
            allowed = (key_row >= start - BLK * b) & (key_row <= token - BLK * b)
            scores = jnp.where(allowed, scores, NEG)
            s_ref[t] = scores
            return jnp.maximum(top, jnp.max(scores.reshape(BLK // 8, 8, rows), axis=0))

        top = lax.fori_loop(0, count, score_step, jnp.full((8, rows), NEG, F32))
        top = jnp.max(top, axis=0, keepdims=True)

        def out_step(t, acc):
            total, mixed = acc
            _, yb, ib = spot(t)
            weights = jnp.exp2((s_ref[t] - top) * EXP2_SCALE)
            s_ref[t] = weights
            total = total + jnp.sum(weights.reshape(BLK // 8, 8, rows), axis=0)
            mixed = mixed + lax.dot_general(
                values_at(yb, ib), weights.astype(BF), tn, preferred_element_type=F32
            )
            return total, mixed

        total, mixed = lax.fori_loop(
            0, count, out_step, (jnp.zeros((8, rows), F32), jnp.zeros((HD, rows), F32))
        )
        inverse = 1.0 / jnp.sum(total, axis=0, keepdims=True)
        mixed = (mixed * inverse).astype(BF).astype(F32)
        rows_to_heads(o_ref, i, mixed.T.astype(BF))
        delta = jnp.sum(mixed * grads.astype(F32).T, axis=0, keepdims=True)

        def grad_step(t, dq):
            _, yb, ib = spot(t)
            probs = s_ref[t] * inverse
            grad_probs = lax.dot_general(values_at(yb, ib), grads, nt, preferred_element_type=F32)
            grad_scores = (probs * (grad_probs - delta)).astype(BF)
            dv = jnp.dot(probs.astype(BF), grads, preferred_element_type=F32)
            dk = jnp.dot(grad_scores, queries, preferred_element_type=F32)
            dv_acc[yb, :, ib] += dv.reshape(NZ, ROWS, HD)
            dk_acc[:, yb, ib] += dk.reshape(NZ, ROWS, HD)
            return dq + lax.dot_general(keys_at(yb, ib), grad_scores, tn, preferred_element_type=F32)

        dq = lax.fori_loop(0, count, grad_step, jnp.zeros((HD, rows), F32))
        rows_to_heads(dq_ref, i, (dq * SCALE).T.astype(BF))
        return carry

    lax.fori_loop(0, NP, group, 0)

    def finish(zz, carry):
        dk_ref[zz] = (dk_acc[zz] * SCALE).astype(BF)
        for yy in range(NY):
            dv_ref[yy, zz] = dv_acc[yy, zz].astype(BF)
        return carry

    lax.fori_loop(0, NZ, finish, 0)


def scatter_kernel(
    o_ref, dq_ref, dk_ref, dv_ref, cs_ref, sidx_ref, stab_ref,
    ao_ref, gq_ref, gk_ref, gv_ref,
    dqx, kr_out, kl_out, kr_in, kl_in, vr_out, vl_out, vr_in, vl_in, ky_out, ky_in, vy_in, kv_out, kv_in,
    o_s, o_r, q_s, q_r, kzr_s, kzr_r, kzl_s, kzl_r, vzr_s, vzr_r, vzl_s, vzl_r,
    ky_s, ky_r, vy_s, vy_r, kv_s, kv_r, own_s,
):
    x, y, c, z = place()
    me = NC * x + c
    block = lax.axis_index("ctx")
    barrier = enter(me, y, z, x, c)
    pl.semaphore_wait(barrier, N_PARTNERS)

    def each_peer(fn):
        def step(d, carry):
            fn((me + d) % NP)
            return carry

        lax.fori_loop(1, NP, step, 0)

    right, left = (z + 1) % NZ, (z + NZ - 1) % NZ
    to_right, to_left = device(x, y, c, right), device(x, y, c, left)

    def head_cols(ref, g):
        return ref.at[:, pl.ds(pl.multiple_of(g * WIDE, WIDE), WIDE)]

    def o_copy(p, slot):
        return remote(o_ref.at[p], head_cols(ao_ref, slot), o_s.at[p], o_r.at[slot], peer(p, y, z))

    def q_copy(p, slot):
        return remote(dq_ref.at[p], dqx.at[slot], q_s.at[p], q_r.at[slot], peer(p, y, z))

    def vy_copy(d, zz, slot):
        yy = (y + d) % NY
        return remote(dv_ref.at[yy, zz], vy_in.at[slot, zz], vy_s.at[d, zz], vy_r.at[slot, zz], device(x, yy, c, z))

    def ring(s, out_r, out_l, in_r, in_l, r_s, r_r, l_s, l_r, cut):
        def piece(ref, low):
            return ref.at[s] if s else ref.at[s, pl.ds(0 if low else cut, cut)]

        return (
            remote(piece(out_r, True), piece(in_r, True), r_s.at[s], r_r.at[s], to_right),
            remote(piece(out_l, False), piece(in_l, False), l_s.at[s], l_r.at[s], to_left),
        )

    def k_ring(s):
        return ring(s, kr_out, kl_out, kr_in, kl_in, kzr_s, kzr_r, kzl_s, kzl_r, NY // 2)

    def v_ring(s):
        return ring(s, vr_out, vl_out, vr_in, vl_in, vzr_s, vzr_r, vzl_s, vzl_r, NP // 2)

    def begin(pair):
        for copy in pair:
            copy.start()

    def arrive(pair):
        for copy in pair:
            copy.wait_recv()

    def k_part(zz):
        return dk_ref[zz].astype(F32)

    def v_part(zz):
        total = dv_ref[y, zz].astype(F32)
        for d in range(1, NY):
            total = total + vy_in[(y + d) % NY, zz].astype(F32)
        return total

    def ring_step(s, part, out_r, out_l, in_r, in_l, copies, cut):
        if s == 0:
            whole = part((z + 4) % NZ).astype(BF)
            out_r[0, :cut] = whole[:cut]
            out_l[0, cut:] = whole[cut:]
            begin(copies(0))
            return
        arrive(copies(s - 1))
        mine_r, mine_l = part((z + 4 - s) % NZ), part((z + 4 + s) % NZ)
        if s == 1:
            out_r[1, :cut] = (mine_r[:cut] + in_r[0, :cut].astype(F32)).astype(BF)
            out_r[1, cut:] = mine_r[cut:].astype(BF)
            out_l[1, :cut] = mine_l[:cut].astype(BF)
            out_l[1, cut:] = (mine_l[cut:] + in_l[0, cut:].astype(F32)).astype(BF)
        else:
            out_r[s] = (mine_r + in_r[s - 1].astype(F32)).astype(BF)
            out_l[s] = (mine_l + in_l[s - 1].astype(F32)).astype(BF)
        begin(copies(s))

    def k_step(s):
        ring_step(s, k_part, kr_out, kl_out, kr_in, kl_in, k_ring, NY // 2)

    def wait_vy(zz):
        for d in range(1, NY):
            vy_copy(d, zz, (y + d) % NY).wait_recv()

    def v_step(s):
        if s == 0:
            wait_vy((z + 4) % NZ)
        else:
            wait_vy((z + 4 - s) % NZ)
            wait_vy((z + 4 + s) % NZ)
        ring_step(s, v_part, vr_out, vl_out, vr_in, vl_in, v_ring, NP // 2)

    k_step(0)
    for off in (4, 3, 5, 2, 6, 1, 7, 0):
        for d in (2, 1, 3):
            vy_copy(d, (z + off) % NZ, y).start()

    each_peer(lambda p: o_copy(p, me).start())
    each_peer(lambda p: q_copy(p, me).start())
    own_o = pltpu.make_async_copy(o_ref.at[me], head_cols(ao_ref, me), own_s)
    own_o.start()
    dqx[me] = dq_ref[me]

    k_step(1)
    v_step(0)
    k_step(2)
    v_step(1)
    v_step(2)
    k_step(3)
    v_step(3)

    def ky_copy(d, slot):
        yy = (y + d) % NY
        return remote(ky_out.at[yy], ky_in.at[slot], ky_s.at[d], ky_r.at[slot], device(x, yy, c, z))

    def kv_copy(p, which, slot):
        return remote(
            kv_out.at[which, p], kv_in.at[which, slot], kv_s.at[which, p], kv_r.at[which, slot], peer(p, y, z)
        )

    arrive(k_ring(3))
    k_total = k_part(z) + kr_in[3].astype(F32) + kl_in[3].astype(F32)
    ky_out[...] = k_total.astype(BF)
    for d in (2, 1, 3):
        ky_copy(d, y).start()

    wait_vy(z)
    arrive(v_ring(3))
    v_total = v_part(z) + vr_in[3].astype(F32) + vl_in[3].astype(F32)
    kv_out[1] = v_total.astype(BF)
    each_peer(lambda p: kv_copy(p, 1, me).start())

    cosine, sine = cs_ref[0], -cs_ref[1]

    def rotate_dq(p):
        for h in range(GRP):
            cols = pl.ds(pl.multiple_of(p * WIDE + h * HD, HD), HD)
            gq_ref[:, cols] = turn(dqx[p, :, h * HD:(h + 1) * HD].astype(F32), cosine, sine).astype(BF)

    rotate_dq(me)

    for d in range(1, NY):
        ky_copy(d, (y + d) % NY).wait_recv()
    k_sum = ky_out[y].astype(F32)
    for d in range(1, NY):
        k_sum = k_sum + ky_in[(y + d) % NY].astype(F32)
    kv_out[0] = k_sum.astype(BF)
    each_peer(lambda p: kv_copy(p, 0, me).start())

    def q_in(p):
        q_copy(p, p).wait_recv()
        rotate_dq(p)

    each_peer(q_in)
    kv_in[0, me] = kv_out[0, me]
    kv_in[1, me] = kv_out[1, me]

    def kv_arrive(p):
        for which in range(2):
            kv_copy(p, which, p).wait_recv()

    each_peer(kv_arrive)
    for h in range(NP):
        cols = slice(h * HD, (h + 1) * HD)
        key_scale = stab_ref[0, sidx_ref[0, block, h]]
        value_scale = stab_ref[1, sidx_ref[1, block, h]]
        gk_ref[:, cols] = (turn(kv_in[0, h].astype(F32), cosine, sine) * key_scale).astype(BF)
        gv_ref[:, cols] = (kv_in[1, h].astype(F32) * value_scale).astype(BF)

    each_peer(lambda p: o_copy(p, p).wait_recv())
    own_o.wait()

    def sent(p):
        o_copy(p, me).wait_send()
        q_copy(p, me).wait_send()
        for which in range(2):
            kv_copy(p, which, me).wait_send()

    each_peer(sent)
    for d in range(1, NY):
        ky_copy(d, y).wait_send()
    for s in range(4):
        for copy in k_ring(s) + v_ring(s):
            copy.wait_send()

    def vy_sent(zz, carry):
        for d in range(1, NY):
            vy_copy(d, zz, y).wait_send()
        return carry

    lax.fori_loop(0, NZ, vy_sent, 0)


def body(queries, keys, values, grad_out, doc_lengths, block_pairs, scale_index, scale_table):
    half = np.arange(HD // 2, dtype=np.float32) * np.float32(-2.0 * math.log(500000.0) / HD)
    freq = np.exp(half.astype(np.float32)).astype(np.float32)
    freq = jnp.asarray(np.tile(np.concatenate([freq, freq])[None], (8, 1)))
    vmem = pl.BlockSpec(memory_space=pltpu.VMEM)
    smem = pl.BlockSpec(memory_space=pltpu.SMEM)
    dma = pltpu.SemaphoreType.DMA
    shape = jax.ShapeDtypeStruct
    qx, gox, ka, va, lists, cs = pl.pallas_call(
        gather_kernel,
        name="gather",
        out_shape=(
            shape((NP, ROWS, WIDE), BF),
            shape((NP, ROWS, WIDE), BF),
            shape((NZ, NY, NP, ROWS, HD), BF),
            shape((NY, NZ, NP, ROWS, HD), BF),
            shape((NP, BLK), jnp.int32),
            shape((2, ROWS, HD), F32),
        ),
        in_specs=[vmem] * 4 + [smem, vmem, smem, smem, vmem],
        out_specs=(vmem,) * 6,
        scratch_shapes=[
            pltpu.VMEM((NP, ROWS, WIDE), BF),
            pltpu.VMEM((NP, ROWS, HD), BF),
            pltpu.VMEM((NP, ROWS, HD), BF),
        ]
        + [dma((NP,))] * 8
        + [dma((NY,))] * 2
        + [dma((4,))] * 8
        + [dma((NY, NZ))] * 2
        + [dma],
        compiler_params=pltpu.CompilerParams(
            collective_id=0, has_side_effects=True, vmem_limit_bytes=VMEM_LIMIT
        ),
    )(queries, keys, values, grad_out, doc_lengths, block_pairs, scale_index, scale_table, freq)

    o, dq, dk, dv = pl.pallas_call(
        attend_kernel,
        name="attend",
        out_shape=(
            shape((NP, ROWS, WIDE), BF),
            shape((NP, ROWS, WIDE), BF),
            shape((NZ, NY, NP, ROWS, HD), BF),
            shape((NY, NZ, NP, ROWS, HD), BF),
        ),
        in_specs=[smem, smem] + [vmem] * 4,
        out_specs=(vmem,) * 4,
        scratch_shapes=[
            pltpu.VMEM((NBLK, BLK, GRP * ROWS), F32),
            pltpu.VMEM((NZ, NY, NP, ROWS, HD), F32),
            pltpu.VMEM((NY, NZ, NP, ROWS, HD), F32),
        ],
        compiler_params=pltpu.CompilerParams(vmem_limit_bytes=VMEM_LIMIT),
    )(lists, doc_lengths, qx, gox, ka, va)

    slab_k = (4, NY, NP, ROWS, HD)
    slab_v = (4, NP, ROWS, HD)
    return pl.pallas_call(
        scatter_kernel,
        name="scatter",
        out_shape=(
            shape((ROWS, NP * WIDE), BF),
            shape((ROWS, NP * WIDE), BF),
            shape((ROWS, NP * HD), BF),
            shape((ROWS, NP * HD), BF),
        ),
        in_specs=[vmem] * 5 + [smem, smem],
        out_specs=(vmem,) * 4,
        scratch_shapes=[pltpu.VMEM((NP, ROWS, WIDE), BF)]
        + [pltpu.VMEM(slab_k, BF)] * 4
        + [pltpu.VMEM(slab_v, BF)] * 4
        + [pltpu.VMEM((NY, NP, ROWS, HD), BF)] * 2
        + [pltpu.VMEM((NY, NZ, NP, ROWS, HD), BF)]
        + [pltpu.VMEM((2, NP, ROWS, HD), BF)] * 2
        + [dma((NP,))] * 4
        + [dma((4,))] * 8
        + [dma((NY,))] * 2
        + [dma((NY, NZ))] * 2
        + [dma((2, NP))] * 2
        + [dma],
        compiler_params=pltpu.CompilerParams(
            collective_id=1, has_side_effects=True, vmem_limit_bytes=VMEM_LIMIT
        ),
    )(o, dq, dk, dv, cs, scale_index, scale_table)


def solution(mesh):
    rows = P(("ctx", "head"), None)
    in_specs = (rows,) * 4 + (P(),) * 4
    return jax.shard_map(body, mesh=mesh, in_specs=in_specs, out_specs=(rows,) * 4, check_vma=False)
```

```python
import functools
import math

import jax
import jax.numpy as jnp
import numpy as np
from jax import lax
from jax.experimental import pallas as pl
from jax.experimental.pallas import tpu as pltpu
from jax.sharding import PartitionSpec as P

HD = 128
BLK = 128
ROWS = 16
GRP = 16
NX, NY, NC, NZ = 4, 4, 2, 8
NP = NX * NC
NBLK = 32
NDOC = 8
WIDE = GRP * HD
NEG = -1e30
CHUNK = 4
TWIN = 2
SCALE = 1.0 / math.sqrt(HD)
EXP2_SCALE = SCALE * math.log2(math.e)
MESH = pl.DeviceIdType.MESH
BF = jnp.bfloat16
F32 = jnp.float32
VMEM_LIMIT = 56 * 1024 * 1024


def place():
    ctx = lax.axis_index("ctx")
    return ctx // (NY * NC), (ctx // NC) % NY, ctx % NC, lax.axis_index("head")


def device(xx, yy, cc, zz):
    return {"ctx": xx * (NY * NC) + yy * NC + cc, "head": zz}


def peer(p, y, z):
    return device(p // NC, y, p % NC, z)


def remote(src, dst, send_sem, recv_sem, dev):
    return pltpu.make_async_remote_copy(
        src_ref=src, dst_ref=dst, send_sem=send_sem, recv_sem=recv_sem, device_id=dev, device_id_type=MESH
    )


def enter(me, x, y, c, z):
    barrier = pltpu.get_barrier_semaphore()

    def greet(dev):
        pl.semaphore_signal(barrier, inc=1, device_id=dev, device_id_type=MESH)

    for off in (2, NZ - 2, 1, NZ - 1):
        greet(device(x, y, c, (z + off) % NZ))

    def step(e, carry):
        greet(peer((me + e % NP) % NP, (y + e // NP) % NY, z))
        return carry

    lax.fori_loop(1, NP * NY, step, 0)
    return barrier


N_PARTNERS = NP * NY - 1 + 4


def loop(lo, hi, fn):
    def step(i, carry):
        fn(i)
        return carry

    lax.fori_loop(lo, hi, step, 0)


def turn(x, cosine, sine):
    return x * cosine + pltpu.roll(x, HD // 2, 1) * sine


def gather_kernel(
    q_ref, k_ref, v_ref, go_ref, doc_ref, pairs_ref, sidx_ref, stab_ref, freq_ref,
    qx_ref, gox_ref, ka_ref, va_ref, lists_ref, cs_ref,
    qs, ks, vs,
    q_s, q_r, go_s, go_r, k_s, k_r, v_s, v_r, kzr_s, kzr_r, kzl_s, kzl_r,
    va_s, va_r, vb_s, vb_r, vy_s, vy_r, own_s,
):
    x, y, c, z = place()
    me = NC * x + c
    block = lax.axis_index("ctx")
    barrier = enter(me, x, y, c, z)

    token = BLK * block + ROWS * z + lax.broadcasted_iota(jnp.int32, (ROWS, HD), 0)
    start = jnp.zeros((ROWS, HD), jnp.int32)
    end = 0
    for d in range(NDOC):
        end = end + doc_ref[d]
        start = start + jnp.where(token >= end, doc_ref[d], 0)
    angle = (token - start).astype(F32) * freq_ref[0:1, :]
    cosine = jnp.cos(angle)
    sine = jnp.sin(angle)
    sine = jnp.where(lax.broadcasted_iota(jnp.int32, (ROWS, HD), 1) < HD // 2, -sine, sine)
    cs_ref[0] = cosine
    cs_ref[1] = sine

    for h in range(NP):
        cols = slice(h * HD, (h + 1) * HD)
        key_scale = stab_ref[0, sidx_ref[0, h, block]]
        value_scale = stab_ref[1, sidx_ref[1, h, block]]
        ks[h] = turn(k_ref[:, cols].astype(F32) * key_scale, cosine, sine).astype(BF)
        vs[h] = (v_ref[:, cols].astype(F32) * value_scale).astype(BF)

    def rotate_q(p):
        for h in range(GRP):
            cols = pl.ds(pl.multiple_of(p * WIDE + h * HD, HD), HD)
            qs[p, :, h * HD:(h + 1) * HD] = turn(q_ref[:, cols].astype(F32), cosine, sine).astype(BF)

    loop(0, NP, rotate_q)
    qx_ref[me] = qs[me]
    ka_ref[z, y, me] = ks[me]
    va_ref[y, z, me] = vs[me]

    pl.semaphore_wait(barrier, N_PARTNERS)

    def each_peer(fn):
        loop(1, NP, lambda d: fn((me + d) % NP))

    def k_copy(e, arriving):
        p, yy = (me + e % NP) % NP, (y + e // NP) % NY
        ys, slot = (yy, p) if arriving else (y, me)
        return remote(ks.at[p], ka_ref.at[z, ys, slot], k_s.at[e], k_r.at[ys, slot], peer(p, yy, z))

    def v_copy(p, slot):
        return remote(vs.at[p], va_ref.at[y, z, slot], v_s.at[p], v_r.at[slot], peer(p, y, z))

    def go_cols(p):
        return go_ref.at[:, pl.ds(pl.multiple_of(p * WIDE, WIDE), WIDE)]

    def go_copy(p, slot):
        return remote(go_cols(p), gox_ref.at[slot], go_s.at[p], go_r.at[slot], peer(p, y, z))

    def q_copy(p, slot):
        return remote(qs.at[p], qx_ref.at[slot], q_s.at[p], q_r.at[slot], peer(p, y, z))

    each_peer(lambda p: v_copy(p, me).start())
    loop(1, NP * NY, lambda e: k_copy(e, False).start())
    each_peer(lambda p: go_copy(p, me).start())
    each_peer(lambda p: q_copy(p, me).start())
    own_go = pltpu.make_async_copy(go_cols(me), gox_ref.at[me], own_s)
    own_go.start()

    def along(off):
        return device(x, y, c, (z + off + NZ) % NZ)

    def k_ring(s, u, rightward, sending):
        far = s if sending else s + 1
        zz = (z + NZ - far) % NZ if rightward else (z + far) % NZ
        ref = ka_ref.at[zz, pl.ds(u * (NY // 2), NY // 2)]
        if rightward:
            return remote(ref, ref, kzr_s.at[s, u], kzr_r.at[s, u], along(1))
        return remote(ref, ref, kzl_s.at[s, u], kzl_r.at[s, u], along(-1))

    def k_sends(s):
        return [(u, r) for u in range(2) for r in (True, False) if s < 3 or (u == 0) == r]

    first_hops = (1, -1, 2, -2)

    def v_first(j, arriving):
        zz = (z + first_hops[j] + NZ) % NZ if arriving else z
        ref = va_ref.at[y, zz]
        return remote(ref, ref, va_s.at[j], va_r.at[j], along(-first_hops[j]))

    def v_second(j, arriving):
        off, part = ((2, None), (-2, None), (2, 0), (-2, 1))[j]
        hop = -1 if off > 0 else 1
        if part is not None:
            hop = 2 * hop
        zz = (z + off - (hop if arriving else 0) + NZ) % NZ
        ref = va_ref.at[y, zz]
        if part is not None:
            ref = va_ref.at[y, zz, pl.ds(part * (NP // 2), NP // 2)]
        return remote(ref, ref, vb_s.at[j], vb_r.at[j], along(hop))

    def v_spread(zz, d, arriving):
        yy = (y + d) % NY
        ys = yy if arriving else y
        return remote(va_ref.at[ys, zz], va_ref.at[ys, zz], vy_s.at[d, zz], vy_r.at[ys, zz], device(x, yy, c, z))

    def spread(off):
        for d in (2, 1, 3):
            v_spread((z + off + NZ) % NZ, d, False).start()

    each_peer(lambda p: v_copy(p, p).wait_recv())
    for j in (2, 3, 0, 1):
        v_first(j, False).start()
    spread(0)
    loop(1, NP * NY, lambda e: k_copy(e, True).wait_recv())
    for u, r in k_sends(0):
        k_ring(0, u, r, True).start()

    lane = lax.broadcasted_iota(jnp.int32, (NP, BLK), 1)
    row = lax.broadcasted_iota(jnp.int32, (NP, BLK), 0)
    own_block = NY * NC * (row // NC) + NC * y + row % NC
    first = BLK * own_block + ROWS * z
    doc_start = jnp.zeros((NP, BLK), jnp.int32)
    end = 0
    for d in range(NDOC):
        end = end + doc_ref[d]
        doc_start = doc_start + jnp.where(first >= end, doc_ref[d], 0)
    pairs = pairs_ref[...]
    n_pairs = pairs.shape[1]
    pair_row = lax.broadcasted_iota(jnp.int32, (NP, n_pairs), 0)
    pair_q = (pairs[0:1] == NY * NC * (pair_row // NC) + NC * y + pair_row % NC).astype(F32)
    pair_k = (pairs[1:2] == lax.broadcasted_iota(jnp.int32, (BLK, n_pairs), 0)).astype(F32)
    listed = lax.dot_general(pair_q, pair_k, (((1,), (1,)), ((), ())), preferred_element_type=F32)
    wanted = ((listed > 0.5) | (lane == own_block)) & (BLK * lane + BLK - 1 >= doc_start) & (lane <= own_block)
    wanted_f = wanted.astype(F32)
    upper = (
        lax.broadcasted_iota(jnp.int32, (BLK, BLK), 0) <= lax.broadcasted_iota(jnp.int32, (BLK, BLK), 1)
    ).astype(F32)
    rank = jnp.dot(wanted_f, upper, preferred_element_type=F32)
    lane_f = lane.astype(F32)

    def list_step(r, out):
        hit = wanted & (rank.astype(jnp.int32) == r + 1)
        entry = jnp.sum(jnp.where(hit, lane_f, 0.0), axis=1, keepdims=True)
        return jnp.where(lane == r, entry, out)

    out = lax.fori_loop(0, NBLK, list_step, jnp.zeros((NP, BLK), F32))
    out = jnp.where(lane == BLK - 1, jnp.sum(wanted_f, axis=1, keepdims=True), out)
    lists_ref[...] = out.astype(jnp.int32)

    def k_step(s):
        onward = k_sends(s) if s < 4 else []
        for u, r in k_sends(s - 1):
            k_ring(s - 1, u, r, False).wait_recv()
            if (u, r) in onward:
                k_ring(s, u, r, True).start()

    for j in (0, 1):
        v_first(j, True).wait_recv()
        spread(first_hops[j])
    for j in (2, 3):
        v_first(j, True).wait_recv()
        v_second(j, False).start()
        v_second(j - 2, False).start()
        spread(first_hops[j])
    k_step(1)
    for j in (0, 1):
        v_second(j, True).wait_recv()
        spread((3, -3)[j])
    for j in (2, 3):
        v_second(j, True).wait_recv()
    spread(4)
    k_step(2)
    k_step(3)
    k_step(4)

    def spread_in(zz):
        for d in range(1, NY):
            v_spread(zz, d, True).wait_recv()

    loop(0, NZ, spread_in)

    def qgo_in(p):
        go_copy(p, p).wait_recv()
        q_copy(p, p).wait_recv()

    each_peer(qgo_in)
    own_go.wait()

    def sent(p):
        v_copy(p, me).wait_send()
        go_copy(p, me).wait_send()
        q_copy(p, me).wait_send()

    each_peer(sent)
    loop(1, NP * NY, lambda e: k_copy(e, False).wait_send())
    for s in range(4):
        for u, r in k_sends(s):
            k_ring(s, u, r, True).wait_send()
    for j in range(4):
        v_first(j, False).wait_send()
        v_second(j, False).wait_send()

    def spread_sent(zz):
        for d in range(1, NY):
            v_spread(zz, d, False).wait_send()

    loop(0, NZ, spread_sent)


def heads_to_rows(ref, i):
    return jnp.concatenate([ref[i, :, h * HD:(h + 1) * HD] for h in range(GRP)], axis=0)


def rows_to_heads(ref, i, rows):
    for h in range(GRP):
        ref[i, :, h * HD:(h + 1) * HD] = rows[h * ROWS:(h + 1) * ROWS]


SPAN = CHUNK * BLK


def attend_kernel(lists_ref, doc_ref, q_ref, go_ref, k_ref, v_ref, o_ref, dq_ref, dk_ref, dv_ref,
                  s_ref, dp_ref, o_acc, dq_acc, dk_acc, dv_acc):
    _, y, _, z = place()
    rows = GRP*ROWS
    dk_acc[...] = jnp.zeros_like(dk_acc)
    dv_acc[...] = jnp.zeros_like(dv_acc)
    key_row = lax.broadcasted_iota(jnp.int32, (BLK, rows), 0)
    lane = lax.broadcasted_iota(jnp.int32, (1, rows), 1)
    nt = (((1,), (1,)), ((), ()))
    tn = (((0,), (0,)), ((), ()))

    def pair(pi, carry):
        gs = [pi*TWIN+j for j in range(TWIN)]
        counts = [lists_ref[g, BLK-1] for g in gs]
        most = functools.reduce(jnp.maximum, counts)
        chunks = (most + CHUNK - 1)//CHUNK
        queries = [heads_to_rows(q_ref, g) for g in gs]
        grads = [heads_to_rows(go_ref, g) for g in gs]
        tokens, starts = [], []
        for g in gs:
            own = NY*NC*(g//NC) + NC*y + g%NC
            token = BLK*own + ROWS*z + lane%ROWS
            start = jnp.zeros((1, rows), jnp.int32)
            end = 0
            for d in range(NDOC):
                end = end + doc_ref[d]
                start = start + jnp.where(token >= end, doc_ref[d], 0)
            tokens.append(token); starts.append(start)

        def spots(j, n):
            out = []
            for u in range(CHUNK):
                t = n*CHUNK + u
                b = lists_ref[gs[j], t]
                out.append((t < counts[j], b, (b//NC)%NY, (b//(NY*NC))*NC + b%NC))
            return out

        def keys_of(sp):
            return jnp.concatenate([k_ref[:, yb, ib].reshape(BLK, HD) for _, _, yb, ib in sp], axis=0)

        def values_of(sp):
            return jnp.concatenate([v_ref[yb, :, ib].reshape(BLK, HD) for _, _, yb, ib in sp], axis=0)

        def fold(x):
            return x.reshape(SPAN//8, 8, rows)

        def score_step(n, tops):
            out = []
            for j in range(TWIN):
                sp = spots(j, n)
                scores = lax.dot_general(keys_of(sp), queries[j], nt, preferred_element_type=F32)
                dp_ref[j, n] = lax.dot_general(values_of(sp), grads[j], nt, preferred_element_type=F32)
                top = tops[j]
                for u, (live, b, _, _) in enumerate(sp):
                    low = jnp.where(live, starts[j] - BLK*b, BLK)
                    allowed = (key_row >= low) & (key_row <= tokens[j] - BLK*b)
                    part = jnp.where(allowed, scores[u*BLK:(u+1)*BLK], NEG)
                    s_ref[j, n, u*BLK:(u+1)*BLK] = part
                    top = jnp.maximum(top, jnp.max(part.reshape(BLK//8, 8, rows), axis=0))
                out.append(top)
            return tuple(out)

        tops = lax.fori_loop(0, chunks, score_step, tuple(jnp.full((8, rows), NEG, F32) for _ in gs))
        tops = [jnp.max(t, axis=0, keepdims=True) for t in tops]
        for j in range(TWIN):
            o_acc[j] = jnp.zeros((HD, rows), F32)
            dq_acc[j] = jnp.zeros((HD, rows), F32)

        def out_step(n, carry):
            out = []
            for j in range(TWIN):
                total, mean = carry[j]
                sp = spots(j, n)
                weights = jnp.exp2((s_ref[j, n] - tops[j])*EXP2_SCALE)
                s_ref[j, n] = weights
                total = total + jnp.sum(fold(weights), axis=0)
                mean = mean + jnp.sum(fold(weights*dp_ref[j, n]), axis=0)
                o_acc[j] += lax.dot_general(values_of(sp), weights.astype(BF), tn, preferred_element_type=F32)
                out.append((total, mean))
            return tuple(out)

        zero = jnp.zeros((8, rows), F32)
        sums = lax.fori_loop(0, chunks, out_step, tuple((zero, zero) for _ in gs))
        inverses, deltas = [], []
        for j in range(TWIN):
            inverse = 1.0/jnp.sum(sums[j][0], axis=0, keepdims=True)
            inverses.append(inverse)
            deltas.append(jnp.sum(sums[j][1], axis=0, keepdims=True)*inverse)

        def grad_step(n, carry):
            for j in range(TWIN):
                sp = spots(j, n)
                probs = s_ref[j, n]*inverses[j]
                grad_scores = (probs*(dp_ref[j, n] - deltas[j])).astype(BF)
                dv = jnp.dot(probs.astype(BF), grads[j], preferred_element_type=F32)
                dk = jnp.dot(grad_scores, queries[j], preferred_element_type=F32)
                dq_acc[j] += lax.dot_general(keys_of(sp), grad_scores, tn, preferred_element_type=F32)
                for u, (_, _, yb, ib) in enumerate(sp):
                    dv_acc[yb, :, ib] += dv[u*BLK:(u+1)*BLK].reshape(NZ, ROWS, HD)
                    dk_acc[:, yb, ib] += dk[u*BLK:(u+1)*BLK].reshape(NZ, ROWS, HD)
            return carry

        lax.fori_loop(0, chunks, grad_step, 0)
        for j in range(TWIN):
            rows_to_heads(o_ref, gs[j], (o_acc[j]*inverses[j]).T.astype(BF))
            rows_to_heads(dq_ref, gs[j], (dq_acc[j]*SCALE).T.astype(BF))
        return carry

    lax.fori_loop(0, NP//TWIN, pair, 0)

    def finish(zz, carry):
        dk_ref[zz] = (dk_acc[zz]*SCALE).astype(BF)
        for yy in range(NY):
            dv_ref[yy, zz] = dv_acc[yy, zz].astype(BF)
        return carry
    lax.fori_loop(0, NZ, finish, 0)


def scatter_kernel(
    o_ref, dq_ref, dk_ref, dv_ref, cs_ref, sidx_ref, stab_ref,
    ao_ref, gq_ref, gk_ref, gv_ref,
    dqx, kr_out, kl_out, kr_in, kl_in, va_out, va_in, vb_out, vb_in, k_out, k_in, vy_in, v_out, v_in,
    o_s, o_r, q_s, q_r, kzr_s, kzr_r, kzl_s, kzl_r, va_s, va_r, vb_s, vb_r,
    vy_s, vy_r, k_s, k_r, v_s, v_r, own_s,
):
    x, y, c, z = place()
    me = NC * x + c
    block = lax.axis_index("ctx")
    barrier = enter(me, x, y, c, z)
    pl.semaphore_wait(barrier, N_PARTNERS)

    def each_peer(fn):
        loop(1, NP, lambda d: fn((me + d) % NP))

    def along(off):
        return device(x, y, c, (z + off + NZ) % NZ)

    def head_cols(ref, g):
        return ref.at[:, pl.ds(pl.multiple_of(g * WIDE, WIDE), WIDE)]

    def o_copy(p, slot):
        return remote(o_ref.at[p], head_cols(ao_ref, slot), o_s.at[p], o_r.at[slot], peer(p, y, z))

    def q_copy(p, slot):
        return remote(dq_ref.at[p], dqx.at[slot], q_s.at[p], q_r.at[slot], peer(p, y, z))

    def vy_copy(off, d, arriving):
        zz, yy = (z + off + NZ) % NZ, (y + d) % NY
        slot = yy if arriving else y
        return remote(dv_ref.at[yy, zz], vy_in.at[slot, zz], vy_s.at[d, zz], vy_r.at[slot, zz], device(x, yy, c, z))

    half = NY // 2

    def k_ring(s, u, rightward):
        if rightward:
            return remote(kr_out.at[s, u], kr_in.at[s, u], kzr_s.at[s, u], kzr_r.at[s, u], along(1))
        return remote(kl_out.at[s, u], kl_in.at[s, u], kzl_s.at[s, u], kzl_r.at[s, u], along(-1))

    def k_part(zz, u):
        return dk_ref[zz, u * half:(u + 1) * half].astype(F32)

    def k_send(s, u, rightward):
        zz = (z + 4 - s) % NZ if rightward else (z + 4 + s) % NZ
        total = k_part(zz, u)
        if s > 1 or (s == 1 and (u == 0) == rightward):
            k_ring(s - 1, u, rightward).wait_recv()
            total = total + (kr_in if rightward else kl_in)[s - 1, u].astype(F32)
        (kr_out if rightward else kl_out)[s, u] = total.astype(BF)
        k_ring(s, u, rightward).start()

    def v_part(off):
        zz = (z + off + NZ) % NZ
        total = dv_ref[y, zz].astype(F32)
        for d in range(1, NY):
            vy_copy(off, d, True).wait_recv()
            total = total + vy_in[(y + d) % NY, zz].astype(F32)
        return total

    cut = NP // 2

    def v_far(j):
        hop = (1, -1, 2, -2)[j]
        if j < 2:
            return remote(va_out.at[j], va_in.at[j], va_s.at[j], va_r.at[j], along(hop))
        part = pl.ds(0 if j == 2 else cut, cut)
        return remote(va_out.at[2, part], va_in.at[2, part], va_s.at[j], va_r.at[j], along(hop))

    near = (1, -1, 2, -2)

    def v_near(j):
        return remote(vb_out.at[j], vb_in.at[j], vb_s.at[j], vb_r.at[j], along(near[j]))

    k_send(0, 0, True)
    k_send(0, 1, False)
    k_send(1, 1, True)
    k_send(1, 0, False)
    order = (3, -3, 4, 2, -2, 1, -1, 0)
    for off in order:
        for d in (2, 1, 3):
            vy_copy(off, d, False).start()
    each_peer(lambda p: o_copy(p, me).start())
    each_peer(lambda p: q_copy(p, me).start())
    own_o = pltpu.make_async_copy(o_ref.at[me], head_cols(ao_ref, me), own_s)
    own_o.start()
    dqx[me] = dq_ref[me]

    k_send(1, 0, True)
    k_send(1, 1, False)
    va_out[0] = v_part(3).astype(BF)
    v_far(0).start()
    va_out[1] = v_part(-3).astype(BF)
    v_far(1).start()
    va_out[2] = v_part(4).astype(BF)
    v_far(2).start()
    v_far(3).start()
    for u, r in ((1, True), (0, False), (0, True), (1, False)):
        k_send(2, u, r)
    v_two = [v_part(2), v_part(-2)]
    for j in range(2):
        v_far(j).wait_recv()
        v_far(j + 2).wait_recv()
        total = v_two[j] + va_in[j].astype(F32)
        low, high = total[:cut], total[cut:]
        if j == 0:
            low = low + va_in[2, :cut].astype(F32)
        else:
            high = high + va_in[2, cut:].astype(F32)
        vb_out[j + 2, :cut] = low.astype(BF)
        vb_out[j + 2, cut:] = high.astype(BF)
        v_near(j + 2).start()
    for j in range(2):
        vb_out[j] = v_part(near[j]).astype(BF)
        v_near(j).start()
    for u, r in ((1, True), (0, False), (0, True), (1, False)):
        k_send(3, u, r)

    def k_copy(e, arriving):
        p, yy = (me + e % NP) % NP, (y + e // NP) % NY
        ys, slot = (yy, p) if arriving else (y, me)
        return remote(k_out.at[yy, p], k_in.at[ys, slot], k_s.at[e], k_r.at[ys, slot], peer(p, yy, z))

    def v_copy(p, slot):
        return remote(v_out.at[p], v_in.at[slot], v_s.at[p], v_r.at[slot], peer(p, y, z))

    cosine, sine = cs_ref[0], -cs_ref[1]

    def rotate_dq(p):
        for h in range(GRP):
            cols = pl.ds(pl.multiple_of(p * WIDE + h * HD, HD), HD)
            gq_ref[:, cols] = turn(dqx[p, :, h * HD:(h + 1) * HD].astype(F32), cosine, sine).astype(BF)

    v_total = v_part(0)
    for j in range(4):
        v_near(j).wait_recv()
        v_total = v_total + vb_in[j].astype(F32)
    v_out[...] = v_total.astype(BF)
    v_in[me] = v_out[me]
    each_peer(lambda p: v_copy(p, me).start())

    for u in range(2):
        k_ring(3, u, True).wait_recv()
        k_ring(3, u, False).wait_recv()
        total = k_part(z, u) + kr_in[3, u].astype(F32) + kl_in[3, u].astype(F32)
        k_out[u * half:(u + 1) * half] = total.astype(BF)
    k_in[y, me] = k_out[y, me]
    loop(1, NP * NY, lambda e: k_copy(e, False).start())

    rotate_dq(me)

    def q_in(p):
        q_copy(p, p).wait_recv()
        rotate_dq(p)

    each_peer(q_in)
    each_peer(lambda p: v_copy(p, p).wait_recv())
    for h in range(NP):
        value_scale = stab_ref[1, sidx_ref[1, h, block]]
        gv_ref[:, h * HD:(h + 1) * HD] = (v_in[h].astype(F32) * value_scale).astype(BF)
    loop(1, NP * NY, lambda e: k_copy(e, True).wait_recv())
    for h in range(NP):
        key_scale = stab_ref[0, sidx_ref[0, h, block]]
        total = k_in[0, h].astype(F32)
        for yy in range(1, NY):
            total = total + k_in[yy, h].astype(F32)
        gk_ref[:, h * HD:(h + 1) * HD] = (turn(total, cosine, sine) * key_scale).astype(BF)

    each_peer(lambda p: o_copy(p, p).wait_recv())
    own_o.wait()

    def sent(p):
        o_copy(p, me).wait_send()
        q_copy(p, me).wait_send()
        v_copy(p, me).wait_send()

    each_peer(sent)
    loop(1, NP * NY, lambda e: k_copy(e, False).wait_send())
    for s in range(4):
        for u in range(2):
            for r in (True, False):
                if s or (u == 0) == r:
                    k_ring(s, u, r).wait_send()
    for j in range(4):
        v_far(j).wait_send()
        v_near(j).wait_send()
    for off in order:
        for d in (2, 1, 3):
            vy_copy(off, d, False).wait_send()


def body(queries, keys, values, grad_out, doc_lengths, block_pairs, scale_index, scale_table):
    half = np.arange(HD // 2, dtype=np.float32) * np.float32(-2.0 * math.log(500000.0) / HD)
    freq = np.exp(half.astype(np.float32)).astype(np.float32)
    freq = jnp.asarray(np.tile(np.concatenate([freq, freq])[None], (8, 1)))
    scale_by_head = scale_index.transpose(0, 2, 1)
    vmem = pl.BlockSpec(memory_space=pltpu.VMEM)
    smem = pl.BlockSpec(memory_space=pltpu.SMEM)
    dma = pltpu.SemaphoreType.DMA
    shape = jax.ShapeDtypeStruct
    qx, gox, ka, va, lists, cs = pl.pallas_call(
        gather_kernel,
        name="gather",
        out_shape=(
            shape((NP, ROWS, WIDE), BF),
            shape((NP, ROWS, WIDE), BF),
            shape((NZ, NY, NP, ROWS, HD), BF),
            shape((NY, NZ, NP, ROWS, HD), BF),
            shape((NP, BLK), jnp.int32),
            shape((2, ROWS, HD), F32),
        ),
        in_specs=[vmem] * 4 + [smem, vmem, smem, smem, vmem],
        out_specs=(vmem,) * 6,
        scratch_shapes=[
            pltpu.VMEM((NP, ROWS, WIDE), BF),
            pltpu.VMEM((NP, ROWS, HD), BF),
            pltpu.VMEM((NP, ROWS, HD), BF),
        ]
        + [dma((NP,))] * 4
        + [dma((NP * NY,)), dma((NY, NP))]
        + [dma((NP,))] * 2
        + [dma((4, 2))] * 4
        + [dma((4,))] * 4
        + [dma((NY, NZ))] * 2
        + [dma],
        compiler_params=pltpu.CompilerParams(
            collective_id=0, has_side_effects=True, vmem_limit_bytes=VMEM_LIMIT
        ),
    )(queries, keys, values, grad_out, doc_lengths, block_pairs.T, scale_by_head, scale_table, freq)

    o, dq, dk, dv = pl.pallas_call(
        attend_kernel,
        name="attend",
        out_shape=(
            shape((NP, ROWS, WIDE), BF),
            shape((NP, ROWS, WIDE), BF),
            shape((NZ, NY, NP, ROWS, HD), BF),
            shape((NY, NZ, NP, ROWS, HD), BF),
        ),
        in_specs=[smem, smem] + [vmem] * 4,
        out_specs=(vmem,) * 4,
        scratch_shapes=[
            pltpu.VMEM((TWIN, NBLK // CHUNK, SPAN, GRP * ROWS), F32),
            pltpu.VMEM((TWIN, NBLK // CHUNK, SPAN, GRP * ROWS), F32),
            pltpu.VMEM((TWIN, HD, GRP * ROWS), F32),
            pltpu.VMEM((TWIN, HD, GRP * ROWS), F32),
            pltpu.VMEM((NZ, NY, NP, ROWS, HD), F32),
            pltpu.VMEM((NY, NZ, NP, ROWS, HD), F32),
        ],
        compiler_params=pltpu.CompilerParams(vmem_limit_bytes=VMEM_LIMIT),
    )(lists, doc_lengths, qx, gox, ka, va)

    return pl.pallas_call(
        scatter_kernel,
        name="scatter",
        out_shape=(
            shape((ROWS, NP * WIDE), BF),
            shape((ROWS, NP * WIDE), BF),
            shape((ROWS, NP * HD), BF),
            shape((ROWS, NP * HD), BF),
        ),
        in_specs=[vmem] * 5 + [smem, smem],
        out_specs=(vmem,) * 4,
        scratch_shapes=[pltpu.VMEM((NP, ROWS, WIDE), BF)]
        + [pltpu.VMEM((4, 2, NY // 2, NP, ROWS, HD), BF)] * 4
        + [pltpu.VMEM((3, NP, ROWS, HD), BF)] * 2
        + [pltpu.VMEM((4, NP, ROWS, HD), BF)] * 2
        + [pltpu.VMEM((NY, NP, ROWS, HD), BF)] * 2
        + [pltpu.VMEM((NY, NZ, NP, ROWS, HD), BF)]
        + [pltpu.VMEM((NP, ROWS, HD), BF)] * 2
        + [dma((NP,))] * 4
        + [dma((4, 2))] * 4
        + [dma((4,))] * 4
        + [dma((NY, NZ))] * 2
        + [dma((NP * NY,)), dma((NY, NP))]
        + [dma((NP,))] * 2
        + [dma],
        compiler_params=pltpu.CompilerParams(
            collective_id=1, has_side_effects=True, vmem_limit_bytes=VMEM_LIMIT
        ),
    )(o, dq, dk, dv, cs, scale_by_head, scale_table)


def solution(mesh):
    rows = P(("ctx", "head"), None)
    in_specs = (rows,) * 4 + (P(),) * 4
    return jax.shard_map(body, mesh=mesh, in_specs=in_specs, out_specs=(rows,) * 4, check_vma=False)
```

```python
import functools
import math

import jax
import jax.numpy as jnp
import numpy as np
from jax import lax
from jax.experimental import pallas as pl
from jax.experimental.pallas import tpu as pltpu
from jax.sharding import PartitionSpec as P

HD = 128
BLK = 128
ROWS = 16
GRP = 16
NX, NY, NC, NZ = 4, 4, 2, 8
NP = NX * NC
NBLK = 32
NDOC = 8
WIDE = GRP * HD
NEG = -1e30
CHUNK = 4
TWIN = 2
SCALE = 1.0 / math.sqrt(HD)
EXP2_SCALE = SCALE * math.log2(math.e)
MESH = pl.DeviceIdType.MESH
BF = jnp.bfloat16
F32 = jnp.float32
VMEM_LIMIT = 56 * 1024 * 1024


def place():
    ctx = lax.axis_index("ctx")
    return ctx // (NY * NC), (ctx // NC) % NY, ctx % NC, lax.axis_index("head")


def device(xx, yy, cc, zz):
    return {"ctx": xx * (NY * NC) + yy * NC + cc, "head": zz}


def peer(p, y, z):
    return device(p // NC, y, p % NC, z)


def remote(src, dst, send_sem, recv_sem, dev):
    return pltpu.make_async_remote_copy(
        src_ref=src, dst_ref=dst, send_sem=send_sem, recv_sem=recv_sem, device_id=dev, device_id_type=MESH
    )


def enter(me, x, y, c, z):
    barrier = pltpu.get_barrier_semaphore()

    def greet(dev):
        pl.semaphore_signal(barrier, inc=1, device_id=dev, device_id_type=MESH)

    for off in (2, NZ - 2, 1, NZ - 1):
        greet(device(x, y, c, (z + off) % NZ))

    def step(e, carry):
        greet(peer((me + e % NP) % NP, (y + e // NP) % NY, z))
        return carry

    lax.fori_loop(1, NP * NY, step, 0)
    return barrier


N_PARTNERS = NP * NY - 1 + 4


def loop(lo, hi, fn):
    def step(i, carry):
        fn(i)
        return carry

    lax.fori_loop(lo, hi, step, 0)


def settle(ref, sem):
    pltpu.make_async_copy(ref, ref, sem).wait()


def turn(x, cosine, sine):
    return x * cosine + pltpu.roll(x, HD // 2, 1) * sine


def gather_kernel(
    q_ref, k_ref, v_ref, go_ref, doc_ref, pairs_ref, sidx_ref, stab_ref, freq_ref,
    qx_ref, gox_ref, ka_out, va_out, lists_ref, cs_ref,
    q_in, qs, ks, vs, ka_ref, va_ref,
    q_s, q_r, go_s, go_r, k_s, k_r, v_s, v_r, kzr_s, kzr_r, kzl_s, kzl_r,
    va_s, va_r, vb_s, vb_r, vy_s, vy_r, own_s, kout_s, vout_s,
):
    x, y, c, z = place()
    me = NC * x + c
    block = lax.axis_index("ctx")
    barrier = enter(me, x, y, c, z)
    q_load = pltpu.make_async_copy(q_ref, q_in, own_s.at[0])
    q_load.start()

    token = BLK * block + ROWS * z + lax.broadcasted_iota(jnp.int32, (ROWS, HD), 0)
    start = jnp.zeros((ROWS, HD), jnp.int32)
    end = 0
    for d in range(NDOC):
        end = end + doc_ref[d]
        start = start + jnp.where(token >= end, doc_ref[d], 0)
    angle = (token - start).astype(F32) * freq_ref[0:1, :]
    cosine = jnp.cos(angle)
    sine = jnp.sin(angle)
    sine = jnp.where(lax.broadcasted_iota(jnp.int32, (ROWS, HD), 1) < HD // 2, -sine, sine)
    cs_ref[0] = cosine
    cs_ref[1] = sine

    for h in range(NP):
        cols = slice(h * HD, (h + 1) * HD)
        key_scale = stab_ref[0, sidx_ref[0, h, block]]
        value_scale = stab_ref[1, sidx_ref[1, h, block]]
        ks[h] = turn(k_ref[:, cols].astype(F32) * key_scale, cosine, sine).astype(BF)
        vs[h] = (v_ref[:, cols].astype(F32) * value_scale).astype(BF)

    def rotate_q(p):
        for h in range(GRP):
            cols = pl.ds(pl.multiple_of(p * WIDE + h * HD, HD), HD)
            qs[p, :, h * HD:(h + 1) * HD] = turn(q_in[:, cols].astype(F32), cosine, sine).astype(BF)

    ka_ref[z, y, me] = ks[me]
    va_ref[y, z, me] = vs[me]

    pl.semaphore_wait(barrier, N_PARTNERS)

    def each_peer(fn):
        loop(1, NP, lambda d: fn((me + d) % NP))

    def k_copy(e, far):
        p, yy = (me + e % NP) % NP, (y + e // NP) % NY
        return remote(ks.at[p], ka_ref.at[z, y, me], k_s.at[far], k_r.at[far], peer(p, yy, z))

    def v_copy(p, slot):
        return remote(vs.at[p], va_ref.at[y, z, slot], v_s, v_r, peer(p, y, z))

    def go_cols(p):
        return go_ref.at[:, pl.ds(pl.multiple_of(p * WIDE, WIDE), WIDE)]

    def go_copy(p, slot):
        return remote(go_cols(p), gox_ref.at[slot], go_s, go_r, peer(p, y, z))

    def q_copy(p, slot):
        return remote(qs.at[p], qx_ref.at[slot], q_s, q_r, peer(p, y, z))

    each_peer(lambda p: v_copy(p, me).start())
    loop(1, NP, lambda e: k_copy(e, 0).start())
    loop(NP, NP * NY, lambda e: k_copy(e, 1).start())
    each_peer(lambda p: go_copy(p, me).start())
    q_load.wait()

    def rotate_and_send(p):
        rotate_q(p)
        q_copy(p, me).start()

    each_peer(rotate_and_send)
    rotate_q(me)
    own_go = pltpu.make_async_copy(go_cols(me), gox_ref.at[me], own_s.at[1])
    own_q = pltpu.make_async_copy(qs.at[me], qx_ref.at[me], own_s.at[2])
    own_go.start()
    own_q.start()

    def along(off):
        return device(x, y, c, (z + off + NZ) % NZ)

    def k_ring(s, u, rightward, sending):
        far = s if sending else s + 1
        zz = (z + NZ - far) % NZ if rightward else (z + far) % NZ
        ref = ka_ref.at[zz, pl.ds(u * (NY // 2), NY // 2)]
        if rightward:
            return remote(ref, ref, kzr_s.at[s, u], kzr_r.at[s, u], along(1))
        return remote(ref, ref, kzl_s.at[s, u], kzl_r.at[s, u], along(-1))

    def k_sends(s):
        return [(u, r) for u in range(2) for r in (True, False) if s < 3 or (u == 0) == r]

    def k_store(s, u, rightward):
        zz = (z + NZ - s) % NZ if rightward else (z + s) % NZ
        part = pl.ds(u * (NY // 2), NY // 2)
        return pltpu.make_async_copy(
            ka_ref.at[zz, part], ka_out.at[zz, part], kout_s.at[s, u if rightward else 1 - u, 0 if rightward else 1]
        )

    def v_store(yy):
        return pltpu.make_async_copy(va_ref.at[yy], va_out.at[yy], vout_s.at[yy])

    first_hops = (1, -1, 2, -2)

    def v_first(j, arriving):
        zz = (z + first_hops[j] + NZ) % NZ if arriving else z
        ref = va_ref.at[y, zz]
        return remote(ref, ref, va_s.at[j], va_r.at[j], along(-first_hops[j]))

    def v_second(j, arriving):
        off, part = ((2, None), (-2, None), (2, 0), (-2, 1))[j]
        hop = -1 if off > 0 else 1
        if part is not None:
            hop = 2 * hop
        zz = (z + off - (hop if arriving else 0) + NZ) % NZ
        ref = va_ref.at[y, zz]
        if part is not None:
            ref = va_ref.at[y, zz, pl.ds(part * (NP // 2), NP // 2)]
        return remote(ref, ref, vb_s.at[j], vb_r.at[j], along(hop))

    def v_spread(zz, d, arriving):
        yy = (y + d) % NY
        ys = yy if arriving else y
        return remote(va_ref.at[ys, zz], va_ref.at[ys, zz], vy_s, vy_r.at[ys], device(x, yy, c, z))

    def spread(off):
        for d in (2, 1, 3):
            v_spread((z + off + NZ) % NZ, d, False).start()

    settle(va_ref.at[y, z, pl.ds(0, NP - 1)], v_r)
    for j in (2, 3, 0, 1):
        v_first(j, False).start()
    spread(0)
    settle(ka_ref.at[z, 0, pl.ds(0, NP - 1)], k_r.at[0])
    settle(ka_ref.at[z, pl.ds(0, NY - 1)], k_r.at[1])
    for u, r in k_sends(0):
        k_ring(0, u, r, True).start()
    for u in range(2):
        k_store(0, u, True).start()

    lane = lax.broadcasted_iota(jnp.int32, (NP, BLK), 1)
    row = lax.broadcasted_iota(jnp.int32, (NP, BLK), 0)
    own_block = NY * NC * (row // NC) + NC * y + row % NC
    first = BLK * own_block + ROWS * z
    doc_start = jnp.zeros((NP, BLK), jnp.int32)
    end = 0
    for d in range(NDOC):
        end = end + doc_ref[d]
        doc_start = doc_start + jnp.where(first >= end, doc_ref[d], 0)
    pairs = pairs_ref[...]
    n_pairs = pairs.shape[1]
    pair_row = lax.broadcasted_iota(jnp.int32, (NP, n_pairs), 0)
    pair_q = (pairs[0:1] == NY * NC * (pair_row // NC) + NC * y + pair_row % NC).astype(F32)
    pair_k = (pairs[1:2] == lax.broadcasted_iota(jnp.int32, (BLK, n_pairs), 0)).astype(F32)
    listed = lax.dot_general(pair_q, pair_k, (((1,), (1,)), ((), ())), preferred_element_type=F32)
    wanted = ((listed > 0.5) | (lane == own_block)) & (BLK * lane + BLK - 1 >= doc_start) & (lane <= own_block)
    wanted_f = wanted.astype(F32)
    upper = (
        lax.broadcasted_iota(jnp.int32, (BLK, BLK), 0) <= lax.broadcasted_iota(jnp.int32, (BLK, BLK), 1)
    ).astype(F32)
    rank = jnp.dot(wanted_f, upper, preferred_element_type=F32)
    lane_f = lane.astype(F32)

    def list_step(r, out):
        hit = wanted & (rank.astype(jnp.int32) == r + 1)
        entry = jnp.sum(jnp.where(hit, lane_f, 0.0), axis=1, keepdims=True)
        return jnp.where(lane == r, entry, out)

    out = lax.fori_loop(0, NBLK, list_step, jnp.zeros((NP, BLK), F32))
    out = jnp.where(lane == BLK - 1, jnp.sum(wanted_f, axis=1, keepdims=True), out)
    lists_ref[...] = out.astype(jnp.int32)

    def k_step(s):
        onward = k_sends(s) if s < 4 else []
        for u, r in k_sends(s - 1):
            k_ring(s - 1, u, r, False).wait_recv()
            if (u, r) in onward:
                k_ring(s, u, r, True).start()
            k_store(s, u, r).start()

    for j in (0, 1):
        v_first(j, True).wait_recv()
        spread(first_hops[j])
    for j in (2, 3):
        v_first(j, True).wait_recv()
        v_second(j, False).start()
        v_second(j - 2, False).start()
        spread(first_hops[j])
    k_step(1)
    for j in (0, 1):
        v_second(j, True).wait_recv()
        spread((3, -3)[j])
    for j in (2, 3):
        v_second(j, True).wait_recv()
    spread(4)
    v_store(y).start()
    k_step(2)
    k_step(3)
    k_step(4)

    for d in (1, 3, 2):
        settle(va_ref.at[(y + d) % NY], vy_r.at[(y + d) % NY])
        v_store((y + d) % NY).start()

    settle(gox_ref.at[pl.ds(0, NP - 1)], go_r)
    settle(qx_ref.at[pl.ds(0, NP - 1)], q_r)
    own_go.wait()
    own_q.wait()

    settle(vs.at[pl.ds(0, NP - 1)], v_s)
    settle(go_ref.at[:, pl.ds(0, (NP - 1) * WIDE)], go_s)
    settle(qs.at[pl.ds(0, NP - 1)], q_s)
    settle(ks.at[pl.ds(0, NP - 1)], k_s.at[0])
    settle(ka_ref.at[z, pl.ds(0, NY - 1)], k_s.at[1])
    settle(va_ref.at[pl.ds(0, NY - 1)], vy_s)
    for s in range(4):
        for u, r in k_sends(s):
            k_ring(s, u, r, True).wait_send()
    for j in range(4):
        v_first(j, False).wait_send()
        v_second(j, False).wait_send()

    for u in range(2):
        k_store(0, u, True).wait()
    for s in range(1, 5):
        for u, r in k_sends(s - 1):
            k_store(s, u, r).wait()
    loop(0, NY, lambda yy: v_store(yy).wait())


def heads_to_rows(ref, i):
    return jnp.concatenate([ref[i, :, h * HD:(h + 1) * HD] for h in range(GRP)], axis=0)


def rows_to_heads(ref, i, rows):
    for h in range(GRP):
        ref[i, :, h * HD:(h + 1) * HD] = rows[h * ROWS:(h + 1) * ROWS]


SPAN = CHUNK * BLK


def attend_kernel(
    lists_ref, doc_ref, q_in, go_in, k_in, v_in, o_out, dq_out, dk_out, dv_out,
    q_ref, go_ref, k_ref, v_ref, o_ref, dq_ref, dk_ref, dv_ref,
    s_ref, dp_ref, o_acc, dq_acc, dk_acc, dv_acc,
    kv_s, q_s, go_s, o_s, dq_s, dk_s, dv_s,
):
    _, y, _, z = place()
    rows = GRP*ROWS

    def twins(ref, pi):
        return ref.at[pl.ds(pi*TWIN, TWIN)]

    def q_load(pi):
        return pltpu.make_async_copy(twins(q_in, pi), twins(q_ref, pi), q_s.at[pi])

    def go_load(pi):
        return pltpu.make_async_copy(twins(go_in, pi), twins(go_ref, pi), go_s.at[pi])

    def o_store(pi):
        return pltpu.make_async_copy(twins(o_ref, pi), twins(o_out, pi), o_s.at[pi])

    def dq_store(pi):
        return pltpu.make_async_copy(twins(dq_ref, pi), twins(dq_out, pi), dq_s.at[pi])

    def dk_store(zz):
        return pltpu.make_async_copy(dk_ref.at[zz], dk_out.at[zz], dk_s.at[zz])

    def dv_store(yy):
        return pltpu.make_async_copy(dv_ref.at[yy], dv_out.at[yy], dv_s.at[yy])

    k_load = pltpu.make_async_copy(k_in, k_ref, kv_s.at[0])
    v_load = pltpu.make_async_copy(v_in, v_ref, kv_s.at[1])
    q_load(0).start()
    go_load(0).start()
    k_load.start()
    v_load.start()
    for pi in range(1, NP//TWIN):
        q_load(pi).start()
        go_load(pi).start()
    dk_acc[...] = jnp.zeros_like(dk_acc)
    dv_acc[...] = jnp.zeros_like(dv_acc)
    k_load.wait()
    v_load.wait()
    key_row = lax.broadcasted_iota(jnp.int32, (BLK, rows), 0)
    lane = lax.broadcasted_iota(jnp.int32, (1, rows), 1)
    nt = (((1,), (1,)), ((), ()))
    tn = (((0,), (0,)), ((), ()))

    def pair(pi, carry):
        gs = [pi*TWIN+j for j in range(TWIN)]
        counts = [lists_ref[g, BLK-1] for g in gs]
        most = functools.reduce(jnp.maximum, counts)
        chunks = (most + CHUNK - 1)//CHUNK
        q_load(pi).wait()
        go_load(pi).wait()
        queries = [heads_to_rows(q_ref, g) for g in gs]
        grads = [heads_to_rows(go_ref, g) for g in gs]
        tokens, starts = [], []
        for g in gs:
            own = NY*NC*(g//NC) + NC*y + g%NC
            token = BLK*own + ROWS*z + lane%ROWS
            start = jnp.zeros((1, rows), jnp.int32)
            end = 0
            for d in range(NDOC):
                end = end + doc_ref[d]
                start = start + jnp.where(token >= end, doc_ref[d], 0)
            tokens.append(token); starts.append(start)

        def spots(j, n):
            out = []
            for u in range(CHUNK):
                t = n*CHUNK + u
                b = lists_ref[gs[j], t]
                out.append((t < counts[j], b, (b//NC)%NY, (b//(NY*NC))*NC + b%NC))
            return out

        def keys_of(sp):
            return jnp.concatenate([k_ref[:, yb, ib].reshape(BLK, HD) for _, _, yb, ib in sp], axis=0)

        def values_of(sp):
            return jnp.concatenate([v_ref[yb, :, ib].reshape(BLK, HD) for _, _, yb, ib in sp], axis=0)

        def fold(x):
            return x.reshape(SPAN//8, 8, rows)

        def score_step(n, tops):
            out = []
            for j in range(TWIN):
                sp = spots(j, n)
                scores = lax.dot_general(keys_of(sp), queries[j], nt, preferred_element_type=F32)
                dp_ref[j, n] = lax.dot_general(values_of(sp), grads[j], nt, preferred_element_type=F32)
                top = tops[j]
                for u, (live, b, _, _) in enumerate(sp):
                    low = jnp.where(live, starts[j] - BLK*b, BLK)
                    allowed = (key_row >= low) & (key_row <= tokens[j] - BLK*b)
                    part = jnp.where(allowed, scores[u*BLK:(u+1)*BLK], NEG)
                    s_ref[j, n, u*BLK:(u+1)*BLK] = part
                    top = jnp.maximum(top, jnp.max(part.reshape(BLK//8, 8, rows), axis=0))
                out.append(top)
            return tuple(out)

        tops = lax.fori_loop(0, chunks, score_step, tuple(jnp.full((8, rows), NEG, F32) for _ in gs))
        tops = [jnp.max(t, axis=0, keepdims=True) for t in tops]
        for j in range(TWIN):
            o_acc[j] = jnp.zeros((HD, rows), F32)
            dq_acc[j] = jnp.zeros((HD, rows), F32)

        def out_step(n, carry):
            out = []
            for j in range(TWIN):
                total, mean = carry[j]
                sp = spots(j, n)
                weights = jnp.exp2((s_ref[j, n] - tops[j])*EXP2_SCALE)
                s_ref[j, n] = weights
                total = total + jnp.sum(fold(weights), axis=0)
                mean = mean + jnp.sum(fold(weights*dp_ref[j, n]), axis=0)
                o_acc[j] += lax.dot_general(values_of(sp), weights.astype(BF), tn, preferred_element_type=F32)
                out.append((total, mean))
            return tuple(out)

        zero = jnp.zeros((8, rows), F32)
        sums = lax.fori_loop(0, chunks, out_step, tuple((zero, zero) for _ in gs))
        inverses, deltas = [], []
        for j in range(TWIN):
            inverse = 1.0/jnp.sum(sums[j][0], axis=0, keepdims=True)
            inverses.append(inverse)
            deltas.append(jnp.sum(sums[j][1], axis=0, keepdims=True)*inverse)

        def grad_step(n, carry):
            for j in range(TWIN):
                sp = spots(j, n)
                probs = s_ref[j, n]*inverses[j]
                grad_scores = (probs*(dp_ref[j, n] - deltas[j])).astype(BF)
                dv = jnp.dot(probs.astype(BF), grads[j], preferred_element_type=F32)
                dk = jnp.dot(grad_scores, queries[j], preferred_element_type=F32)
                dq_acc[j] += lax.dot_general(keys_of(sp), grad_scores, tn, preferred_element_type=F32)
                for u, (_, _, yb, ib) in enumerate(sp):
                    dv_acc[yb, :, ib] += dv[u*BLK:(u+1)*BLK].reshape(NZ, ROWS, HD)
                    dk_acc[:, yb, ib] += dk[u*BLK:(u+1)*BLK].reshape(NZ, ROWS, HD)
            return carry

        lax.fori_loop(0, chunks, grad_step, 0)
        for j in range(TWIN):
            rows_to_heads(o_ref, gs[j], (o_acc[j]*inverses[j]).T.astype(BF))
            rows_to_heads(dq_ref, gs[j], (dq_acc[j]*SCALE).T.astype(BF))
        o_store(pi).start()
        dq_store(pi).start()
        return carry

    lax.fori_loop(0, NP//TWIN, pair, 0)

    def finish_k(zz):
        dk_ref[zz] = (dk_acc[zz]*SCALE).astype(BF)
        dk_store(zz).start()

    def finish_v(yy):
        dv_ref[yy] = dv_acc[yy].astype(BF)
        dv_store(yy).start()

    loop(0, NZ, finish_k)
    loop(0, NY, finish_v)
    for pi in range(NP//TWIN):
        o_store(pi).wait()
        dq_store(pi).wait()
    loop(0, NZ, lambda zz: dk_store(zz).wait())
    loop(0, NY, lambda yy: dv_store(yy).wait())


def scatter_kernel(
    o_ref, dq_ref, dk_hbm, dv_ref, cs_ref, sidx_ref, stab_ref,
    ao_ref, dqx, gk_ref, gv_ref,
    dk_ref, dv_own, kr_out, kl_out, kr_in, kl_in, va_out, va_in, vb_out, vb_in, k_out, k_in, vy_in, v_out, v_in,
    o_s, o_r, q_s, q_r, kzr_s, kzr_r, kzl_s, kzl_r, va_s, va_r, vb_s, vb_r,
    vy_s, vy_r, k_s, k_r, v_s, v_r, own_s,
):
    x, y, c, z = place()
    me = NC * x + c
    block = lax.axis_index("ctx")
    barrier = enter(me, x, y, c, z)
    dk_load = pltpu.make_async_copy(dk_hbm, dk_ref, own_s.at[2])
    dv_load = pltpu.make_async_copy(dv_ref.at[y], dv_own, own_s.at[3])
    dk_load.start()
    dv_load.start()
    pl.semaphore_wait(barrier, N_PARTNERS)

    def each_peer(fn):
        loop(1, NP, lambda d: fn((me + d) % NP))

    def along(off):
        return device(x, y, c, (z + off + NZ) % NZ)

    def head_cols(ref, g):
        return ref.at[:, pl.ds(pl.multiple_of(g * WIDE, WIDE), WIDE)]

    def o_copy(p, slot):
        return remote(o_ref.at[p], head_cols(ao_ref, slot), o_s, o_r, peer(p, y, z))

    def q_copy(p, slot):
        return remote(dq_ref.at[p], dqx.at[slot], q_s, q_r, peer(p, y, z))

    def vy_copy(off, d, arriving):
        zz, yy = (z + off + NZ) % NZ, (y + d) % NY
        slot = yy if arriving else y
        return remote(dv_ref.at[yy, zz], vy_in.at[slot, zz], vy_s, vy_r.at[zz], device(x, yy, c, z))

    half = NY // 2

    def k_ring(s, u, rightward):
        if rightward:
            return remote(kr_out.at[s, u], kr_in.at[s, u], kzr_s.at[s, u], kzr_r.at[s, u], along(1))
        return remote(kl_out.at[s, u], kl_in.at[s, u], kzl_s.at[s, u], kzl_r.at[s, u], along(-1))

    def k_part(zz, u):
        return dk_ref[zz, u * half:(u + 1) * half].astype(F32)

    def k_send(s, u, rightward):
        zz = (z + 4 - s) % NZ if rightward else (z + 4 + s) % NZ
        total = k_part(zz, u)
        if s > 1 or (s == 1 and (u == 0) == rightward):
            k_ring(s - 1, u, rightward).wait_recv()
            total = total + (kr_in if rightward else kl_in)[s - 1, u].astype(F32)
        (kr_out if rightward else kl_out)[s, u] = total.astype(BF)
        k_ring(s, u, rightward).start()

    def v_part(off):
        zz = (z + off + NZ) % NZ
        total = dv_own[zz].astype(F32)
        settle(dv_own.at[pl.ds(0, NY - 1)], vy_r.at[zz])
        for d in range(1, NY):
            total = total + vy_in[(y + d) % NY, zz].astype(F32)
        return total

    cut = NP // 2

    def v_far(j):
        hop = (1, -1, 2, -2)[j]
        if j < 2:
            return remote(va_out.at[j], va_in.at[j], va_s.at[j], va_r.at[j], along(hop))
        part = pl.ds(0 if j == 2 else cut, cut)
        return remote(va_out.at[2, part], va_in.at[2, part], va_s.at[j], va_r.at[j], along(hop))

    near = (1, -1, 2, -2)

    def v_near(j):
        return remote(vb_out.at[j], vb_in.at[j], vb_s.at[j], vb_r.at[j], along(near[j]))

    order = (3, -3, 4, 2, -2, 1, -1, 0)
    for off in order[:3]:
        for d in (2, 1, 3):
            vy_copy(off, d, False).start()
    dk_load.wait()
    k_send(0, 0, True)
    k_send(0, 1, False)
    k_send(1, 1, True)
    k_send(1, 0, False)
    for off in order[3:]:
        for d in (2, 1, 3):
            vy_copy(off, d, False).start()
    each_peer(lambda p: o_copy(p, me).start())
    each_peer(lambda p: q_copy(p, me).start())
    own_o = pltpu.make_async_copy(o_ref.at[me], head_cols(ao_ref, me), own_s.at[0])
    own_q = pltpu.make_async_copy(dq_ref.at[me], dqx.at[me], own_s.at[1])
    own_o.start()
    own_q.start()

    dv_load.wait()
    k_send(1, 0, True)
    k_send(1, 1, False)
    va_out[0] = v_part(3).astype(BF)
    v_far(0).start()
    va_out[1] = v_part(-3).astype(BF)
    v_far(1).start()
    va_out[2] = v_part(4).astype(BF)
    v_far(2).start()
    v_far(3).start()
    for u, r in ((1, True), (0, False), (0, True), (1, False)):
        k_send(2, u, r)
    v_two = [v_part(2), v_part(-2)]
    for j in range(2):
        v_far(j).wait_recv()
        v_far(j + 2).wait_recv()
        total = v_two[j] + va_in[j].astype(F32)
        low, high = total[:cut], total[cut:]
        if j == 0:
            low = low + va_in[2, :cut].astype(F32)
        else:
            high = high + va_in[2, cut:].astype(F32)
        vb_out[j + 2, :cut] = low.astype(BF)
        vb_out[j + 2, cut:] = high.astype(BF)
        v_near(j + 2).start()
    for j in range(2):
        vb_out[j] = v_part(near[j]).astype(BF)
        v_near(j).start()
    for u, r in ((1, True), (0, False), (0, True), (1, False)):
        k_send(3, u, r)

    def k_copy(e, far):
        p, yy = (me + e % NP) % NP, (y + e // NP) % NY
        return remote(k_out.at[yy, p], k_in.at[y, me], k_s.at[far], k_r.at[far], peer(p, yy, z))

    def v_copy(p, slot):
        return remote(v_out.at[p], v_in.at[slot], v_s, v_r, peer(p, y, z))

    cosine, sine = cs_ref[0], -cs_ref[1]

    v_total = v_part(0)
    for j in range(4):
        v_near(j).wait_recv()
        v_total = v_total + vb_in[j].astype(F32)
    v_out[...] = v_total.astype(BF)
    v_in[me] = v_out[me]
    each_peer(lambda p: v_copy(p, me).start())

    for u in range(2):
        k_ring(3, u, True).wait_recv()
        k_ring(3, u, False).wait_recv()
        total = k_part(z, u) + kr_in[3, u].astype(F32) + kl_in[3, u].astype(F32)
        k_out[u * half:(u + 1) * half] = total.astype(BF)
    k_in[y, me] = k_out[y, me]
    loop(1, NP, lambda e: k_copy(e, 0).start())
    loop(NP, NP * NY, lambda e: k_copy(e, 1).start())

    settle(v_in.at[pl.ds(0, NP - 1)], v_r)
    for h in range(NP):
        value_scale = stab_ref[1, sidx_ref[1, h, block]]
        gv_ref[:, h * HD:(h + 1) * HD] = (v_in[h].astype(F32) * value_scale).astype(BF)
    settle(k_in.at[0, pl.ds(0, NP - 1)], k_r.at[0])
    settle(k_in.at[pl.ds(0, NY - 1)], k_r.at[1])
    for h in range(NP):
        key_scale = stab_ref[0, sidx_ref[0, h, block]]
        total = k_in[0, h].astype(F32)
        for yy in range(1, NY):
            total = total + k_in[yy, h].astype(F32)
        gk_ref[:, h * HD:(h + 1) * HD] = (turn(total, cosine, sine) * key_scale).astype(BF)

    settle(o_ref.at[pl.ds(0, NP - 1)], o_r)
    settle(dqx.at[pl.ds(0, NP - 1)], q_r)
    own_o.wait()
    own_q.wait()

    settle(o_ref.at[pl.ds(0, NP - 1)], o_s)
    settle(dq_ref.at[pl.ds(0, NP - 1)], q_s)
    settle(v_out.at[pl.ds(0, NP - 1)], v_s)
    settle(k_out.at[0, pl.ds(0, NP - 1)], k_s.at[0])
    settle(k_out.at[pl.ds(0, NY - 1)], k_s.at[1])
    settle(dv_ref.at[pl.ds(0, NY - 1)], vy_s)
    for s in range(4):
        for u in range(2):
            for r in (True, False):
                if s or (u == 0) == r:
                    k_ring(s, u, r).wait_send()
    for j in range(4):
        v_far(j).wait_send()
        v_near(j).wait_send()


def finish_kernel(ao_in, dqx_ref, gk_in, gv_in, cs_ref, ao_out, gq_out, gk_out, gv_out, gq_ref, sems, gq_s):
    copies = [
        pltpu.make_async_copy(src, dst, sems.at[i])
        for i, (src, dst) in enumerate(((ao_in, ao_out), (gk_in, gk_out), (gv_in, gv_out)))
    ]
    for copy in copies:
        copy.start()
    cosine, sine = cs_ref[0], -cs_ref[1]

    def store(p):
        cols = pl.ds(pl.multiple_of(p * WIDE, WIDE), WIDE)
        return pltpu.make_async_copy(gq_ref.at[:, cols], gq_out.at[:, cols], gq_s.at[p])

    def rotate_back(p):
        for h in range(GRP):
            cols = pl.ds(pl.multiple_of(p * WIDE + h * HD, HD), HD)
            gq_ref[:, cols] = turn(dqx_ref[p, :, h * HD:(h + 1) * HD].astype(F32), cosine, sine).astype(BF)
        store(p).start()

    loop(0, NP, rotate_back)
    for copy in copies:
        copy.wait()
    loop(0, NP, lambda p: store(p).wait())


def body(queries, keys, values, grad_out, doc_lengths, block_pairs, scale_index, scale_table):
    half = np.arange(HD // 2, dtype=np.float32) * np.float32(-2.0 * math.log(500000.0) / HD)
    freq = np.exp(half.astype(np.float32)).astype(np.float32)
    freq = jnp.asarray(np.tile(np.concatenate([freq, freq])[None], (8, 1)))
    scale_by_head = scale_index.transpose(0, 2, 1)
    vmem = pl.BlockSpec(memory_space=pltpu.VMEM)
    anywhere = pl.BlockSpec(memory_space=pl.ANY)
    smem = pl.BlockSpec(memory_space=pltpu.SMEM)
    dma = pltpu.SemaphoreType.DMA
    shape = jax.ShapeDtypeStruct
    qx, gox, ka, va, lists, cs = pl.pallas_call(
        gather_kernel,
        name="gather",
        out_shape=(
            shape((NP, ROWS, WIDE), BF),
            shape((NP, ROWS, WIDE), BF),
            shape((NZ, NY, NP, ROWS, HD), BF),
            shape((NY, NZ, NP, ROWS, HD), BF),
            shape((NP, BLK), jnp.int32),
            shape((2, ROWS, HD), F32),
        ),
        in_specs=[anywhere, vmem, vmem, anywhere, smem, vmem, smem, smem, vmem],
        out_specs=(anywhere,) * 4 + (vmem,) * 2,
        scratch_shapes=[
            pltpu.VMEM((ROWS, NP * WIDE), BF),
            pltpu.VMEM((NP, ROWS, WIDE), BF),
            pltpu.VMEM((NP, ROWS, HD), BF),
            pltpu.VMEM((NP, ROWS, HD), BF),
            pltpu.VMEM((NZ, NY, NP, ROWS, HD), BF),
            pltpu.VMEM((NY, NZ, NP, ROWS, HD), BF),
        ]
        + [dma] * 4
        + [dma((2,))] * 2
        + [dma] * 2
        + [dma((4, 2))] * 4
        + [dma((4,))] * 4
        + [dma, dma((NY,))]
        + [dma((3,)), dma((5, 2, 2)), dma((NY,))],
        compiler_params=pltpu.CompilerParams(
            collective_id=0, has_side_effects=True, vmem_limit_bytes=VMEM_LIMIT
        ),
    )(queries, keys, values, grad_out, doc_lengths, block_pairs.T, scale_by_head, scale_table, freq)

    o, dq, dk, dv = pl.pallas_call(
        attend_kernel,
        name="attend",
        out_shape=(
            shape((NP, ROWS, WIDE), BF),
            shape((NP, ROWS, WIDE), BF),
            shape((NZ, NY, NP, ROWS, HD), BF),
            shape((NY, NZ, NP, ROWS, HD), BF),
        ),
        in_specs=[smem, smem] + [anywhere] * 4,
        out_specs=(anywhere,) * 4,
        scratch_shapes=([pltpu.VMEM((NP, ROWS, WIDE), BF)] * 2
        + [pltpu.VMEM((NZ, NY, NP, ROWS, HD), BF), pltpu.VMEM((NY, NZ, NP, ROWS, HD), BF)]) * 2
        + [
            pltpu.VMEM((TWIN, NBLK // CHUNK, SPAN, GRP * ROWS), F32),
            pltpu.VMEM((TWIN, NBLK // CHUNK, SPAN, GRP * ROWS), F32),
            pltpu.VMEM((TWIN, HD, GRP * ROWS), F32),
            pltpu.VMEM((TWIN, HD, GRP * ROWS), F32),
            pltpu.VMEM((NZ, NY, NP, ROWS, HD), F32),
            pltpu.VMEM((NY, NZ, NP, ROWS, HD), F32),
        ]
        + [dma((2,))]
        + [dma((NP // TWIN,))] * 4
        + [dma((NZ,)), dma((NY,))],
        compiler_params=pltpu.CompilerParams(vmem_limit_bytes=VMEM_LIMIT),
    )(lists, doc_lengths, qx, gox, ka, va)

    ao, dqx, gk, gv = pl.pallas_call(
        scatter_kernel,
        name="scatter",
        out_shape=(
            shape((ROWS, NP * WIDE), BF),
            shape((NP, ROWS, WIDE), BF),
            shape((ROWS, NP * HD), BF),
            shape((ROWS, NP * HD), BF),
        ),
        in_specs=[anywhere] * 4 + [vmem, smem, smem],
        out_specs=(anywhere,) * 2 + (vmem,) * 2,
        scratch_shapes=[pltpu.VMEM((NZ, NY, NP, ROWS, HD), BF), pltpu.VMEM((NZ, NP, ROWS, HD), BF)]
        + [pltpu.VMEM((4, 2, NY // 2, NP, ROWS, HD), BF)] * 4
        + [pltpu.VMEM((3, NP, ROWS, HD), BF)] * 2
        + [pltpu.VMEM((4, NP, ROWS, HD), BF)] * 2
        + [pltpu.VMEM((NY, NP, ROWS, HD), BF)] * 2
        + [pltpu.VMEM((NY, NZ, NP, ROWS, HD), BF)]
        + [pltpu.VMEM((NP, ROWS, HD), BF)] * 2
        + [dma] * 4
        + [dma((4, 2))] * 4
        + [dma((4,))] * 4
        + [dma, dma((NZ,))]
        + [dma((2,))] * 2
        + [dma] * 2
        + [dma((4,))],
        compiler_params=pltpu.CompilerParams(
            collective_id=1, has_side_effects=True, vmem_limit_bytes=VMEM_LIMIT
        ),
    )(o, dq, dk, dv, cs, scale_by_head, scale_table)

    return pl.pallas_call(
        finish_kernel,
        name="finish",
        out_shape=(
            shape((ROWS, NP * WIDE), BF),
            shape((ROWS, NP * WIDE), BF),
            shape((ROWS, NP * HD), BF),
            shape((ROWS, NP * HD), BF),
        ),
        in_specs=[vmem] * 5,
        out_specs=(anywhere,) * 4,
        scratch_shapes=[pltpu.VMEM((ROWS, NP * WIDE), BF), dma((3,)), dma((NP,))],
        compiler_params=pltpu.CompilerParams(vmem_limit_bytes=VMEM_LIMIT),
    )(ao, dqx, gk, gv, cs)


def solution(mesh):
    rows = P(("ctx", "head"), None)
    in_specs = (rows,) * 4 + (P(),) * 4
    return jax.shard_map(body, mesh=mesh, in_specs=in_specs, out_specs=(rows,) * 4, check_vma=False)
```

```python
import functools
import math

import jax
import jax.numpy as jnp
import numpy as np
from jax import lax
from jax.experimental import pallas as pl
from jax.experimental.pallas import tpu as pltpu
from jax.sharding import PartitionSpec as P

HD = 128
BLK = 128
ROWS = 16
GRP = 16
NX, NY, NC, NZ = 4, 4, 2, 8
NP = NX * NC
NBLK = 32
NDOC = 8
WIDE = GRP * HD
NEG = -1e30
UNROLL = 6
SCALE = 1.0 / math.sqrt(HD)
EXP2_SCALE = SCALE * math.log2(math.e)
MESH = pl.DeviceIdType.MESH
BF = jnp.bfloat16
F32 = jnp.float32
VMEM_LIMIT = 56 * 1024 * 1024


def place():
    ctx = lax.axis_index("ctx")
    return ctx // (NY * NC), (ctx // NC) % NY, ctx % NC, lax.axis_index("head")


def device(xx, yy, cc, zz):
    return {"ctx": xx * (NY * NC) + yy * NC + cc, "head": zz}


def peer(p, y, z):
    return device(p // NC, y, p % NC, z)


def remote(src, dst, send_sem, recv_sem, dev):
    return pltpu.make_async_remote_copy(
        src_ref=src, dst_ref=dst, send_sem=send_sem, recv_sem=recv_sem, device_id=dev, device_id_type=MESH
    )


def enter(me, x, y, c, z):
    barrier = pltpu.get_barrier_semaphore()

    def greet(dev):
        pl.semaphore_signal(barrier, inc=1, device_id=dev, device_id_type=MESH)

    for off in (2, NZ - 2, 1, NZ - 1):
        greet(device(x, y, c, (z + off) % NZ))

    def step(e, carry):
        greet(peer((me + e % NP) % NP, (y + e // NP) % NY, z))
        return carry

    lax.fori_loop(1, NP * NY, step, 0)
    return barrier


N_PARTNERS = NP * NY - 1 + 4


def loop(lo, hi, fn):
    def step(i, carry):
        fn(i)
        return carry

    lax.fori_loop(lo, hi, step, 0)


def settle(ref, sem):
    pltpu.make_async_copy(ref, ref, sem).wait()


def turn(x, cosine, sine):
    return x * cosine + pltpu.roll(x, HD // 2, 1) * sine


def gather_kernel(
    q_ref, k_hbm, v_hbm, go_ref, doc_hbm, pairs_hbm, sidx_hbm, stab_hbm, freq_hbm,
    qx_ref, gox_ref, ka_out, va_out, lists_out, cs_out,
    k_ref, v_ref, doc_ref, pairs_ref, sidx_ref, stab_ref, freq_ref, lists_ref, cs_ref, q_in, qs, ks, vs, ka_ref, va_ref,
    q_s, q_r, go_s, go_r, k_s, k_r, v_s, v_r, kzr_s, kzr_r, kzl_s, kzl_r,
    va_s, va_r, vb_s, vb_r, vy_s, vy_r, own_s, kout_s, vout_s, load_s,
):
    x, y, c, z = place()
    me = NC * x + c
    block = lax.axis_index("ctx")
    loads = [
        pltpu.make_async_copy(src, dst, load_s.at[n])
        for n, (src, dst) in enumerate((
            (doc_hbm, doc_ref), (freq_hbm, freq_ref), (k_hbm, k_ref), (v_hbm, v_ref),
            (sidx_hbm, sidx_ref), (stab_hbm, stab_ref), (pairs_hbm, pairs_ref),
        ))
    ]
    for load in loads:
        load.start()
    q_load = pltpu.make_async_copy(q_ref, q_in, own_s.at[0])
    q_load.start()
    barrier = enter(me, x, y, c, z)
    for load in loads:
        load.wait()

    token = BLK * block + ROWS * z + lax.broadcasted_iota(jnp.int32, (ROWS, HD), 0)
    start = jnp.zeros((ROWS, HD), jnp.int32)
    end = 0
    for d in range(NDOC):
        end = end + doc_ref[d]
        start = start + jnp.where(token >= end, doc_ref[d], 0)
    angle = (token - start).astype(F32) * freq_ref[0:1, :]
    cosine = jnp.cos(angle)
    sine = jnp.sin(angle)
    sine = jnp.where(lax.broadcasted_iota(jnp.int32, (ROWS, HD), 1) < HD // 2, -sine, sine)
    cs_ref[0] = cosine
    cs_ref[1] = sine
    cs_store = pltpu.make_async_copy(cs_ref, cs_out, own_s.at[3])
    cs_store.start()

    for h in range(NP):
        cols = slice(h * HD, (h + 1) * HD)
        key_scale = stab_ref[0, sidx_ref[0, h, block]]
        value_scale = stab_ref[1, sidx_ref[1, h, block]]
        ks[h] = turn(k_ref[:, cols].astype(F32) * key_scale, cosine, sine).astype(BF)
        vs[h] = (v_ref[:, cols].astype(F32) * value_scale).astype(BF)

    def rotate_q(p):
        for h in range(GRP):
            cols = pl.ds(pl.multiple_of(p * WIDE + h * HD, HD), HD)
            qs[p, :, h * HD:(h + 1) * HD] = turn(q_in[:, cols].astype(F32), cosine, sine).astype(BF)

    ka_ref[z, y, me] = ks[me]
    va_ref[y, z, me] = vs[me]

    pl.semaphore_wait(barrier, N_PARTNERS)

    def each_peer(fn):
        loop(1, NP, lambda d: fn((me + d) % NP))

    def k_copy(e, far):
        p, yy = (me + e % NP) % NP, (y + e // NP) % NY
        return remote(ks.at[p], ka_ref.at[z, y, me], k_s.at[far], k_r.at[far], peer(p, yy, z))

    def v_copy(p, slot):
        return remote(vs.at[p], va_ref.at[y, z, slot], v_s, v_r, peer(p, y, z))

    def go_cols(p):
        return go_ref.at[:, pl.ds(pl.multiple_of(p * WIDE, WIDE), WIDE)]

    def go_copy(p, slot):
        return remote(go_cols(p), gox_ref.at[slot], go_s, go_r, peer(p, y, z))

    def q_copy(p, slot):
        return remote(qs.at[p], qx_ref.at[slot], q_s, q_r, peer(p, y, z))

    each_peer(lambda p: v_copy(p, me).start())
    loop(1, NP, lambda e: k_copy(e, 0).start())
    loop(NP, NP * NY, lambda e: k_copy(e, 1).start())
    each_peer(lambda p: go_copy(p, me).start())
    q_load.wait()

    def rotate_and_send(p):
        rotate_q(p)
        q_copy(p, me).start()

    each_peer(rotate_and_send)
    rotate_q(me)
    own_go = pltpu.make_async_copy(go_cols(me), gox_ref.at[me], own_s.at[1])
    own_q = pltpu.make_async_copy(qs.at[me], qx_ref.at[me], own_s.at[2])
    own_go.start()
    own_q.start()

    def along(off):
        return device(x, y, c, (z + off + NZ) % NZ)

    def k_ring(s, u, rightward, sending):
        far = s if sending else s + 1
        zz = (z + NZ - far) % NZ if rightward else (z + far) % NZ
        ref = ka_ref.at[zz, pl.ds(u * (NY // 2), NY // 2)]
        if rightward:
            return remote(ref, ref, kzr_s.at[s, u], kzr_r.at[s, u], along(1))
        return remote(ref, ref, kzl_s.at[s, u], kzl_r.at[s, u], along(-1))

    def k_sends(s):
        return [(u, r) for u in range(2) for r in (True, False) if s < 3 or (u == 0) == r]

    def k_store(s, u, rightward):
        zz = (z + NZ - s) % NZ if rightward else (z + s) % NZ
        part = pl.ds(u * (NY // 2), NY // 2)
        return pltpu.make_async_copy(
            ka_ref.at[zz, part], ka_out.at[zz, part], kout_s.at[s, u if rightward else 1 - u, 0 if rightward else 1]
        )

    def v_store(yy):
        return pltpu.make_async_copy(va_ref.at[yy], va_out.at[yy], vout_s.at[yy])

    first_hops = (1, -1, 2, -2)

    def v_first(j, arriving):
        zz = (z + first_hops[j] + NZ) % NZ if arriving else z
        ref = va_ref.at[y, zz]
        return remote(ref, ref, va_s.at[j], va_r.at[j], along(-first_hops[j]))

    def v_second(j, arriving):
        off, part = ((2, None), (-2, None), (2, 0), (-2, 1))[j]
        hop = -1 if off > 0 else 1
        if part is not None:
            hop = 2 * hop
        zz = (z + off - (hop if arriving else 0) + NZ) % NZ
        ref = va_ref.at[y, zz]
        if part is not None:
            ref = va_ref.at[y, zz, pl.ds(part * (NP // 2), NP // 2)]
        return remote(ref, ref, vb_s.at[j], vb_r.at[j], along(hop))

    def v_spread(zz, d, arriving):
        yy = (y + d) % NY
        ys = yy if arriving else y
        return remote(va_ref.at[ys, zz], va_ref.at[ys, zz], vy_s, vy_r.at[ys], device(x, yy, c, z))

    def spread(off):
        for d in (2, 1, 3):
            v_spread((z + off + NZ) % NZ, d, False).start()

    settle(va_ref.at[y, z, pl.ds(0, NP - 1)], v_r)
    for j in (2, 3, 0, 1):
        v_first(j, False).start()
    spread(0)
    settle(ka_ref.at[z, 0, pl.ds(0, NP - 1)], k_r.at[0])
    settle(ka_ref.at[z, pl.ds(0, NY - 1)], k_r.at[1])
    for u, r in k_sends(0):
        k_ring(0, u, r, True).start()
    for u in range(2):
        k_store(0, u, True).start()

    lane = lax.broadcasted_iota(jnp.int32, (NP, BLK), 1)
    row = lax.broadcasted_iota(jnp.int32, (NP, BLK), 0)
    own_block = NY * NC * (row // NC) + NC * y + row % NC
    first = BLK * own_block + ROWS * z
    doc_start = jnp.zeros((NP, BLK), jnp.int32)
    end = 0
    for d in range(NDOC):
        end = end + doc_ref[d]
        doc_start = doc_start + jnp.where(first >= end, doc_ref[d], 0)
    pairs = pairs_ref[...]
    n_pairs = pairs.shape[1]
    pair_row = lax.broadcasted_iota(jnp.int32, (NP, n_pairs), 0)
    pair_q = (pairs[0:1] == NY * NC * (pair_row // NC) + NC * y + pair_row % NC).astype(F32)
    pair_k = (pairs[1:2] == lax.broadcasted_iota(jnp.int32, (BLK, n_pairs), 0)).astype(F32)
    listed = lax.dot_general(pair_q, pair_k, (((1,), (1,)), ((), ())), preferred_element_type=F32)
    wanted = ((listed > 0.5) | (lane == own_block)) & (BLK * lane + BLK - 1 >= doc_start) & (lane <= own_block)
    wanted_f = wanted.astype(F32)
    upper = (
        lax.broadcasted_iota(jnp.int32, (BLK, BLK), 0) <= lax.broadcasted_iota(jnp.int32, (BLK, BLK), 1)
    ).astype(F32)
    rank = jnp.dot(wanted_f, upper, preferred_element_type=F32)
    lane_f = lane.astype(F32)

    def list_step(r, out):
        hit = wanted & (rank.astype(jnp.int32) == r + 1)
        entry = jnp.sum(jnp.where(hit, lane_f, 0.0), axis=1, keepdims=True)
        return jnp.where(lane == r, entry, out)

    out = lax.fori_loop(0, NBLK, list_step, jnp.zeros((NP, BLK), F32))
    out = jnp.where(lane == BLK - 1, jnp.sum(wanted_f, axis=1, keepdims=True), out)
    lists_ref[...] = out.astype(jnp.int32)
    lists_store = pltpu.make_async_copy(lists_ref, lists_out, own_s.at[4])
    lists_store.start()

    def k_step(s):
        onward = k_sends(s) if s < 4 else []
        for u, r in k_sends(s - 1):
            k_ring(s - 1, u, r, False).wait_recv()
            if (u, r) in onward:
                k_ring(s, u, r, True).start()
            k_store(s, u, r).start()

    for j in (0, 1):
        v_first(j, True).wait_recv()
        spread(first_hops[j])
    for j in (2, 3):
        v_first(j, True).wait_recv()
        v_second(j, False).start()
        v_second(j - 2, False).start()
        spread(first_hops[j])
    k_step(1)
    for j in (0, 1):
        v_second(j, True).wait_recv()
        spread((3, -3)[j])
    for j in (2, 3):
        v_second(j, True).wait_recv()
    spread(4)
    v_store(y).start()
    k_step(2)
    k_step(3)
    k_step(4)

    for d in (1, 3, 2):
        settle(va_ref.at[(y + d) % NY], vy_r.at[(y + d) % NY])
        v_store((y + d) % NY).start()

    settle(gox_ref.at[pl.ds(0, NP - 1)], go_r)
    settle(qx_ref.at[pl.ds(0, NP - 1)], q_r)
    own_go.wait()
    own_q.wait()
    cs_store.wait()
    lists_store.wait()

    settle(vs.at[pl.ds(0, NP - 1)], v_s)
    settle(go_ref.at[:, pl.ds(0, (NP - 1) * WIDE)], go_s)
    settle(qs.at[pl.ds(0, NP - 1)], q_s)
    settle(ks.at[pl.ds(0, NP - 1)], k_s.at[0])
    settle(ka_ref.at[z, pl.ds(0, NY - 1)], k_s.at[1])
    settle(va_ref.at[pl.ds(0, NY - 1)], vy_s)
    for s in range(4):
        for u, r in k_sends(s):
            k_ring(s, u, r, True).wait_send()
    for j in range(4):
        v_first(j, False).wait_send()
        v_second(j, False).wait_send()

    for u in range(2):
        k_store(0, u, True).wait()
    for s in range(1, 5):
        for u, r in k_sends(s - 1):
            k_store(s, u, r).wait()
    loop(0, NY, lambda yy: v_store(yy).wait())


def heads_to_rows(ref, i):
    return jnp.concatenate([ref[i, :, h * HD:(h + 1) * HD] for h in range(GRP)], axis=0)


def rows_to_heads(ref, i, rows):
    for h in range(GRP):
        ref[i, :, h * HD:(h + 1) * HD] = rows[h * ROWS:(h + 1) * ROWS]


WIDTH = 2
SPAN = WIDTH * BLK
MOST_UNITS = NP * (NBLK // 2 // WIDTH + 1)


def attend_kernel(
    lists_in, doc_in, q_in, go_in, k_in, v_in, o_out, dq_out, dk_out, dv_out,
    lists_ref, doc_ref, q_ref, go_ref, k_ref, v_ref, o_ref, dq_ref, dk_ref, dv_ref,
    s_ref, dp_ref, o_acc, dq_acc, dk_acc, dv_acc, bounds_ref, top_ref, total_ref, mean_ref, flat_ref,
    load_s, o_s, dq_s, dk_s, dv_s,
):
    _, y, _, z = place()
    rows = GRP * ROWS
    loads = [
        pltpu.make_async_copy(src, dst, load_s.at[n])
        for n, (src, dst) in enumerate(((q_in, q_ref), (k_in, k_ref), (go_in, go_ref), (v_in, v_ref)))
    ]
    small = [
        pltpu.make_async_copy(src, dst, load_s.at[n])
        for n, (src, dst) in ((4, (lists_in, lists_ref)), (5, (doc_in, doc_ref)))
    ]
    for load in small + loads:
        load.start()

    def o_store(g):
        return pltpu.make_async_copy(o_ref.at[g], o_out.at[g], o_s.at[g])

    def dq_store(g):
        return pltpu.make_async_copy(dq_ref.at[g], dq_out.at[g], dq_s.at[g])

    def dk_store(zz):
        return pltpu.make_async_copy(dk_ref.at[zz], dk_out.at[zz], dk_s.at[zz])

    def dv_store(yy):
        return pltpu.make_async_copy(dv_ref.at[yy], dv_out.at[yy], dv_s.at[yy])

    for ref in (total_ref, mean_ref, o_acc, dq_acc, dk_acc, dv_acc):
        ref[...] = jnp.zeros_like(ref)
    top_ref[...] = jnp.full_like(top_ref, NEG)
    for load in small:
        load.wait()

    def list_group(g, base):
        count = (lists_ref[g, BLK - 1] + WIDTH - 1) // WIDTH

        def put(n):
            flat_ref[base + n] = n * NP + g

        loop(0, count, put)
        return base + count

    units = lax.fori_loop(0, NP, list_group, 0)
    for u in range(UNROLL):
        flat_ref[units + u] = NBLK * NP
    steps = (units + UNROLL - 1) // UNROLL

    lane = lax.broadcasted_iota(jnp.int32, (1, rows), 1)
    for g in range(NP):
        token = BLK * (NY * NC * (g // NC) + NC * y + g % NC) + ROWS * z + lane % ROWS
        start = jnp.zeros((1, rows), jnp.int32)
        end = 0
        for d in range(NDOC):
            end = end + doc_ref[d]
            start = start + jnp.where(token >= end, doc_ref[d], 0)
        bounds_ref[g, 0:1] = start
        bounds_ref[g, 1:2] = token
    key_row = lax.broadcasted_iota(jnp.int32, (BLK, rows), 0)
    nt = (((1,), (1,)), ((), ()))
    tn = (((0,), (0,)), ((), ()))
    for load in loads:
        load.wait()

    def units_of(n):
        out = []
        for u in range(UNROLL):
            entry = flat_ref[n * UNROLL + u]
            g, first = entry % NP, entry // NP * WIDTH
            count = lists_ref[g, BLK - 1]
            parts = []
            for w in range(WIDTH):
                live = first + w < count
                b = lists_ref[g, jnp.where(live, first + w, 0)]
                parts.append((live, b, (b // NC) % NY, (b // (NY * NC)) * NC + b % NC))
            out.append((n * UNROLL + u, g, parts))
        return out

    def keys_at(parts):
        return jnp.concatenate([k_ref[:, yb, ib].reshape(BLK, HD) for _, _, yb, ib in parts], axis=0)

    def values_at(parts):
        return jnp.concatenate([v_ref[yb, :, ib].reshape(BLK, HD) for _, _, yb, ib in parts], axis=0)

    def fold(x):
        return x.reshape(x.shape[0] // 8, 8, rows)

    def score_step(n):
        for t, g, parts in units_of(n):
            scores = lax.dot_general(keys_at(parts), heads_to_rows(q_ref, g), nt, preferred_element_type=F32)
            dp_ref[t] = lax.dot_general(values_at(parts), heads_to_rows(go_ref, g), nt, preferred_element_type=F32)
            top = top_ref[g]
            for w, (live, b, _, _) in enumerate(parts):
                low = jnp.where(live, bounds_ref[g, 0:1] - BLK * b, BLK)
                allowed = (key_row >= low) & (key_row <= bounds_ref[g, 1:2] - BLK * b)
                part = jnp.where(allowed, scores[w * BLK:(w + 1) * BLK], NEG)
                s_ref[t, w * BLK:(w + 1) * BLK] = part
                top = jnp.maximum(top, jnp.max(fold(part), axis=0))
            top_ref[g] = top

    loop(0, steps, score_step)
    for g in range(NP):
        top_ref[g] = jnp.broadcast_to(jnp.max(top_ref[g], axis=0, keepdims=True), (8, rows))

    def out_step(n):
        for t, g, parts in units_of(n):
            weights = jnp.exp2((s_ref[t] - top_ref[g, 0:1]) * EXP2_SCALE)
            s_ref[t] = weights
            total_ref[g] += jnp.sum(fold(weights), axis=0)
            mean_ref[g] += jnp.sum(fold(weights * dp_ref[t]), axis=0)
            o_acc[g] += lax.dot_general(values_at(parts), weights.astype(BF), tn, preferred_element_type=F32)

    loop(0, steps, out_step)
    for g in range(NP):
        inverse = 1.0 / jnp.sum(total_ref[g], axis=0, keepdims=True)
        total_ref[g, 0:1] = inverse
        mean_ref[g, 0:1] = jnp.sum(mean_ref[g], axis=0, keepdims=True) * inverse
        rows_to_heads(o_ref, g, (o_acc[g] * inverse).astype(BF).T)
        o_store(g).start()

    def grad_step(n):
        for t, g, parts in units_of(n):
            probs = s_ref[t] * total_ref[g, 0:1]
            grad_scores = (probs * (dp_ref[t] - mean_ref[g, 0:1])).astype(BF)
            dv = jnp.dot(probs.astype(BF), heads_to_rows(go_ref, g), preferred_element_type=F32)
            dk = jnp.dot(grad_scores, heads_to_rows(q_ref, g), preferred_element_type=F32)
            dq_acc[g] += lax.dot_general(keys_at(parts), grad_scores, tn, preferred_element_type=F32)
            for w, (_, _, yb, ib) in enumerate(parts):
                dv_acc[yb, :, ib] += dv[w * BLK:(w + 1) * BLK].reshape(NZ, ROWS, HD)
                dk_acc[:, yb, ib] += dk[w * BLK:(w + 1) * BLK].reshape(NZ, ROWS, HD)

    loop(0, steps, grad_step)

    def finish_k(zz):
        dk_ref[zz] = (dk_acc[zz] * SCALE).astype(BF)
        dk_store(zz).start()

    def finish_v(yy):
        dv_ref[yy] = dv_acc[yy].astype(BF)
        dv_store(yy).start()

    loop(0, NZ, finish_k)
    loop(0, NY, finish_v)
    for g in range(NP):
        rows_to_heads(dq_ref, g, (dq_acc[g] * SCALE).astype(BF).T)
        dq_store(g).start()
    for g in range(NP):
        o_store(g).wait()
        dq_store(g).wait()
    loop(0, NZ, lambda zz: dk_store(zz).wait())
    loop(0, NY, lambda yy: dv_store(yy).wait())


def scatter_kernel(
    o_ref, dq_ref, dk_hbm, dv_ref,
    ao_ref, dqx, k_in, v_in,
    dk_ref, dv_own, kr_out, kl_out, kr_in, kl_in, va_out, va_in, vb_out, vb_in, k_out, vy_in, v_out,
    o_s, o_r, q_s, q_r, kzr_s, kzr_r, kzl_s, kzl_r, va_s, va_r, vb_s, vb_r,
    vy_s, vy_r, k_s, k_r, v_s, v_r, own_s,
):
    x, y, c, z = place()
    me = NC * x + c
    dk_load = pltpu.make_async_copy(dk_hbm, dk_ref, own_s.at[2])
    dv_load = pltpu.make_async_copy(dv_ref.at[y], dv_own, own_s.at[3])
    dk_load.start()
    dv_load.start()
    barrier = enter(me, x, y, c, z)
    pl.semaphore_wait(barrier, N_PARTNERS)

    def each_peer(fn):
        loop(1, NP, lambda d: fn((me + d) % NP))

    def along(off):
        return device(x, y, c, (z + off + NZ) % NZ)

    def head_cols(ref, g):
        return ref.at[:, pl.ds(pl.multiple_of(g * WIDE, WIDE), WIDE)]

    def o_copy(p, slot):
        return remote(o_ref.at[p], head_cols(ao_ref, slot), o_s, o_r, peer(p, y, z))

    def q_copy(p, slot):
        return remote(dq_ref.at[p], dqx.at[slot], q_s, q_r, peer(p, y, z))

    def vy_copy(off, d, arriving):
        zz, yy = (z + off + NZ) % NZ, (y + d) % NY
        slot = yy if arriving else y
        return remote(dv_ref.at[yy, zz], vy_in.at[slot, zz], vy_s, vy_r.at[zz], device(x, yy, c, z))

    half = NY // 2

    def k_ring(s, u, rightward):
        if rightward:
            return remote(kr_out.at[s, u], kr_in.at[s, u], kzr_s.at[s, u], kzr_r.at[s, u], along(1))
        return remote(kl_out.at[s, u], kl_in.at[s, u], kzl_s.at[s, u], kzl_r.at[s, u], along(-1))

    def k_part(zz, u):
        return dk_ref[zz, u * half:(u + 1) * half].astype(F32)

    def k_send(s, u, rightward):
        zz = (z + 4 - s) % NZ if rightward else (z + 4 + s) % NZ
        total = k_part(zz, u)
        if s > 1 or (s == 1 and (u == 0) == rightward):
            k_ring(s - 1, u, rightward).wait_recv()
            total = total + (kr_in if rightward else kl_in)[s - 1, u].astype(F32)
        (kr_out if rightward else kl_out)[s, u] = total.astype(BF)
        k_ring(s, u, rightward).start()

    def v_part(off):
        zz = (z + off + NZ) % NZ
        total = dv_own[zz].astype(F32)
        settle(dv_own.at[pl.ds(0, NY - 1)], vy_r.at[zz])
        for d in range(1, NY):
            total = total + vy_in[(y + d) % NY, zz].astype(F32)
        return total

    cut = NP // 2

    def v_far(j):
        hop = (1, -1, 2, -2)[j]
        if j < 2:
            return remote(va_out.at[j], va_in.at[j], va_s.at[j], va_r.at[j], along(hop))
        part = pl.ds(0 if j == 2 else cut, cut)
        return remote(va_out.at[2, part], va_in.at[2, part], va_s.at[j], va_r.at[j], along(hop))

    near = (1, -1, 2, -2)

    def v_near(j):
        return remote(vb_out.at[j], vb_in.at[j], vb_s.at[j], vb_r.at[j], along(near[j]))

    order = (3, -3, 4, 2, -2, 1, -1, 0)
    for off in order[:3]:
        for d in (2, 1, 3):
            vy_copy(off, d, False).start()
    dk_load.wait()
    k_send(0, 0, True)
    k_send(0, 1, False)
    k_send(1, 1, True)
    k_send(1, 0, False)
    for off in order[3:]:
        for d in (2, 1, 3):
            vy_copy(off, d, False).start()
    each_peer(lambda p: o_copy(p, me).start())
    each_peer(lambda p: q_copy(p, me).start())
    own_o = pltpu.make_async_copy(o_ref.at[me], head_cols(ao_ref, me), own_s.at[0])
    own_q = pltpu.make_async_copy(dq_ref.at[me], dqx.at[me], own_s.at[1])
    own_o.start()
    own_q.start()

    dv_load.wait()
    k_send(1, 0, True)
    k_send(1, 1, False)
    va_out[0] = v_part(3).astype(BF)
    v_far(0).start()
    va_out[1] = v_part(-3).astype(BF)
    v_far(1).start()
    va_out[2] = v_part(4).astype(BF)
    v_far(2).start()
    v_far(3).start()
    for u, r in ((1, True), (0, False), (0, True), (1, False)):
        k_send(2, u, r)
    v_two = [v_part(2), v_part(-2)]
    for j in range(2):
        v_far(j).wait_recv()
        v_far(j + 2).wait_recv()
        total = v_two[j] + va_in[j].astype(F32)
        low, high = total[:cut], total[cut:]
        if j == 0:
            low = low + va_in[2, :cut].astype(F32)
        else:
            high = high + va_in[2, cut:].astype(F32)
        vb_out[j + 2, :cut] = low.astype(BF)
        vb_out[j + 2, cut:] = high.astype(BF)
        v_near(j + 2).start()
    for j in range(2):
        vb_out[j] = v_part(near[j]).astype(BF)
        v_near(j).start()
    for u, r in ((1, True), (0, False), (0, True), (1, False)):
        k_send(3, u, r)

    def k_copy(e, far):
        p, yy = (me + e % NP) % NP, (y + e // NP) % NY
        return remote(k_out.at[yy, p], k_in.at[y, me], k_s.at[far], k_r.at[far], peer(p, yy, z))

    def v_copy(p, slot):
        return remote(v_out.at[p], v_in.at[slot], v_s, v_r, peer(p, y, z))

    v_total = v_part(0)
    for j in range(4):
        v_near(j).wait_recv()
        v_total = v_total + vb_in[j].astype(F32)
    v_out[...] = v_total.astype(BF)
    each_peer(lambda p: v_copy(p, me).start())
    own_v = pltpu.make_async_copy(v_out.at[me], v_in.at[me], own_s.at[4])
    own_v.start()

    for u in range(2):
        k_ring(3, u, True).wait_recv()
        k_ring(3, u, False).wait_recv()
        total = k_part(z, u) + kr_in[3, u].astype(F32) + kl_in[3, u].astype(F32)
        k_out[u * half:(u + 1) * half] = total.astype(BF)
    loop(1, NP, lambda e: k_copy(e, 0).start())
    loop(NP, NP * NY, lambda e: k_copy(e, 1).start())

    own_k = pltpu.make_async_copy(k_out.at[y, me], k_in.at[y, me], own_s.at[5])
    own_k.start()
    settle(v_in.at[pl.ds(0, NP - 1)], v_r)
    settle(o_ref.at[pl.ds(0, NP - 1)], o_r)
    settle(dqx.at[pl.ds(0, NP - 1)], q_r)
    own_o.wait()
    own_q.wait()
    own_v.wait()
    own_k.wait()

    settle(o_ref.at[pl.ds(0, NP - 1)], o_s)
    settle(dq_ref.at[pl.ds(0, NP - 1)], q_s)
    settle(v_out.at[pl.ds(0, NP - 1)], v_s)
    settle(k_out.at[0, pl.ds(0, NP - 1)], k_s.at[0])
    settle(k_out.at[pl.ds(0, NY - 1)], k_s.at[1])
    settle(dv_ref.at[pl.ds(0, NY - 1)], vy_s)
    for s in range(4):
        for u in range(2):
            for r in (True, False):
                if s or (u == 0) == r:
                    k_ring(s, u, r).wait_send()
    for j in range(4):
        v_far(j).wait_send()
        v_near(j).wait_send()
    settle(k_in.at[0, pl.ds(0, NP - 1)], k_r.at[0])
    settle(k_in.at[pl.ds(0, NY - 1)], k_r.at[1])


def finish_kernel(
    ao_ref, dq_ref, k_ref, v_ref, cs_ref, sidx_ref, stab_ref,
    ao_out, gq_out, gk_out, gv_out,
    gq_ref, gk_ref, gv_ref, sems, gq_s,
):
    block = lax.axis_index("ctx")
    ao_store, gk_store, gv_store = [
        pltpu.make_async_copy(src, dst, sems.at[n])
        for n, (src, dst) in enumerate(((ao_ref, ao_out), (gk_ref, gk_out), (gv_ref, gv_out)))
    ]
    ao_store.start()

    def store(p):
        cols = pl.ds(pl.multiple_of(p * WIDE, WIDE), WIDE)
        return pltpu.make_async_copy(gq_ref.at[:, cols], gq_out.at[:, cols], gq_s.at[p])

    cosine, sine = cs_ref[0], -cs_ref[1]

    def rotate_back(p):
        for h in range(GRP):
            cols = pl.ds(pl.multiple_of(p * WIDE + h * HD, HD), HD)
            gq_ref[:, cols] = turn(dq_ref[p, :, h * HD:(h + 1) * HD].astype(F32), cosine, sine).astype(BF)
        store(p).start()

    loop(0, NP, rotate_back)
    for h in range(NP):
        cols = slice(h * HD, (h + 1) * HD)
        value_scale = stab_ref[1, sidx_ref[1, h, block]]
        gv_ref[:, cols] = (v_ref[h].astype(F32) * value_scale).astype(BF)
        key_scale = stab_ref[0, sidx_ref[0, h, block]]
        total = k_ref[0, h].astype(F32)
        for yy in range(1, NY):
            total = total + k_ref[yy, h].astype(F32)
        gk_ref[:, cols] = (turn(total, cosine, sine) * key_scale).astype(BF)
    gv_store.start()
    gk_store.start()
    ao_store.wait()
    loop(0, NP, lambda p: store(p).wait())
    gv_store.wait()
    gk_store.wait()


def body(queries, keys, values, grad_out, doc_lengths, block_pairs, scale_index, scale_table):
    half = np.arange(HD // 2, dtype=np.float32) * np.float32(-2.0 * math.log(500000.0) / HD)
    freq = np.exp(half.astype(np.float32)).astype(np.float32)
    freq = jnp.asarray(np.tile(np.concatenate([freq, freq])[None], (8, 1)))
    scale_by_head = scale_index.transpose(0, 2, 1)
    vmem = pl.BlockSpec(memory_space=pltpu.VMEM)
    anywhere = pl.BlockSpec(memory_space=pl.ANY)
    smem = pl.BlockSpec(memory_space=pltpu.SMEM)
    dma = pltpu.SemaphoreType.DMA
    shape = jax.ShapeDtypeStruct
    qx, gox, ka, va, lists, cs = pl.pallas_call(
        gather_kernel,
        name="gather",
        out_shape=(
            shape((NP, ROWS, WIDE), BF),
            shape((NP, ROWS, WIDE), BF),
            shape((NZ, NY, NP, ROWS, HD), BF),
            shape((NY, NZ, NP, ROWS, HD), BF),
            shape((NP, BLK), jnp.int32),
            shape((2, ROWS, HD), F32),
        ),
        in_specs=[anywhere] * 9,
        out_specs=(anywhere,) * 6,
        scratch_shapes=[
            pltpu.VMEM((ROWS, NP * HD), BF),
            pltpu.VMEM((ROWS, NP * HD), BF),
            pltpu.SMEM(doc_lengths.shape, jnp.int32),
            pltpu.VMEM(block_pairs.shape[::-1], jnp.int32),
            pltpu.SMEM(scale_by_head.shape, jnp.int32),
            pltpu.SMEM(scale_table.shape, F32),
            pltpu.VMEM(freq.shape, F32),
            pltpu.VMEM((NP, BLK), jnp.int32),
            pltpu.VMEM((2, ROWS, HD), F32),
            pltpu.VMEM((ROWS, NP * WIDE), BF),
            pltpu.VMEM((NP, ROWS, WIDE), BF),
            pltpu.VMEM((NP, ROWS, HD), BF),
            pltpu.VMEM((NP, ROWS, HD), BF),
            pltpu.VMEM((NZ, NY, NP, ROWS, HD), BF),
            pltpu.VMEM((NY, NZ, NP, ROWS, HD), BF),
        ]
        + [dma] * 4
        + [dma((2,))] * 2
        + [dma] * 2
        + [dma((4, 2))] * 4
        + [dma((4,))] * 4
        + [dma, dma((NY,))]
        + [dma((5,)), dma((5, 2, 2)), dma((NY,)), dma((7,))],
        compiler_params=pltpu.CompilerParams(
            collective_id=0, has_side_effects=True, vmem_limit_bytes=VMEM_LIMIT
        ),
    )(queries, keys, values, grad_out, doc_lengths, block_pairs.T, scale_by_head, scale_table, freq)

    o, dq, dk, dv = pl.pallas_call(
        attend_kernel,
        name="attend",
        out_shape=(
            shape((NP, ROWS, WIDE), BF),
            shape((NP, ROWS, WIDE), BF),
            shape((NZ, NY, NP, ROWS, HD), BF),
            shape((NY, NZ, NP, ROWS, HD), BF),
        ),
        in_specs=[anywhere] * 6,
        out_specs=(anywhere,) * 4,
        scratch_shapes=[pltpu.SMEM((NP, BLK), jnp.int32), pltpu.SMEM(doc_lengths.shape, jnp.int32)]
        + ([pltpu.VMEM((NP, ROWS, WIDE), BF)] * 2
        + [pltpu.VMEM((NZ, NY, NP, ROWS, HD), BF), pltpu.VMEM((NY, NZ, NP, ROWS, HD), BF)]) * 2
        + [pltpu.VMEM((MOST_UNITS + UNROLL, SPAN, GRP * ROWS), F32)] * 2
        + [pltpu.VMEM((NP, HD, GRP * ROWS), F32)] * 2
        + [pltpu.VMEM((NZ, NY, NP, ROWS, HD), F32), pltpu.VMEM((NY, NZ, NP, ROWS, HD), F32)]
        + [pltpu.VMEM((NP, 8, GRP * ROWS), jnp.int32)]
        + [pltpu.VMEM((NP, 8, GRP * ROWS), F32)] * 3
        + [pltpu.SMEM((MOST_UNITS + UNROLL,), jnp.int32)]
        + [dma((6,)), dma((NP,)), dma((NP,)), dma((NZ,)), dma((NY,))],
        compiler_params=pltpu.CompilerParams(vmem_limit_bytes=VMEM_LIMIT),
    )(lists, doc_lengths, qx, gox, ka, va)

    ao, dqx, k_terms, v_sums = pl.pallas_call(
        scatter_kernel,
        name="scatter",
        out_shape=(
            shape((ROWS, NP * WIDE), BF),
            shape((NP, ROWS, WIDE), BF),
            shape((NY, NP, ROWS, HD), BF),
            shape((NP, ROWS, HD), BF),
        ),
        in_specs=[anywhere] * 4,
        out_specs=(anywhere,) * 4,
        scratch_shapes=[pltpu.VMEM((NZ, NY, NP, ROWS, HD), BF), pltpu.VMEM((NZ, NP, ROWS, HD), BF)]
        + [pltpu.VMEM((4, 2, NY // 2, NP, ROWS, HD), BF)] * 4
        + [pltpu.VMEM((3, NP, ROWS, HD), BF)] * 2
        + [pltpu.VMEM((4, NP, ROWS, HD), BF)] * 2
        + [pltpu.VMEM((NY, NP, ROWS, HD), BF)]
        + [pltpu.VMEM((NY, NZ, NP, ROWS, HD), BF)]
        + [pltpu.VMEM((NP, ROWS, HD), BF)]
        + [dma] * 4
        + [dma((4, 2))] * 4
        + [dma((4,))] * 4
        + [dma, dma((NZ,))]
        + [dma((2,))] * 2
        + [dma] * 2
        + [dma((6,))],
        compiler_params=pltpu.CompilerParams(
            collective_id=1, has_side_effects=True, vmem_limit_bytes=VMEM_LIMIT
        ),
    )(o, dq, dk, dv)

    return pl.pallas_call(
        finish_kernel,
        name="finish",
        out_shape=(
            shape((ROWS, NP * WIDE), BF),
            shape((ROWS, NP * WIDE), BF),
            shape((ROWS, NP * HD), BF),
            shape((ROWS, NP * HD), BF),
        ),
        in_specs=[vmem] * 5 + [smem] * 2,
        out_specs=(anywhere,) * 4,
        scratch_shapes=[
            pltpu.VMEM((ROWS, NP * WIDE), BF),
            pltpu.VMEM((ROWS, NP * HD), BF),
            pltpu.VMEM((ROWS, NP * HD), BF),
            dma((3,)),
            dma((NP,)),
        ],
        compiler_params=pltpu.CompilerParams(vmem_limit_bytes=VMEM_LIMIT),
    )(ao, dqx, k_terms, v_sums, cs, scale_by_head, scale_table)


def solution(mesh):
    rows = P(("ctx", "head"), None)
    in_specs = (rows,) * 4 + (P(),) * 4
    return jax.shard_map(body, mesh=mesh, in_specs=in_specs, out_specs=(rows,) * 4, check_vma=False)
```

```python
import functools
import math

import jax
import jax.numpy as jnp
import numpy as np
from jax import lax
from jax.experimental import pallas as pl
from jax.experimental.pallas import tpu as pltpu
from jax.sharding import PartitionSpec as P

HD = 128
BLK = 128
ROWS = 16
GRP = 16
NX, NY, NC, NZ = 4, 4, 2, 8
NP = NX * NC
NBLK = 32
NDOC = 8
WIDE = GRP * HD
NEG = -1e30
UNROLL = 7
SCALE = 1.0 / math.sqrt(HD)
EXP2_SCALE = SCALE * math.log2(math.e)
MESH = pl.DeviceIdType.MESH
BF = jnp.bfloat16
F32 = jnp.float32
VMEM_LIMIT = 56 * 1024 * 1024


def place():
    ctx = lax.axis_index("ctx")
    return ctx // (NY * NC), (ctx // NC) % NY, ctx % NC, lax.axis_index("head")


def device(xx, yy, cc, zz):
    return {"ctx": xx * (NY * NC) + yy * NC + cc, "head": zz}


def peer(p, y, z):
    return device(p // NC, y, p % NC, z)


def remote(src, dst, send_sem, recv_sem, dev):
    return pltpu.make_async_remote_copy(
        src_ref=src, dst_ref=dst, send_sem=send_sem, recv_sem=recv_sem, device_id=dev, device_id_type=MESH
    )


def enter(me, x, y, c, z):
    barrier = pltpu.get_barrier_semaphore()

    def greet(dev):
        pl.semaphore_signal(barrier, inc=1, device_id=dev, device_id_type=MESH)

    for off in (2, NZ - 2, 1, NZ - 1):
        greet(device(x, y, c, (z + off) % NZ))

    def step(e, carry):
        greet(peer((me + e % NP) % NP, (y + e // NP) % NY, z))
        return carry

    lax.fori_loop(1, NP * NY, step, 0)
    return barrier


N_PARTNERS = NP * NY - 1 + 4


def loop(lo, hi, fn):
    def step(i, carry):
        fn(i)
        return carry

    lax.fori_loop(lo, hi, step, 0)


def by_reach(less, fn):
    pl.when(less)(lambda: fn(NP - NC))
    pl.when(jnp.logical_not(less))(lambda: fn(NP))


def settle(ref, sem):
    pltpu.make_async_copy(ref, ref, sem).wait()


def turn(x, cosine, sine):
    return x * cosine + pltpu.roll(x, HD // 2, 1) * sine


def gather_kernel(
    q_ref, k_hbm, v_hbm, go_ref, doc_hbm, pairs_hbm, sidx_hbm, stab_hbm, freq_hbm,
    qx_ref, gox_ref, ka_out, va_out, lists_out, cs_out,
    k_ref, v_ref, doc_ref, pairs_ref, sidx_ref, stab_ref, freq_ref, lists_ref, cs_ref, q_in, qs, ks, vs, ka_ref, va_ref,
    q_s, q_r, go_s, go_r, k_s, k_r, v_s, v_r, kzr_s, kzr_r, kzl_s, kzl_r,
    va_s, va_r, vb_s, vb_r, vy_s, vy_r, own_s, kout_s, vout_s, load_s,
):
    x, y, c, z = place()
    me = NC * x + c
    block = lax.axis_index("ctx")
    va_ref[:, :, NP - NC:] = jnp.zeros((NY, NZ, NC, ROWS, HD), BF)
    loads = [
        pltpu.make_async_copy(src, dst, load_s.at[n])
        for n, (src, dst) in enumerate((
            (doc_hbm, doc_ref), (freq_hbm, freq_ref), (k_hbm, k_ref), (v_hbm, v_ref),
            (sidx_hbm, sidx_ref), (stab_hbm, stab_ref), (pairs_hbm, pairs_ref),
        ))
    ]
    for load in loads:
        load.start()
    q_load = pltpu.make_async_copy(q_ref, q_in, own_s.at[0])
    q_load.start()
    barrier = enter(me, x, y, c, z)
    for load in loads:
        load.wait()

    token = BLK * block + ROWS * z + lax.broadcasted_iota(jnp.int32, (ROWS, HD), 0)
    start = jnp.zeros((ROWS, HD), jnp.int32)
    end = 0
    for d in range(NDOC):
        end = end + doc_ref[d]
        start = start + jnp.where(token >= end, doc_ref[d], 0)
    angle = (token - start).astype(F32) * freq_ref[0:1, :]
    cosine = jnp.cos(angle)
    sine = jnp.sin(angle)
    sine = jnp.where(lax.broadcasted_iota(jnp.int32, (ROWS, HD), 1) < HD // 2, -sine, sine)
    cs_ref[0] = cosine
    cs_ref[1] = sine
    cs_store = pltpu.make_async_copy(cs_ref, cs_out, own_s.at[3])
    cs_store.start()

    for h in range(NP):
        cols = slice(h * HD, (h + 1) * HD)
        key_scale = stab_ref[0, sidx_ref[0, h, block]]
        value_scale = stab_ref[1, sidx_ref[1, h, block]]
        ks[h] = turn(k_ref[:, cols].astype(F32) * key_scale, cosine, sine).astype(BF)
        vs[h] = (v_ref[:, cols].astype(F32) * value_scale).astype(BF)

    def rotate_q(p):
        for h in range(GRP):
            cols = pl.ds(pl.multiple_of(p * WIDE + h * HD, HD), HD)
            qs[p, :, h * HD:(h + 1) * HD] = turn(q_in[:, cols].astype(F32), cosine, sine).astype(BF)

    ka_ref[z, y, me] = ks[me]
    va_ref[y, z, me] = vs[me]

    pl.semaphore_wait(barrier, N_PARTNERS)

    def each_peer(fn):
        loop(1, NP, lambda d: fn((me + d) % NP))

    def k_copy(e, far):
        p, yy = (me + e % NP) % NP, (y + e // NP) % NY
        return remote(ks.at[p], ka_ref.at[z, y, me], k_s.at[far], k_r.at[far], peer(p, yy, z))

    def v_copy(p, slot):
        return remote(vs.at[p], va_ref.at[y, z, slot], v_s, v_r, peer(p, y, z))

    def go_cols(p):
        return go_ref.at[:, pl.ds(pl.multiple_of(p * WIDE, WIDE), WIDE)]

    def go_copy(p, slot):
        return remote(go_cols(p), gox_ref.at[slot], go_s, go_r, peer(p, y, z))

    def q_copy(p, slot):
        return remote(qs.at[p], qx_ref.at[slot], q_s, q_r, peer(p, y, z))

    each_peer(lambda p: v_copy(p, me).start())
    loop(1, NP, lambda e: k_copy(e, 0).start())
    loop(NP, NP * NY, lambda e: k_copy(e, 1).start())
    each_peer(lambda p: go_copy(p, me).start())
    q_load.wait()

    def rotate_and_send(p):
        rotate_q(p)
        q_copy(p, me).start()

    each_peer(rotate_and_send)
    rotate_q(me)
    own_go = pltpu.make_async_copy(go_cols(me), gox_ref.at[me], own_s.at[1])
    own_q = pltpu.make_async_copy(qs.at[me], qx_ref.at[me], own_s.at[2])
    own_go.start()
    own_q.start()

    def along(off):
        return device(x, y, c, (z + off + NZ) % NZ)

    def k_ring(s, u, rightward, sending):
        far = s if sending else s + 1
        zz = (z + NZ - far) % NZ if rightward else (z + far) % NZ
        ref = ka_ref.at[zz, pl.ds(u * (NY // 2), NY // 2)]
        if rightward:
            return remote(ref, ref, kzr_s.at[s, u], kzr_r.at[s, u], along(1))
        return remote(ref, ref, kzl_s.at[s, u], kzl_r.at[s, u], along(-1))

    def k_sends(s):
        return [(u, r) for u in range(2) for r in (True, False) if s < 3 or (u == 0) == r]

    def k_store(s, u, rightward):
        zz = (z + NZ - s) % NZ if rightward else (z + s) % NZ
        part = pl.ds(u * (NY // 2), NY // 2)
        return pltpu.make_async_copy(
            ka_ref.at[zz, part], ka_out.at[zz, part], kout_s.at[s, u if rightward else 1 - u, 0 if rightward else 1]
        )

    def v_store(yy):
        return pltpu.make_async_copy(va_ref.at[yy], va_out.at[yy], vout_s.at[yy])

    first_hops = (1, -1, 2, -2)

    def v_first(j, arriving):
        zz = (z + first_hops[j] + NZ) % NZ if arriving else z
        ref = va_ref.at[y, zz]
        return remote(ref, ref, va_s.at[j], va_r.at[j], along(-first_hops[j]))

    def v_second(j, arriving):
        off, part = ((2, None), (-2, None), (2, 0), (-2, 1))[j]
        hop = -1 if off > 0 else 1
        if part is not None:
            hop = 2 * hop
        zz = (z + off - (hop if arriving else 0) + NZ) % NZ
        ref = va_ref.at[y, zz]
        if part is not None:
            ref = va_ref.at[y, zz, pl.ds(part * (NP // 2), NP // 2)]
        return remote(ref, ref, vb_s.at[j], vb_r.at[j], along(hop))

    def v_spread(zz, d):
        yy = (y + d) % NY

        def start(n):
            ref = va_ref.at[y, zz, pl.ds(0, n)]
            remote(ref, ref, vy_s.at[d], vy_r.at[y], device(x, yy, c, z)).start()

        by_reach(yy < y, start)

    def spread(off):
        for d in (2, 1, 3):
            v_spread((z + off + NZ) % NZ, d)

    settle(va_ref.at[y, z, pl.ds(0, NP - 1)], v_r)
    for j in (2, 3, 0, 1):
        v_first(j, False).start()
    spread(0)
    settle(ka_ref.at[z, 0, pl.ds(0, NP - 1)], k_r.at[0])
    settle(ka_ref.at[z, pl.ds(0, NY - 1)], k_r.at[1])
    for u, r in k_sends(0):
        k_ring(0, u, r, True).start()
    for u in range(2):
        k_store(0, u, True).start()

    lane = lax.broadcasted_iota(jnp.int32, (NP, BLK), 1)
    row = lax.broadcasted_iota(jnp.int32, (NP, BLK), 0)
    own_block = NY * NC * (row // NC) + NC * y + row % NC
    first = BLK * own_block + ROWS * z
    doc_start = jnp.zeros((NP, BLK), jnp.int32)
    end = 0
    for d in range(NDOC):
        end = end + doc_ref[d]
        doc_start = doc_start + jnp.where(first >= end, doc_ref[d], 0)
    pairs = pairs_ref[...]
    n_pairs = pairs.shape[1]
    pair_row = lax.broadcasted_iota(jnp.int32, (NP, n_pairs), 0)
    pair_q = (pairs[0:1] == NY * NC * (pair_row // NC) + NC * y + pair_row % NC).astype(F32)
    pair_k = (pairs[1:2] == lax.broadcasted_iota(jnp.int32, (BLK, n_pairs), 0)).astype(F32)
    listed = lax.dot_general(pair_q, pair_k, (((1,), (1,)), ((), ())), preferred_element_type=F32)
    wanted = ((listed > 0.5) | (lane == own_block)) & (BLK * lane + BLK - 1 >= doc_start) & (lane <= own_block)
    wanted_f = wanted.astype(F32)
    upper = (
        lax.broadcasted_iota(jnp.int32, (BLK, BLK), 0) <= lax.broadcasted_iota(jnp.int32, (BLK, BLK), 1)
    ).astype(F32)
    rank = jnp.dot(wanted_f, upper, preferred_element_type=F32)
    lane_f = lane.astype(F32)

    def list_step(r, out):
        hit = wanted & (rank.astype(jnp.int32) == r + 1)
        entry = jnp.sum(jnp.where(hit, lane_f, 0.0), axis=1, keepdims=True)
        return jnp.where(lane == r, entry, out)

    out = lax.fori_loop(0, NBLK, list_step, jnp.zeros((NP, BLK), F32))
    out = jnp.where(lane == BLK - 1, jnp.sum(wanted_f, axis=1, keepdims=True), out)
    lists_ref[...] = out.astype(jnp.int32)
    lists_store = pltpu.make_async_copy(lists_ref, lists_out, own_s.at[4])
    lists_store.start()

    def k_step(s):
        onward = k_sends(s) if s < 4 else []
        for u, r in k_sends(s - 1):
            k_ring(s - 1, u, r, False).wait_recv()
            if (u, r) in onward:
                k_ring(s, u, r, True).start()
            k_store(s, u, r).start()

    for j in (0, 1):
        v_first(j, True).wait_recv()
        spread(first_hops[j])
    for j in (2, 3):
        v_first(j, True).wait_recv()
        v_second(j, False).start()
        v_second(j - 2, False).start()
        spread(first_hops[j])
    k_step(1)
    for j in (0, 1):
        v_second(j, True).wait_recv()
        spread((3, -3)[j])
    for j in (2, 3):
        v_second(j, True).wait_recv()
    spread(4)
    v_store(y).start()
    k_step(2)
    k_step(3)
    k_step(4)

    for d in (1, 3, 2):
        yy = (y + d) % NY
        by_reach(y < yy, lambda n: settle(va_ref.at[yy, :, pl.ds(0, n)], vy_r.at[yy]))
        v_store(yy).start()

    settle(gox_ref.at[pl.ds(0, NP - 1)], go_r)
    settle(qx_ref.at[pl.ds(0, NP - 1)], q_r)
    own_go.wait()
    own_q.wait()
    cs_store.wait()
    lists_store.wait()

    settle(vs.at[pl.ds(0, NP - 1)], v_s)
    settle(go_ref.at[:, pl.ds(0, (NP - 1) * WIDE)], go_s)
    settle(qs.at[pl.ds(0, NP - 1)], q_s)
    settle(ks.at[pl.ds(0, NP - 1)], k_s.at[0])
    settle(ka_ref.at[z, pl.ds(0, NY - 1)], k_s.at[1])
    for d in range(1, NY):
        by_reach((y + d) % NY < y, lambda n: settle(va_ref.at[y, :, pl.ds(0, n)], vy_s.at[d]))
    for s in range(4):
        for u, r in k_sends(s):
            k_ring(s, u, r, True).wait_send()
    for j in range(4):
        v_first(j, False).wait_send()
        v_second(j, False).wait_send()

    for u in range(2):
        k_store(0, u, True).wait()
    for s in range(1, 5):
        for u, r in k_sends(s - 1):
            k_store(s, u, r).wait()
    loop(0, NY, lambda yy: v_store(yy).wait())


def heads_to_rows(ref, i):
    return jnp.concatenate([ref[i, :, h * HD:(h + 1) * HD] for h in range(GRP)], axis=0)


def rows_to_heads(ref, i, rows):
    for h in range(GRP):
        ref[i, :, h * HD:(h + 1) * HD] = rows[h * ROWS:(h + 1) * ROWS]


WIDTH = 2
SPAN = WIDTH * BLK
MOST_UNITS = NP * (NBLK // 2 // WIDTH + 1)


def attend_kernel(
    lists_in, doc_in, q_in, go_in, k_in, v_in, o_out, dq_out, dk_out, dv_out,
    lists_ref, doc_ref, q_ref, go_ref, k_ref, v_ref, o_ref, dq_ref, dk_ref, dv_ref,
    s_ref, dp_ref, o_acc, dq_acc, dk_acc, dv_acc, bounds_ref, top_ref, total_ref, mean_ref, flat_ref,
    load_s, o_s, dq_s, dk_s, dv_s,
):
    _, y, _, z = place()
    rows = GRP * ROWS
    loads = [
        pltpu.make_async_copy(src, dst, load_s.at[n])
        for n, (src, dst) in enumerate(((q_in, q_ref), (k_in, k_ref), (go_in, go_ref), (v_in, v_ref)))
    ]
    small = [
        pltpu.make_async_copy(src, dst, load_s.at[n])
        for n, (src, dst) in ((4, (lists_in, lists_ref)), (5, (doc_in, doc_ref)))
    ]
    for load in small + loads:
        load.start()

    def o_store(g):
        return pltpu.make_async_copy(o_ref.at[g], o_out.at[g], o_s.at[g])

    def dq_store(g):
        return pltpu.make_async_copy(dq_ref.at[g], dq_out.at[g], dq_s.at[g])

    def dk_store(zz):
        return pltpu.make_async_copy(dk_ref.at[zz], dk_out.at[zz], dk_s.at[zz])

    def dv_store(yy):
        return pltpu.make_async_copy(dv_ref.at[yy], dv_out.at[yy], dv_s.at[yy])

    for ref in (total_ref, mean_ref, o_acc, dq_acc, dk_acc, dv_acc):
        ref[...] = jnp.zeros_like(ref)
    top_ref[...] = jnp.full_like(top_ref, NEG)
    for load in small:
        load.wait()

    def list_group(g, base):
        count = (lists_ref[g, BLK - 1] + WIDTH - 1) // WIDTH

        def put(n):
            flat_ref[base + n] = n * NP + g

        loop(0, count, put)
        return base + count

    units = lax.fori_loop(0, NP, list_group, 0)
    for u in range(UNROLL):
        flat_ref[units + u] = NBLK * NP
    steps = (units + UNROLL - 1) // UNROLL

    lane = lax.broadcasted_iota(jnp.int32, (1, rows), 1)
    for g in range(NP):
        token = BLK * (NY * NC * (g // NC) + NC * y + g % NC) + ROWS * z + lane % ROWS
        start = jnp.zeros((1, rows), jnp.int32)
        end = 0
        for d in range(NDOC):
            end = end + doc_ref[d]
            start = start + jnp.where(token >= end, doc_ref[d], 0)
        bounds_ref[g, 0:1] = start
        bounds_ref[g, 1:2] = token
    key_row = lax.broadcasted_iota(jnp.int32, (BLK, rows), 0)
    nt = (((1,), (1,)), ((), ()))
    tn = (((0,), (0,)), ((), ()))
    for load in loads:
        load.wait()

    def units_of(n):
        out = []
        for u in range(UNROLL):
            entry = flat_ref[n * UNROLL + u]
            g, first = entry % NP, entry // NP * WIDTH
            count = lists_ref[g, BLK - 1]
            parts = []
            for w in range(WIDTH):
                live = first + w < count
                b = lists_ref[g, jnp.where(live, first + w, 0)]
                parts.append((live, b, (b // NC) % NY, (b // (NY * NC)) * NC + b % NC))
            out.append((n * UNROLL + u, g, parts))
        return out

    def keys_at(parts):
        return jnp.concatenate([k_ref[:, yb, ib].reshape(BLK, HD) for _, _, yb, ib in parts], axis=0)

    def values_at(parts):
        return jnp.concatenate([v_ref[yb, :, ib].reshape(BLK, HD) for _, _, yb, ib in parts], axis=0)

    def fold(x):
        return x.reshape(x.shape[0] // 8, 8, rows)

    def score_step(n):
        for t, g, parts in units_of(n):
            scores = lax.dot_general(keys_at(parts), heads_to_rows(q_ref, g), nt, preferred_element_type=F32)
            dp_ref[t] = lax.dot_general(values_at(parts), heads_to_rows(go_ref, g), nt, preferred_element_type=F32)
            top = top_ref[g]
            for w, (live, b, _, _) in enumerate(parts):
                low = jnp.where(live, bounds_ref[g, 0:1] - BLK * b, BLK)
                allowed = (key_row >= low) & (key_row <= bounds_ref[g, 1:2] - BLK * b)
                part = jnp.where(allowed, scores[w * BLK:(w + 1) * BLK], NEG)
                s_ref[t, w * BLK:(w + 1) * BLK] = part
                top = jnp.maximum(top, jnp.max(fold(part), axis=0))
            top_ref[g] = top

    loop(0, steps, score_step)
    for g in range(NP):
        top_ref[g] = jnp.broadcast_to(jnp.max(top_ref[g], axis=0, keepdims=True), (8, rows))

    def out_step(n):
        for t, g, parts in units_of(n):
            weights = jnp.exp2((s_ref[t] - top_ref[g, 0:1]) * EXP2_SCALE)
            s_ref[t] = weights
            total_ref[g] += jnp.sum(fold(weights), axis=0)
            mean_ref[g] += jnp.sum(fold(weights * dp_ref[t]), axis=0)
            o_acc[g] += lax.dot_general(values_at(parts), weights.astype(BF), tn, preferred_element_type=F32)

    loop(0, steps, out_step)
    for g in range(NP):
        inverse = 1.0 / jnp.sum(total_ref[g], axis=0, keepdims=True)
        total_ref[g, 0:1] = inverse
        mean_ref[g, 0:1] = jnp.sum(mean_ref[g], axis=0, keepdims=True) * inverse
        rows_to_heads(o_ref, g, (o_acc[g] * inverse).astype(BF).T)
        o_store(g).start()

    def grad_step(n):
        for t, g, parts in units_of(n):
            probs = s_ref[t] * total_ref[g, 0:1]
            grad_scores = (probs * (dp_ref[t] - mean_ref[g, 0:1])).astype(BF)
            dv = jnp.dot(probs.astype(BF), heads_to_rows(go_ref, g), preferred_element_type=F32)
            dk = jnp.dot(grad_scores, heads_to_rows(q_ref, g), preferred_element_type=F32)
            dq_acc[g] += lax.dot_general(keys_at(parts), grad_scores, tn, preferred_element_type=F32)
            for w, (_, _, yb, ib) in enumerate(parts):
                dv_acc[yb, :, ib] += dv[w * BLK:(w + 1) * BLK].reshape(NZ, ROWS, HD)
                dk_acc[:, yb, ib] += dk[w * BLK:(w + 1) * BLK].reshape(NZ, ROWS, HD)

    loop(0, steps, grad_step)

    def finish_k(zz):
        dk_ref[zz] = (dk_acc[zz] * SCALE).astype(BF)
        dk_store(zz).start()

    def finish_v(yy):
        dv_ref[yy] = dv_acc[yy].astype(BF)
        dv_store(yy).start()

    loop(0, NZ, finish_k)
    loop(0, NY, finish_v)
    for g in range(NP):
        rows_to_heads(dq_ref, g, (dq_acc[g] * SCALE).astype(BF).T)
        dq_store(g).start()
    for g in range(NP):
        o_store(g).wait()
        dq_store(g).wait()
    loop(0, NZ, lambda zz: dk_store(zz).wait())
    loop(0, NY, lambda yy: dv_store(yy).wait())


def scatter_kernel(
    o_ref, dq_ref, dk_hbm, dv_ref,
    ao_ref, dqx, k_in, v_in,
    dk_ref, dv_own, kr_out, kl_out, kr_in, kl_in, va_out, va_in, vb_out, vb_in, k_out, vy_in, v_out,
    o_s, o_r, q_s, q_r, kzr_s, kzr_r, kzl_s, kzl_r, va_s, va_r, vb_s, vb_r,
    vy_s, vy_r, k_s, k_r, v_s, v_r, own_s,
):
    x, y, c, z = place()
    me = NC * x + c
    dk_load = pltpu.make_async_copy(dk_hbm, dk_ref, own_s.at[2])
    dv_load = pltpu.make_async_copy(dv_ref.at[y], dv_own, own_s.at[3])
    dk_load.start()
    dv_load.start()
    vy_in[:, :, NP - NC:] = jnp.zeros((NY, NZ, NC, ROWS, HD), BF)
    barrier = enter(me, x, y, c, z)
    pl.semaphore_wait(barrier, N_PARTNERS)

    def each_peer(fn):
        loop(1, NP, lambda d: fn((me + d) % NP))

    def along(off):
        return device(x, y, c, (z + off + NZ) % NZ)

    def head_cols(ref, g):
        return ref.at[:, pl.ds(pl.multiple_of(g * WIDE, WIDE), WIDE)]

    def o_copy(p, slot):
        return remote(o_ref.at[p], head_cols(ao_ref, slot), o_s, o_r, peer(p, y, z))

    def q_copy(p, slot):
        return remote(dq_ref.at[p], dqx.at[slot], q_s, q_r, peer(p, y, z))

    def vy_send(off, d):
        zz, yy = (z + off + NZ) % NZ, (y + d) % NY

        def start(n):
            part = pl.ds(0, n)
            remote(
                dv_ref.at[yy, zz, part], vy_in.at[y, zz, part], vy_s.at[d], vy_r.at[NY - d, zz], device(x, yy, c, z)
            ).start()

        by_reach(yy > y, start)

    def vy_arrive(zz, d):
        yy = (y + d) % NY
        by_reach(y > yy, lambda n: settle(vy_in.at[yy, zz, pl.ds(0, n)], vy_r.at[d, zz]))

    half = NY // 2

    def k_ring(s, u, rightward):
        if rightward:
            return remote(kr_out.at[s, u], kr_in.at[s, u], kzr_s.at[s, u], kzr_r.at[s, u], along(1))
        return remote(kl_out.at[s, u], kl_in.at[s, u], kzl_s.at[s, u], kzl_r.at[s, u], along(-1))

    def k_part(zz, u):
        return dk_ref[zz, u * half:(u + 1) * half].astype(F32)

    def k_send(s, u, rightward):
        zz = (z + 4 - s) % NZ if rightward else (z + 4 + s) % NZ
        total = k_part(zz, u)
        if s > 1 or (s == 1 and (u == 0) == rightward):
            k_ring(s - 1, u, rightward).wait_recv()
            total = total + (kr_in if rightward else kl_in)[s - 1, u].astype(F32)
        (kr_out if rightward else kl_out)[s, u] = total.astype(BF)
        k_ring(s, u, rightward).start()

    def v_part(off):
        zz = (z + off + NZ) % NZ
        total = dv_own[zz].astype(F32)
        for d in range(1, NY):
            vy_arrive(zz, d)
            total = total + vy_in[(y + d) % NY, zz].astype(F32)
        return total

    cut = NP // 2

    def v_far(j):
        hop = (1, -1, 2, -2)[j]
        if j < 2:
            return remote(va_out.at[j], va_in.at[j], va_s.at[j], va_r.at[j], along(hop))
        part = pl.ds(0 if j == 2 else cut, cut)
        return remote(va_out.at[2, part], va_in.at[2, part], va_s.at[j], va_r.at[j], along(hop))

    near = (1, -1, 2, -2)

    def v_near(j):
        return remote(vb_out.at[j], vb_in.at[j], vb_s.at[j], vb_r.at[j], along(near[j]))

    order = (3, -3, 4, 2, -2, 1, -1, 0)
    for off in order[:3]:
        for d in (2, 1, 3):
            vy_send(off, d)
    dk_load.wait()
    k_send(0, 0, True)
    k_send(0, 1, False)
    k_send(1, 1, True)
    k_send(1, 0, False)
    for off in order[3:]:
        for d in (2, 1, 3):
            vy_send(off, d)
    each_peer(lambda p: o_copy(p, me).start())
    each_peer(lambda p: q_copy(p, me).start())
    own_o = pltpu.make_async_copy(o_ref.at[me], head_cols(ao_ref, me), own_s.at[0])
    own_q = pltpu.make_async_copy(dq_ref.at[me], dqx.at[me], own_s.at[1])
    own_o.start()
    own_q.start()

    dv_load.wait()
    k_send(1, 0, True)
    k_send(1, 1, False)
    va_out[0] = v_part(3).astype(BF)
    v_far(0).start()
    va_out[1] = v_part(-3).astype(BF)
    v_far(1).start()
    for u, r in ((1, True), (0, False), (0, True), (1, False)):
        k_send(2, u, r)
    va_out[2] = v_part(4).astype(BF)
    v_far(2).start()
    v_far(3).start()
    for u, r in ((1, True), (0, False), (0, True), (1, False)):
        k_send(3, u, r)
    v_two = [v_part(2), v_part(-2)]
    for j in range(2):
        v_far(j).wait_recv()
        v_far(j + 2).wait_recv()
        total = v_two[j] + va_in[j].astype(F32)
        low, high = total[:cut], total[cut:]
        if j == 0:
            low = low + va_in[2, :cut].astype(F32)
        else:
            high = high + va_in[2, cut:].astype(F32)
        vb_out[j + 2, :cut] = low.astype(BF)
        vb_out[j + 2, cut:] = high.astype(BF)
        v_near(j + 2).start()
    for j in range(2):
        vb_out[j] = v_part(near[j]).astype(BF)
        v_near(j).start()

    def k_copy(e, far):
        p, yy = (me + e % NP) % NP, (y + e // NP) % NY
        return remote(k_out.at[yy, p], k_in.at[y, me], k_s.at[far], k_r.at[far], peer(p, yy, z))

    def v_copy(p, slot):
        return remote(v_out.at[p], v_in.at[slot], v_s, v_r, peer(p, y, z))

    for u in range(2):
        k_ring(3, u, True).wait_recv()
        k_ring(3, u, False).wait_recv()
        total = k_part(z, u) + kr_in[3, u].astype(F32) + kl_in[3, u].astype(F32)
        k_out[u * half:(u + 1) * half] = total.astype(BF)
    loop(1, NP, lambda e: k_copy(e, 0).start())
    loop(NP, NP * NY, lambda e: k_copy(e, 1).start())

    own_k = pltpu.make_async_copy(k_out.at[y, me], k_in.at[y, me], own_s.at[5])
    own_k.start()
    v_total = v_part(0)
    for j in range(4):
        v_near(j).wait_recv()
        v_total = v_total + vb_in[j].astype(F32)
    v_out[...] = v_total.astype(BF)
    each_peer(lambda p: v_copy(p, me).start())
    own_v = pltpu.make_async_copy(v_out.at[me], v_in.at[me], own_s.at[4])
    own_v.start()

    settle(v_in.at[pl.ds(0, NP - 1)], v_r)
    settle(o_ref.at[pl.ds(0, NP - 1)], o_r)
    settle(dqx.at[pl.ds(0, NP - 1)], q_r)
    own_o.wait()
    own_q.wait()
    own_v.wait()
    own_k.wait()

    settle(o_ref.at[pl.ds(0, NP - 1)], o_s)
    settle(dq_ref.at[pl.ds(0, NP - 1)], q_s)
    settle(v_out.at[pl.ds(0, NP - 1)], v_s)
    settle(k_out.at[0, pl.ds(0, NP - 1)], k_s.at[0])
    settle(k_out.at[pl.ds(0, NY - 1)], k_s.at[1])
    for d in range(1, NY):
        by_reach((y + d) % NY > y, lambda n: settle(dv_ref.at[y, :, pl.ds(0, n)], vy_s.at[d]))
    for s in range(4):
        for u in range(2):
            for r in (True, False):
                if s or (u == 0) == r:
                    k_ring(s, u, r).wait_send()
    for j in range(4):
        v_far(j).wait_send()
        v_near(j).wait_send()
    settle(k_in.at[0, pl.ds(0, NP - 1)], k_r.at[0])
    settle(k_in.at[pl.ds(0, NY - 1)], k_r.at[1])


def finish_kernel(
    ao_ref, dq_ref, k_ref, v_ref, cs_ref, sidx_ref, stab_ref,
    ao_out, gq_out, gk_out, gv_out,
    gq_ref, gk_ref, gv_ref, sems, gq_s,
):
    block = lax.axis_index("ctx")
    ao_store, gk_store, gv_store = [
        pltpu.make_async_copy(src, dst, sems.at[n])
        for n, (src, dst) in enumerate(((ao_ref, ao_out), (gk_ref, gk_out), (gv_ref, gv_out)))
    ]
    ao_store.start()

    def store(p):
        cols = pl.ds(pl.multiple_of(p * WIDE, WIDE), WIDE)
        return pltpu.make_async_copy(gq_ref.at[:, cols], gq_out.at[:, cols], gq_s.at[p])

    cosine, sine = cs_ref[0], -cs_ref[1]

    def rotate_back(p):
        for h in range(GRP):
            cols = pl.ds(pl.multiple_of(p * WIDE + h * HD, HD), HD)
            gq_ref[:, cols] = turn(dq_ref[p, :, h * HD:(h + 1) * HD].astype(F32), cosine, sine).astype(BF)
        store(p).start()

    loop(0, NP, rotate_back)
    for h in range(NP):
        cols = slice(h * HD, (h + 1) * HD)
        value_scale = stab_ref[1, sidx_ref[1, h, block]]
        gv_ref[:, cols] = (v_ref[h].astype(F32) * value_scale).astype(BF)
        key_scale = stab_ref[0, sidx_ref[0, h, block]]
        total = k_ref[0, h].astype(F32)
        for yy in range(1, NY):
            total = total + k_ref[yy, h].astype(F32)
        gk_ref[:, cols] = (turn(total, cosine, sine) * key_scale).astype(BF)
    gv_store.start()
    gk_store.start()
    ao_store.wait()
    loop(0, NP, lambda p: store(p).wait())
    gv_store.wait()
    gk_store.wait()


def body(queries, keys, values, grad_out, doc_lengths, block_pairs, scale_index, scale_table):
    half = np.arange(HD // 2, dtype=np.float32) * np.float32(-2.0 * math.log(500000.0) / HD)
    freq = np.exp(half.astype(np.float32)).astype(np.float32)
    freq = jnp.asarray(np.tile(np.concatenate([freq, freq])[None], (8, 1)))
    scale_by_head = scale_index.transpose(0, 2, 1)
    vmem = pl.BlockSpec(memory_space=pltpu.VMEM)
    anywhere = pl.BlockSpec(memory_space=pl.ANY)
    smem = pl.BlockSpec(memory_space=pltpu.SMEM)
    dma = pltpu.SemaphoreType.DMA
    shape = jax.ShapeDtypeStruct
    qx, gox, ka, va, lists, cs = pl.pallas_call(
        gather_kernel,
        name="gather",
        out_shape=(
            shape((NP, ROWS, WIDE), BF),
            shape((NP, ROWS, WIDE), BF),
            shape((NZ, NY, NP, ROWS, HD), BF),
            shape((NY, NZ, NP, ROWS, HD), BF),
            shape((NP, BLK), jnp.int32),
            shape((2, ROWS, HD), F32),
        ),
        in_specs=[anywhere] * 9,
        out_specs=(anywhere,) * 6,
        scratch_shapes=[
            pltpu.VMEM((ROWS, NP * HD), BF),
            pltpu.VMEM((ROWS, NP * HD), BF),
            pltpu.SMEM(doc_lengths.shape, jnp.int32),
            pltpu.VMEM(block_pairs.shape[::-1], jnp.int32),
            pltpu.SMEM(scale_by_head.shape, jnp.int32),
            pltpu.SMEM(scale_table.shape, F32),
            pltpu.VMEM(freq.shape, F32),
            pltpu.VMEM((NP, BLK), jnp.int32),
            pltpu.VMEM((2, ROWS, HD), F32),
            pltpu.VMEM((ROWS, NP * WIDE), BF),
            pltpu.VMEM((NP, ROWS, WIDE), BF),
            pltpu.VMEM((NP, ROWS, HD), BF),
            pltpu.VMEM((NP, ROWS, HD), BF),
            pltpu.VMEM((NZ, NY, NP, ROWS, HD), BF),
            pltpu.VMEM((NY, NZ, NP, ROWS, HD), BF),
        ]
        + [dma] * 4
        + [dma((2,))] * 2
        + [dma] * 2
        + [dma((4, 2))] * 4
        + [dma((4,))] * 4
        + [dma((NY,)), dma((NY,))]
        + [dma((5,)), dma((5, 2, 2)), dma((NY,)), dma((7,))],
        compiler_params=pltpu.CompilerParams(
            collective_id=0, has_side_effects=True, vmem_limit_bytes=VMEM_LIMIT
        ),
    )(queries, keys, values, grad_out, doc_lengths, block_pairs.T, scale_by_head, scale_table, freq)

    o, dq, dk, dv = pl.pallas_call(
        attend_kernel,
        name="attend",
        out_shape=(
            shape((NP, ROWS, WIDE), BF),
            shape((NP, ROWS, WIDE), BF),
            shape((NZ, NY, NP, ROWS, HD), BF),
            shape((NY, NZ, NP, ROWS, HD), BF),
        ),
        in_specs=[anywhere] * 6,
        out_specs=(anywhere,) * 4,
        scratch_shapes=[pltpu.SMEM((NP, BLK), jnp.int32), pltpu.SMEM(doc_lengths.shape, jnp.int32)]
        + ([pltpu.VMEM((NP, ROWS, WIDE), BF)] * 2
        + [pltpu.VMEM((NZ, NY, NP, ROWS, HD), BF), pltpu.VMEM((NY, NZ, NP, ROWS, HD), BF)]) * 2
        + [pltpu.VMEM((MOST_UNITS + UNROLL, SPAN, GRP * ROWS), F32)] * 2
        + [pltpu.VMEM((NP, HD, GRP * ROWS), F32)] * 2
        + [pltpu.VMEM((NZ, NY, NP, ROWS, HD), F32), pltpu.VMEM((NY, NZ, NP, ROWS, HD), F32)]
        + [pltpu.VMEM((NP, 8, GRP * ROWS), jnp.int32)]
        + [pltpu.VMEM((NP, 8, GRP * ROWS), F32)] * 3
        + [pltpu.SMEM((MOST_UNITS + UNROLL,), jnp.int32)]
        + [dma((6,)), dma((NP,)), dma((NP,)), dma((NZ,)), dma((NY,))],
        compiler_params=pltpu.CompilerParams(vmem_limit_bytes=VMEM_LIMIT),
    )(lists, doc_lengths, qx, gox, ka, va)

    ao, dqx, k_terms, v_sums = pl.pallas_call(
        scatter_kernel,
        name="scatter",
        out_shape=(
            shape((ROWS, NP * WIDE), BF),
            shape((NP, ROWS, WIDE), BF),
            shape((NY, NP, ROWS, HD), BF),
            shape((NP, ROWS, HD), BF),
        ),
        in_specs=[anywhere] * 4,
        out_specs=(anywhere,) * 4,
        scratch_shapes=[pltpu.VMEM((NZ, NY, NP, ROWS, HD), BF), pltpu.VMEM((NZ, NP, ROWS, HD), BF)]
        + [pltpu.VMEM((4, 2, NY // 2, NP, ROWS, HD), BF)] * 4
        + [pltpu.VMEM((3, NP, ROWS, HD), BF)] * 2
        + [pltpu.VMEM((4, NP, ROWS, HD), BF)] * 2
        + [pltpu.VMEM((NY, NP, ROWS, HD), BF)]
        + [pltpu.VMEM((NY, NZ, NP, ROWS, HD), BF)]
        + [pltpu.VMEM((NP, ROWS, HD), BF)]
        + [dma] * 4
        + [dma((4, 2))] * 4
        + [dma((4,))] * 4
        + [dma((NY,)), dma((NY, NZ))]
        + [dma((2,))] * 2
        + [dma] * 2
        + [dma((6,))],
        compiler_params=pltpu.CompilerParams(
            collective_id=1, has_side_effects=True, vmem_limit_bytes=VMEM_LIMIT
        ),
    )(o, dq, dk, dv)

    return pl.pallas_call(
        finish_kernel,
        name="finish",
        out_shape=(
            shape((ROWS, NP * WIDE), BF),
            shape((ROWS, NP * WIDE), BF),
            shape((ROWS, NP * HD), BF),
            shape((ROWS, NP * HD), BF),
        ),
        in_specs=[vmem] * 5 + [smem] * 2,
        out_specs=(anywhere,) * 4,
        scratch_shapes=[
            pltpu.VMEM((ROWS, NP * WIDE), BF),
            pltpu.VMEM((ROWS, NP * HD), BF),
            pltpu.VMEM((ROWS, NP * HD), BF),
            dma((3,)),
            dma((NP,)),
        ],
        compiler_params=pltpu.CompilerParams(vmem_limit_bytes=VMEM_LIMIT),
    )(ao, dqx, k_terms, v_sums, cs, scale_by_head, scale_table)


def solution(mesh):
    rows = P(("ctx", "head"), None)
    in_specs = (rows,) * 4 + (P(),) * 4
    return jax.shard_map(body, mesh=mesh, in_specs=in_specs, out_specs=(rows,) * 4, check_vma=False)
```

```python
import functools
import math

import jax
import jax.numpy as jnp
import numpy as np
from jax import lax
from jax.experimental import pallas as pl
from jax.experimental.pallas import tpu as pltpu
from jax.sharding import PartitionSpec as P

HD = 128
BLK = 128
ROWS = 16
GRP = 16
NX, NY, NC, NZ = 4, 4, 2, 8
NP = NX * NC
NBLK = 32
NDOC = 8
WIDE = GRP * HD
NEG = -1e30
SUB = 4
UNROLL = 7
SCALE = 1.0 / math.sqrt(HD)
EXP2_SCALE = SCALE * math.log2(math.e)
MESH = pl.DeviceIdType.MESH
BF = jnp.bfloat16
F32 = jnp.float32
VMEM_LIMIT = 56 * 1024 * 1024


def place():
    ctx = lax.axis_index("ctx")
    return ctx // (NY * NC), (ctx // NC) % NY, ctx % NC, lax.axis_index("head")


def device(xx, yy, cc, zz):
    return {"ctx": xx * (NY * NC) + yy * NC + cc, "head": zz}


def peer(p, y, z):
    return device(p // NC, y, p % NC, z)


def remote(src, dst, send_sem, recv_sem, dev):
    return pltpu.make_async_remote_copy(
        src_ref=src, dst_ref=dst, send_sem=send_sem, recv_sem=recv_sem, device_id=dev, device_id_type=MESH
    )


def enter(me, x, y, c, z):
    barrier = pltpu.get_barrier_semaphore()

    def greet(dev):
        pl.semaphore_signal(barrier, inc=1, device_id=dev, device_id_type=MESH)

    for off in (2, NZ - 2, 1, NZ - 1):
        greet(device(x, y, c, (z + off) % NZ))

    def step(e, carry):
        greet(peer((me + e % NP) % NP, (y + e // NP) % NY, z))
        return carry

    lax.fori_loop(1, NP * NY, step, 0)
    return barrier


N_PARTNERS = NP * NY - 1 + 4


def loop(lo, hi, fn):
    def step(i, carry):
        fn(i)
        return carry

    lax.fori_loop(lo, hi, step, 0)


def by_reach(less, fn):
    pl.when(less)(lambda: fn(NP - NC))
    pl.when(jnp.logical_not(less))(lambda: fn(NP))


def settle(ref, sem):
    pltpu.make_async_copy(ref, ref, sem).wait()


def turn(x, cosine, sine):
    return x * cosine + pltpu.roll(x, HD // 2, 1) * sine


def gather_kernel(
    q_ref, k_hbm, v_hbm, go_ref, doc_hbm, pairs_hbm, sidx_hbm, stab_hbm, freq_hbm,
    qx_ref, gox_ref, ka_out, va_out, lists_out, cs_out,
    k_ref, v_ref, doc_ref, pairs_ref, sidx_ref, stab_ref, freq_ref, lists_ref, cs_ref, q_in, qs, ks, vs, ka_ref, va_ref,
    q_s, q_r, go_s, go_r, k_s, k_r, v_s, v_r, kzr_s, kzr_r, kzl_s, kzl_r,
    va_s, va_r, vb_s, vb_r, vy_s, vy_r, own_s, kout_s, vout_s, load_s,
):
    x, y, c, z = place()
    me = NC * x + c
    block = lax.axis_index("ctx")
    va_ref[:, :, NP - NC:] = jnp.zeros((NY, NZ, NC, ROWS, HD), BF)
    loads = [
        pltpu.make_async_copy(src, dst, load_s.at[n])
        for n, (src, dst) in enumerate((
            (doc_hbm, doc_ref), (freq_hbm, freq_ref), (k_hbm, k_ref), (v_hbm, v_ref),
            (sidx_hbm, sidx_ref), (stab_hbm, stab_ref), (pairs_hbm, pairs_ref),
        ))
    ]
    for load in loads:
        load.start()
    q_load = pltpu.make_async_copy(q_ref, q_in, own_s.at[0])
    q_load.start()
    barrier = enter(me, x, y, c, z)
    for load in loads:
        load.wait()

    for h in range(NP):
        value_scale = stab_ref[1, sidx_ref[1, h, block]]
        vs[h] = (v_ref[:, h * HD:(h + 1) * HD].astype(F32) * value_scale).astype(BF)
    va_ref[y, z, me] = vs[me]

    pl.semaphore_wait(barrier, N_PARTNERS)

    def each_peer(fn):
        loop(1, NP, lambda d: fn((me + d) % NP))

    def v_copy(p, slot):
        return remote(vs.at[p], va_ref.at[y, z, slot], v_s, v_r, peer(p, y, z))

    each_peer(lambda p: v_copy(p, me).start())

    token = BLK * block + ROWS * z + lax.broadcasted_iota(jnp.int32, (ROWS, HD), 0)
    start = jnp.zeros((ROWS, HD), jnp.int32)
    end = 0
    for d in range(NDOC):
        end = end + doc_ref[d]
        start = start + jnp.where(token >= end, doc_ref[d], 0)
    angle = (token - start).astype(F32) * freq_ref[0:1, :]
    cosine = jnp.cos(angle)
    sine = jnp.sin(angle)
    sine = jnp.where(lax.broadcasted_iota(jnp.int32, (ROWS, HD), 1) < HD // 2, -sine, sine)
    cs_ref[0] = cosine
    cs_ref[1] = sine
    cs_store = pltpu.make_async_copy(cs_ref, cs_out, own_s.at[3])
    cs_store.start()

    for h in range(NP):
        key_scale = stab_ref[0, sidx_ref[0, h, block]]
        keys = k_ref[:, h * HD:(h + 1) * HD].astype(F32) * key_scale
        ks[h] = turn(keys, cosine, sine).astype(BF)
    ka_ref[z, y, me] = ks[me]

    def rotate_q(p):
        for h in range(GRP):
            cols = pl.ds(pl.multiple_of(p * WIDE + h * HD, HD), HD)
            qs[p, :, h * HD:(h + 1) * HD] = turn(q_in[:, cols].astype(F32), cosine, sine).astype(BF)

    def k_copy(e, far):
        p, yy = (me + e % NP) % NP, (y + e // NP) % NY
        return remote(ks.at[p], ka_ref.at[z, y, me], k_s.at[far], k_r.at[far], peer(p, yy, z))

    def go_cols(p):
        return go_ref.at[:, pl.ds(pl.multiple_of(p * WIDE, WIDE), WIDE)]

    def go_copy(p, slot):
        return remote(go_cols(p), gox_ref.at[slot], go_s, go_r, peer(p, y, z))

    def q_copy(p, slot):
        return remote(qs.at[p], qx_ref.at[slot], q_s, q_r, peer(p, y, z))

    loop(1, NP, lambda e: k_copy(e, 0).start())
    loop(NP, NP * NY, lambda e: k_copy(e, 1).start())
    each_peer(lambda p: go_copy(p, me).start())
    q_load.wait()

    def rotate_and_send(p):
        rotate_q(p)
        q_copy(p, me).start()

    each_peer(rotate_and_send)
    rotate_q(me)
    own_go = pltpu.make_async_copy(go_cols(me), gox_ref.at[me], own_s.at[1])
    own_q = pltpu.make_async_copy(qs.at[me], qx_ref.at[me], own_s.at[2])
    own_go.start()
    own_q.start()

    def along(off):
        return device(x, y, c, (z + off + NZ) % NZ)

    def k_ring(s, u, rightward, sending):
        far = s if sending else s + 1
        zz = (z + NZ - far) % NZ if rightward else (z + far) % NZ
        ref = ka_ref.at[zz, pl.ds(u * (NY // SUB), NY // SUB)]
        if rightward:
            return remote(ref, ref, kzr_s.at[s, u], kzr_r.at[s, u], along(1))
        return remote(ref, ref, kzl_s.at[s, u], kzl_r.at[s, u], along(-1))

    def k_sends(s):
        return [(u, r) for u in range(SUB) for r in (True, False) if s < 3 or (u < SUB // 2) == r]

    def k_store(s, u, rightward):
        zz = (z + NZ - s) % NZ if rightward else (z + s) % NZ
        part = pl.ds(u * (NY // SUB), NY // SUB)
        return pltpu.make_async_copy(
            ka_ref.at[zz, part], ka_out.at[zz, part], kout_s.at[s, u, 0 if rightward else 1]
        )

    def v_store(yy):
        return pltpu.make_async_copy(va_ref.at[yy], va_out.at[yy], vout_s.at[yy])

    first_hops = (1, -1, 2, -2)

    def v_first(j, arriving):
        zz = (z + first_hops[j] + NZ) % NZ if arriving else z
        ref = va_ref.at[y, zz]
        return remote(ref, ref, va_s.at[j], va_r.at[j], along(-first_hops[j]))

    def v_second(j, arriving):
        off, part = ((2, None), (-2, None), (2, 0), (-2, 1))[j]
        hop = -1 if off > 0 else 1
        if part is not None:
            hop = 2 * hop
        zz = (z + off - (hop if arriving else 0) + NZ) % NZ
        ref = va_ref.at[y, zz]
        if part is not None:
            ref = va_ref.at[y, zz, pl.ds(part * (NP // 2), NP // 2)]
        return remote(ref, ref, vb_s.at[j], vb_r.at[j], along(hop))

    def v_spread(zz, d):
        yy = (y + d) % NY

        def start(n):
            ref = va_ref.at[y, zz, pl.ds(0, n)]
            remote(ref, ref, vy_s.at[d], vy_r.at[y], device(x, yy, c, z)).start()

        by_reach(yy < y, start)

    def spread(off):
        for d in (2, 1, 3):
            v_spread((z + off + NZ) % NZ, d)

    settle(va_ref.at[y, z, pl.ds(0, NP - 1)], v_r)
    for j in (2, 3, 0, 1):
        v_first(j, False).start()
    spread(0)
    settle(ka_ref.at[z, 0, pl.ds(0, NP - 1)], k_r.at[0])
    settle(ka_ref.at[z, pl.ds(0, NY - 1)], k_r.at[1])
    for u, r in k_sends(0):
        k_ring(0, u, r, True).start()
    for u in range(SUB):
        k_store(0, u, True).start()

    lane = lax.broadcasted_iota(jnp.int32, (NP, BLK), 1)
    row = lax.broadcasted_iota(jnp.int32, (NP, BLK), 0)
    own_block = NY * NC * (row // NC) + NC * y + row % NC
    first = BLK * own_block + ROWS * z
    doc_start = jnp.zeros((NP, BLK), jnp.int32)
    end = 0
    for d in range(NDOC):
        end = end + doc_ref[d]
        doc_start = doc_start + jnp.where(first >= end, doc_ref[d], 0)
    pairs = pairs_ref[...]
    n_pairs = pairs.shape[1]
    pair_row = lax.broadcasted_iota(jnp.int32, (NP, n_pairs), 0)
    pair_q = (pairs[0:1] == NY * NC * (pair_row // NC) + NC * y + pair_row % NC).astype(F32)
    pair_k = (pairs[1:2] == lax.broadcasted_iota(jnp.int32, (BLK, n_pairs), 0)).astype(F32)
    listed = lax.dot_general(pair_q, pair_k, (((1,), (1,)), ((), ())), preferred_element_type=F32)
    wanted = ((listed > 0.5) | (lane == own_block)) & (BLK * lane + BLK - 1 >= doc_start) & (lane <= own_block)
    wanted_f = wanted.astype(F32)
    upper = (
        lax.broadcasted_iota(jnp.int32, (BLK, BLK), 0) <= lax.broadcasted_iota(jnp.int32, (BLK, BLK), 1)
    ).astype(F32)
    rank = jnp.dot(wanted_f, upper, preferred_element_type=F32)
    lane_f = lane.astype(F32)

    def list_step(r, out):
        hit = wanted & (rank.astype(jnp.int32) == r + 1)
        entry = jnp.sum(jnp.where(hit, lane_f, 0.0), axis=1, keepdims=True)
        return jnp.where(lane == r, entry, out)

    out = lax.fori_loop(0, NBLK, list_step, jnp.zeros((NP, BLK), F32))
    out = jnp.where(lane == BLK - 1, jnp.sum(wanted_f, axis=1, keepdims=True), out)
    lists_ref[...] = out.astype(jnp.int32)
    lists_store = pltpu.make_async_copy(lists_ref, lists_out, own_s.at[4])
    lists_store.start()

    def k_step(s):
        onward = k_sends(s) if s < 4 else []
        for u, r in k_sends(s - 1):
            k_ring(s - 1, u, r, False).wait_recv()
            if (u, r) in onward:
                k_ring(s, u, r, True).start()
            k_store(s, u, r).start()

    for j in (0, 1):
        v_first(j, True).wait_recv()
        spread(first_hops[j])
    for j in (2, 3):
        v_first(j, True).wait_recv()
        v_second(j, False).start()
        v_second(j - 2, False).start()
        spread(first_hops[j])
    k_step(1)
    for j in (0, 1):
        v_second(j, True).wait_recv()
        spread((3, -3)[j])
    for j in (2, 3):
        v_second(j, True).wait_recv()
    spread(4)
    v_store(y).start()
    k_step(2)
    k_step(3)
    k_step(4)

    for d in (1, 3, 2):
        yy = (y + d) % NY
        by_reach(y < yy, lambda n: settle(va_ref.at[yy, :, pl.ds(0, n)], vy_r.at[yy]))
        v_store(yy).start()

    settle(gox_ref.at[pl.ds(0, NP - 1)], go_r)
    settle(qx_ref.at[pl.ds(0, NP - 1)], q_r)
    own_go.wait()
    own_q.wait()
    cs_store.wait()
    lists_store.wait()

    settle(vs.at[pl.ds(0, NP - 1)], v_s)
    settle(go_ref.at[:, pl.ds(0, (NP - 1) * WIDE)], go_s)
    settle(qs.at[pl.ds(0, NP - 1)], q_s)
    settle(ks.at[pl.ds(0, NP - 1)], k_s.at[0])
    settle(ka_ref.at[z, pl.ds(0, NY - 1)], k_s.at[1])
    for d in range(1, NY):
        by_reach((y + d) % NY < y, lambda n: settle(va_ref.at[y, :, pl.ds(0, n)], vy_s.at[d]))
    for s in range(4):
        for u, r in k_sends(s):
            k_ring(s, u, r, True).wait_send()
    for j in range(4):
        v_first(j, False).wait_send()
        v_second(j, False).wait_send()

    for u in range(SUB):
        k_store(0, u, True).wait()
    for s in range(1, 5):
        for u, r in k_sends(s - 1):
            k_store(s, u, r).wait()
    loop(0, NY, lambda yy: v_store(yy).wait())


def heads_to_rows(ref, i):
    return jnp.concatenate([ref[i, :, h * HD:(h + 1) * HD] for h in range(GRP)], axis=0)


def rows_to_heads(ref, i, rows):
    for h in range(GRP):
        ref[i, :, h * HD:(h + 1) * HD] = rows[h * ROWS:(h + 1) * ROWS]


WIDTH = 2
SPAN = WIDTH * BLK
MOST_UNITS = NP * (NBLK // 2 // WIDTH + 1)


def attend_kernel(
    lists_in, doc_in, q_in, go_in, k_in, v_in, o_out, dq_out, dk_out, dv_out,
    lists_ref, doc_ref, q_ref, go_ref, k_ref, v_ref, o_ref, dq_ref, dk_ref, dv_ref,
    s_ref, dp_ref, o_acc, dq_acc, dk_acc, dv_acc, bounds_ref, top_ref, total_ref, mean_ref, flat_ref,
    load_s, o_s, dq_s, dk_s, dv_s,
):
    _, y, _, z = place()
    rows = GRP * ROWS
    loads = [
        pltpu.make_async_copy(src, dst, load_s.at[n])
        for n, (src, dst) in enumerate(((q_in, q_ref), (k_in, k_ref), (go_in, go_ref), (v_in, v_ref)))
    ]
    small = [
        pltpu.make_async_copy(src, dst, load_s.at[n])
        for n, (src, dst) in ((4, (lists_in, lists_ref)), (5, (doc_in, doc_ref)))
    ]
    for load in small + loads:
        load.start()

    def o_store(g):
        return pltpu.make_async_copy(o_ref.at[g], o_out.at[g], o_s.at[g])

    def dq_store(g):
        return pltpu.make_async_copy(dq_ref.at[g], dq_out.at[g], dq_s.at[g])

    def dk_store(zz):
        return pltpu.make_async_copy(dk_ref.at[zz], dk_out.at[zz], dk_s.at[zz])

    def dv_store(yy):
        return pltpu.make_async_copy(dv_ref.at[yy], dv_out.at[yy], dv_s.at[yy])

    for ref in (total_ref, mean_ref, o_acc, dq_acc, dk_acc, dv_acc):
        ref[...] = jnp.zeros_like(ref)
    top_ref[...] = jnp.full_like(top_ref, NEG)
    for load in small:
        load.wait()

    def list_group(g, base):
        count = (lists_ref[g, BLK - 1] + WIDTH - 1) // WIDTH

        def put(n):
            flat_ref[base + n] = n * NP + g

        loop(0, count, put)
        return base + count

    units = lax.fori_loop(0, NP, list_group, 0)
    for u in range(UNROLL):
        flat_ref[units + u] = NBLK * NP
    steps = (units + UNROLL - 1) // UNROLL

    lane = lax.broadcasted_iota(jnp.int32, (1, rows), 1)
    for g in range(NP):
        token = BLK * (NY * NC * (g // NC) + NC * y + g % NC) + ROWS * z + lane % ROWS
        start = jnp.zeros((1, rows), jnp.int32)
        end = 0
        for d in range(NDOC):
            end = end + doc_ref[d]
            start = start + jnp.where(token >= end, doc_ref[d], 0)
        bounds_ref[g, 0:1] = start
        bounds_ref[g, 1:2] = token
    key_row = lax.broadcasted_iota(jnp.int32, (BLK, rows), 0)
    nt = (((1,), (1,)), ((), ()))
    tn = (((0,), (0,)), ((), ()))
    for load in loads:
        load.wait()

    def units_of(n):
        out = []
        for u in range(UNROLL):
            entry = flat_ref[n * UNROLL + u]
            g, first = entry % NP, entry // NP * WIDTH
            count = lists_ref[g, BLK - 1]
            parts = []
            for w in range(WIDTH):
                live = first + w < count
                b = lists_ref[g, jnp.where(live, first + w, 0)]
                parts.append((live, b, (b // NC) % NY, (b // (NY * NC)) * NC + b % NC))
            out.append((n * UNROLL + u, g, parts))
        return out

    def keys_at(parts):
        return jnp.concatenate([k_ref[:, yb, ib].reshape(BLK, HD) for _, _, yb, ib in parts], axis=0)

    def values_at(parts):
        return jnp.concatenate([v_ref[yb, :, ib].reshape(BLK, HD) for _, _, yb, ib in parts], axis=0)

    def fold(x):
        return x.reshape(x.shape[0] // 8, 8, rows)

    def score_step(n):
        for t, g, parts in units_of(n):
            scores = lax.dot_general(keys_at(parts), heads_to_rows(q_ref, g), nt, preferred_element_type=F32)
            dp_ref[t] = lax.dot_general(values_at(parts), heads_to_rows(go_ref, g), nt, preferred_element_type=F32)
            top = top_ref[g]
            for w, (live, b, _, _) in enumerate(parts):
                low = jnp.where(live, bounds_ref[g, 0:1] - BLK * b, BLK)
                allowed = (key_row >= low) & (key_row <= bounds_ref[g, 1:2] - BLK * b)
                part = jnp.where(allowed, scores[w * BLK:(w + 1) * BLK], NEG)
                s_ref[t, w * BLK:(w + 1) * BLK] = part
                top = jnp.maximum(top, jnp.max(fold(part), axis=0))
            top_ref[g] = top

    loop(0, steps, score_step)
    for g in range(NP):
        top_ref[g] = jnp.broadcast_to(jnp.max(top_ref[g], axis=0, keepdims=True), (8, rows))

    def out_step(n):
        for t, g, parts in units_of(n):
            weights = jnp.exp2((s_ref[t] - top_ref[g, 0:1]) * EXP2_SCALE)
            s_ref[t] = weights
            total_ref[g] += jnp.sum(fold(weights), axis=0)
            mean_ref[g] += jnp.sum(fold(weights * dp_ref[t]), axis=0)
            o_acc[g] += lax.dot_general(values_at(parts), weights.astype(BF), tn, preferred_element_type=F32)

    loop(0, steps, out_step)
    for g in range(NP):
        inverse = 1.0 / jnp.sum(total_ref[g], axis=0, keepdims=True)
        total_ref[g, 0:1] = inverse
        mean_ref[g, 0:1] = jnp.sum(mean_ref[g], axis=0, keepdims=True) * inverse
        rows_to_heads(o_ref, g, (o_acc[g] * inverse).astype(BF).T)
        o_store(g).start()

    def grad_step(n):
        for t, g, parts in units_of(n):
            probs = s_ref[t] * total_ref[g, 0:1]
            grad_scores = (probs * (dp_ref[t] - mean_ref[g, 0:1])).astype(BF)
            dv = jnp.dot(probs.astype(BF), heads_to_rows(go_ref, g), preferred_element_type=F32)
            dk = jnp.dot(grad_scores, heads_to_rows(q_ref, g), preferred_element_type=F32)
            dq_acc[g] += lax.dot_general(keys_at(parts), grad_scores, tn, preferred_element_type=F32)
            for w, (_, _, yb, ib) in enumerate(parts):
                dv_acc[yb, :, ib] += dv[w * BLK:(w + 1) * BLK].reshape(NZ, ROWS, HD)
                dk_acc[:, yb, ib] += dk[w * BLK:(w + 1) * BLK].reshape(NZ, ROWS, HD)

    loop(0, steps, grad_step)

    def finish_k(zz):
        dk_ref[zz] = (dk_acc[zz] * SCALE).astype(BF)
        dk_store(zz).start()

    def finish_v(yy):
        dv_ref[yy] = dv_acc[yy].astype(BF)
        dv_store(yy).start()

    loop(0, NZ, finish_k)
    loop(0, NY, finish_v)
    for g in range(NP):
        rows_to_heads(dq_ref, g, (dq_acc[g] * SCALE).astype(BF).T)
        dq_store(g).start()
    for g in range(NP):
        o_store(g).wait()
        dq_store(g).wait()
    loop(0, NZ, lambda zz: dk_store(zz).wait())
    loop(0, NY, lambda yy: dv_store(yy).wait())


def scatter_kernel(
    o_ref, dq_ref, dk_hbm, dv_ref,
    ao_ref, dqx, k_in, v_in,
    dk_ref, dv_own, kr_out, kl_out, kr_in, kl_in, va_out, va_in, vb_out, vb_in, k_out, vy_in, v_out,
    o_s, o_r, q_s, q_r, kzr_s, kzr_r, kzl_s, kzl_r, va_s, va_r, vb_s, vb_r,
    vy_s, vy_r, k_s, k_r, v_s, v_r, own_s,
):
    x, y, c, z = place()
    me = NC * x + c
    dk_load = pltpu.make_async_copy(dk_hbm, dk_ref, own_s.at[2])
    dv_load = pltpu.make_async_copy(dv_ref.at[y], dv_own, own_s.at[3])
    dk_load.start()
    dv_load.start()
    vy_in[:, :, NP - NC:] = jnp.zeros((NY, NZ, NC, ROWS, HD), BF)
    barrier = enter(me, x, y, c, z)
    pl.semaphore_wait(barrier, N_PARTNERS)

    def each_peer(fn):
        loop(1, NP, lambda d: fn((me + d) % NP))

    def along(off):
        return device(x, y, c, (z + off + NZ) % NZ)

    def head_cols(ref, g):
        return ref.at[:, pl.ds(pl.multiple_of(g * WIDE, WIDE), WIDE)]

    def o_copy(p, slot):
        return remote(o_ref.at[p], head_cols(ao_ref, slot), o_s, o_r, peer(p, y, z))

    def q_copy(p, slot):
        return remote(dq_ref.at[p], dqx.at[slot], q_s, q_r, peer(p, y, z))

    def vy_send(off, d):
        zz, yy = (z + off + NZ) % NZ, (y + d) % NY

        def start(n):
            part = pl.ds(0, n)
            remote(
                dv_ref.at[yy, zz, part], vy_in.at[y, zz, part], vy_s.at[d], vy_r.at[NY - d, zz], device(x, yy, c, z)
            ).start()

        by_reach(yy > y, start)

    def vy_arrive(zz, d):
        yy = (y + d) % NY
        by_reach(y > yy, lambda n: settle(vy_in.at[yy, zz, pl.ds(0, n)], vy_r.at[d, zz]))

    part_y = NY // SUB
    early = [(u, u >= SUB // 2) for u in range(SUB)]
    late = [(u, u < SUB // 2) for u in range(SUB)]

    def k_ring(s, u, rightward):
        if rightward:
            return remote(kr_out.at[s, u], kr_in.at[s, u], kzr_s.at[s, u], kzr_r.at[s, u], along(1))
        return remote(kl_out.at[s, u], kl_in.at[s, u], kzl_s.at[s, u], kzl_r.at[s, u], along(-1))

    def k_part(zz, u):
        return dk_ref[zz, u * part_y:(u + 1) * part_y].astype(F32)

    def k_send(s, u, rightward):
        zz = (z + 4 - s) % NZ if rightward else (z + 4 + s) % NZ
        total = k_part(zz, u)
        if s > 1 or (s == 1 and (u < SUB // 2) == rightward):
            k_ring(s - 1, u, rightward).wait_recv()
            total = total + (kr_in if rightward else kl_in)[s - 1, u].astype(F32)
        (kr_out if rightward else kl_out)[s, u] = total.astype(BF)
        k_ring(s, u, rightward).start()

    def v_part(off):
        zz = (z + off + NZ) % NZ
        total = dv_own[zz].astype(F32)
        for d in range(1, NY):
            vy_arrive(zz, d)
            total = total + vy_in[(y + d) % NY, zz].astype(F32)
        return total

    cut = NP // 2

    def v_far(j):
        hop = (1, -1, 2, -2)[j]
        if j < 2:
            return remote(va_out.at[j], va_in.at[j], va_s.at[j], va_r.at[j], along(hop))
        part = pl.ds(0 if j == 2 else cut, cut)
        return remote(va_out.at[2, part], va_in.at[2, part], va_s.at[j], va_r.at[j], along(hop))

    near = (1, -1, 2, -2)

    def v_near(j):
        return remote(vb_out.at[j], vb_in.at[j], vb_s.at[j], vb_r.at[j], along(near[j]))

    order = (3, -3, 4, 2, -2, 1, -1, 0)
    for off in order[:3]:
        for d in (2, 1, 3):
            vy_send(off, d)
    dk_load.wait()
    for u, r in late:
        k_send(0, u, r)
    for u, r in early:
        k_send(1, u, r)
    for off in order[3:]:
        for d in (2, 1, 3):
            vy_send(off, d)
    each_peer(lambda p: o_copy(p, me).start())
    each_peer(lambda p: q_copy(p, me).start())
    own_o = pltpu.make_async_copy(o_ref.at[me], head_cols(ao_ref, me), own_s.at[0])
    own_q = pltpu.make_async_copy(dq_ref.at[me], dqx.at[me], own_s.at[1])
    own_o.start()
    own_q.start()

    dv_load.wait()
    for u, r in late:
        k_send(1, u, r)
    va_out[0] = v_part(3).astype(BF)
    v_far(0).start()
    va_out[1] = v_part(-3).astype(BF)
    v_far(1).start()
    for u, r in early + late:
        k_send(2, u, r)
    va_out[2] = v_part(4).astype(BF)
    v_far(2).start()
    v_far(3).start()
    for u, r in early + late:
        k_send(3, u, r)
    v_two = [v_part(2), v_part(-2)]
    for j in range(2):
        v_far(j).wait_recv()
        v_far(j + 2).wait_recv()
        total = v_two[j] + va_in[j].astype(F32)
        low, high = total[:cut], total[cut:]
        if j == 0:
            low = low + va_in[2, :cut].astype(F32)
        else:
            high = high + va_in[2, cut:].astype(F32)
        vb_out[j + 2, :cut] = low.astype(BF)
        vb_out[j + 2, cut:] = high.astype(BF)
        v_near(j + 2).start()
    for j in range(2):
        vb_out[j] = v_part(near[j]).astype(BF)
        v_near(j).start()

    def k_copy(e, far):
        p, yy = (me + e % NP) % NP, (y + e // NP) % NY
        return remote(k_out.at[yy, p], k_in.at[y, me], k_s.at[far], k_r.at[far], peer(p, yy, z))

    def v_copy(p, slot):
        return remote(v_out.at[p], v_in.at[slot], v_s, v_r, peer(p, y, z))

    for u in range(SUB):
        k_ring(3, u, True).wait_recv()
        k_ring(3, u, False).wait_recv()
        total = k_part(z, u) + kr_in[3, u].astype(F32) + kl_in[3, u].astype(F32)
        k_out[u * part_y:(u + 1) * part_y] = total.astype(BF)
    loop(1, NP, lambda e: k_copy(e, 0).start())
    loop(NP, NP * NY, lambda e: k_copy(e, 1).start())

    own_k = pltpu.make_async_copy(k_out.at[y, me], k_in.at[y, me], own_s.at[5])
    own_k.start()
    v_total = v_part(0)
    for j in range(4):
        v_near(j).wait_recv()
        v_total = v_total + vb_in[j].astype(F32)
    v_out[...] = v_total.astype(BF)
    each_peer(lambda p: v_copy(p, me).start())
    own_v = pltpu.make_async_copy(v_out.at[me], v_in.at[me], own_s.at[4])
    own_v.start()

    settle(v_in.at[pl.ds(0, NP - 1)], v_r)
    settle(o_ref.at[pl.ds(0, NP - 1)], o_r)
    settle(dqx.at[pl.ds(0, NP - 1)], q_r)
    own_o.wait()
    own_q.wait()
    own_v.wait()
    own_k.wait()

    settle(o_ref.at[pl.ds(0, NP - 1)], o_s)
    settle(dq_ref.at[pl.ds(0, NP - 1)], q_s)
    settle(v_out.at[pl.ds(0, NP - 1)], v_s)
    settle(k_out.at[0, pl.ds(0, NP - 1)], k_s.at[0])
    settle(k_out.at[pl.ds(0, NY - 1)], k_s.at[1])
    for d in range(1, NY):
        by_reach((y + d) % NY > y, lambda n: settle(dv_ref.at[y, :, pl.ds(0, n)], vy_s.at[d]))
    for s in range(4):
        for u in range(SUB):
            for r in (True, False):
                if s or (u < SUB // 2) == r:
                    k_ring(s, u, r).wait_send()
    for j in range(4):
        v_far(j).wait_send()
        v_near(j).wait_send()
    settle(k_in.at[0, pl.ds(0, NP - 1)], k_r.at[0])
    settle(k_in.at[pl.ds(0, NY - 1)], k_r.at[1])


def finish_kernel(
    ao_in, dq_in, k_in, v_in, cs_in, sidx_in, stab_in,
    ao_out, gq_out, gk_out, gv_out,
    ao_ref, dq_ref, k_ref, v_ref, cs_ref, sidx_ref, stab_ref,
    gq_ref, gk_ref, gv_ref, sems, gq_s, dq_s, load_s,
):
    block = lax.axis_index("ctx")

    def dq_load(p):
        return pltpu.make_async_copy(dq_in.at[p], dq_ref.at[p], dq_s.at[p])

    cs_load, ao_load, *rest = [
        pltpu.make_async_copy(src, dst, load_s.at[n])
        for n, (src, dst) in enumerate((
            (cs_in, cs_ref), (ao_in, ao_ref), (k_in, k_ref), (v_in, v_ref), (sidx_in, sidx_ref), (stab_in, stab_ref)
        ))
    ]
    cs_load.start()
    loop(0, NP, lambda p: dq_load(p).start())
    ao_load.start()
    for load in rest:
        load.start()
    ao_store, gk_store, gv_store = [
        pltpu.make_async_copy(src, dst, sems.at[n])
        for n, (src, dst) in enumerate(((ao_ref, ao_out), (gk_ref, gk_out), (gv_ref, gv_out)))
    ]

    def store(p):
        cols = pl.ds(pl.multiple_of(p * WIDE, WIDE), WIDE)
        return pltpu.make_async_copy(gq_ref.at[:, cols], gq_out.at[:, cols], gq_s.at[p])

    cs_load.wait()
    cosine, sine = cs_ref[0], -cs_ref[1]

    def rotate_back(p):
        dq_load(p).wait()
        for h in range(GRP):
            cols = pl.ds(pl.multiple_of(p * WIDE + h * HD, HD), HD)
            gq_ref[:, cols] = turn(dq_ref[p, :, h * HD:(h + 1) * HD].astype(F32), cosine, sine).astype(BF)
        store(p).start()

    loop(0, NP // 2, rotate_back)
    ao_load.wait()
    ao_store.start()
    loop(NP // 2, NP, rotate_back)
    for load in rest:
        load.wait()
    for h in range(NP):
        cols = slice(h * HD, (h + 1) * HD)
        value_scale = stab_ref[1, sidx_ref[1, h, block]]
        gv_ref[:, cols] = (v_ref[h].astype(F32) * value_scale).astype(BF)
        key_scale = stab_ref[0, sidx_ref[0, h, block]]
        total = k_ref[0, h].astype(F32)
        for yy in range(1, NY):
            total = total + k_ref[yy, h].astype(F32)
        gk_ref[:, cols] = (turn(total, cosine, sine) * key_scale).astype(BF)
    gv_store.start()
    gk_store.start()
    ao_store.wait()
    loop(0, NP, lambda p: store(p).wait())
    gv_store.wait()
    gk_store.wait()


def body(queries, keys, values, grad_out, doc_lengths, block_pairs, scale_index, scale_table):
    half = np.arange(HD // 2, dtype=np.float32) * np.float32(-2.0 * math.log(500000.0) / HD)
    freq = np.exp(half.astype(np.float32)).astype(np.float32)
    freq = jnp.asarray(np.tile(np.concatenate([freq, freq])[None], (8, 1)))
    scale_by_head = scale_index.transpose(0, 2, 1)
    anywhere = pl.BlockSpec(memory_space=pl.ANY)
    dma = pltpu.SemaphoreType.DMA
    shape = jax.ShapeDtypeStruct
    qx, gox, ka, va, lists, cs = pl.pallas_call(
        gather_kernel,
        name="gather",
        out_shape=(
            shape((NP, ROWS, WIDE), BF),
            shape((NP, ROWS, WIDE), BF),
            shape((NZ, NY, NP, ROWS, HD), BF),
            shape((NY, NZ, NP, ROWS, HD), BF),
            shape((NP, BLK), jnp.int32),
            shape((2, ROWS, HD), F32),
        ),
        in_specs=[anywhere] * 9,
        out_specs=(anywhere,) * 6,
        scratch_shapes=[
            pltpu.VMEM((ROWS, NP * HD), BF),
            pltpu.VMEM((ROWS, NP * HD), BF),
            pltpu.SMEM(doc_lengths.shape, jnp.int32),
            pltpu.VMEM(block_pairs.shape[::-1], jnp.int32),
            pltpu.SMEM(scale_by_head.shape, jnp.int32),
            pltpu.SMEM(scale_table.shape, F32),
            pltpu.VMEM(freq.shape, F32),
            pltpu.VMEM((NP, BLK), jnp.int32),
            pltpu.VMEM((2, ROWS, HD), F32),
            pltpu.VMEM((ROWS, NP * WIDE), BF),
            pltpu.VMEM((NP, ROWS, WIDE), BF),
            pltpu.VMEM((NP, ROWS, HD), BF),
            pltpu.VMEM((NP, ROWS, HD), BF),
            pltpu.VMEM((NZ, NY, NP, ROWS, HD), BF),
            pltpu.VMEM((NY, NZ, NP, ROWS, HD), BF),
        ]
        + [dma] * 4
        + [dma((2,))] * 2
        + [dma] * 2
        + [dma((4, SUB))] * 4
        + [dma((4,))] * 4
        + [dma((NY,)), dma((NY,))]
        + [dma((5,)), dma((5, SUB, 2)), dma((NY,)), dma((7,))],
        compiler_params=pltpu.CompilerParams(
            collective_id=0, has_side_effects=True, vmem_limit_bytes=VMEM_LIMIT
        ),
    )(queries, keys, values, grad_out, doc_lengths, block_pairs.T, scale_by_head, scale_table, freq)

    o, dq, dk, dv = pl.pallas_call(
        attend_kernel,
        name="attend",
        out_shape=(
            shape((NP, ROWS, WIDE), BF),
            shape((NP, ROWS, WIDE), BF),
            shape((NZ, NY, NP, ROWS, HD), BF),
            shape((NY, NZ, NP, ROWS, HD), BF),
        ),
        in_specs=[anywhere] * 6,
        out_specs=(anywhere,) * 4,
        scratch_shapes=[pltpu.SMEM((NP, BLK), jnp.int32), pltpu.SMEM(doc_lengths.shape, jnp.int32)]
        + ([pltpu.VMEM((NP, ROWS, WIDE), BF)] * 2
        + [pltpu.VMEM((NZ, NY, NP, ROWS, HD), BF), pltpu.VMEM((NY, NZ, NP, ROWS, HD), BF)]) * 2
        + [pltpu.VMEM((MOST_UNITS + UNROLL, SPAN, GRP * ROWS), F32)] * 2
        + [pltpu.VMEM((NP, HD, GRP * ROWS), F32)] * 2
        + [pltpu.VMEM((NZ, NY, NP, ROWS, HD), F32), pltpu.VMEM((NY, NZ, NP, ROWS, HD), F32)]
        + [pltpu.VMEM((NP, 8, GRP * ROWS), jnp.int32)]
        + [pltpu.VMEM((NP, 8, GRP * ROWS), F32)] * 3
        + [pltpu.SMEM((MOST_UNITS + UNROLL,), jnp.int32)]
        + [dma((6,)), dma((NP,)), dma((NP,)), dma((NZ,)), dma((NY,))],
        compiler_params=pltpu.CompilerParams(vmem_limit_bytes=VMEM_LIMIT),
    )(lists, doc_lengths, qx, gox, ka, va)

    ao, dqx, k_terms, v_sums = pl.pallas_call(
        scatter_kernel,
        name="scatter",
        out_shape=(
            shape((ROWS, NP * WIDE), BF),
            shape((NP, ROWS, WIDE), BF),
            shape((NY, NP, ROWS, HD), BF),
            shape((NP, ROWS, HD), BF),
        ),
        in_specs=[anywhere] * 4,
        out_specs=(anywhere,) * 4,
        scratch_shapes=[pltpu.VMEM((NZ, NY, NP, ROWS, HD), BF), pltpu.VMEM((NZ, NP, ROWS, HD), BF)]
        + [pltpu.VMEM((4, SUB, NY // SUB, NP, ROWS, HD), BF)] * 4
        + [pltpu.VMEM((3, NP, ROWS, HD), BF)] * 2
        + [pltpu.VMEM((4, NP, ROWS, HD), BF)] * 2
        + [pltpu.VMEM((NY, NP, ROWS, HD), BF)]
        + [pltpu.VMEM((NY, NZ, NP, ROWS, HD), BF)]
        + [pltpu.VMEM((NP, ROWS, HD), BF)]
        + [dma] * 4
        + [dma((4, SUB))] * 4
        + [dma((4,))] * 4
        + [dma((NY,)), dma((NY, NZ))]
        + [dma((2,))] * 2
        + [dma] * 2
        + [dma((6,))],
        compiler_params=pltpu.CompilerParams(
            collective_id=1, has_side_effects=True, vmem_limit_bytes=VMEM_LIMIT
        ),
    )(o, dq, dk, dv)

    return pl.pallas_call(
        finish_kernel,
        name="finish",
        out_shape=(
            shape((ROWS, NP * WIDE), BF),
            shape((ROWS, NP * WIDE), BF),
            shape((ROWS, NP * HD), BF),
            shape((ROWS, NP * HD), BF),
        ),
        in_specs=[anywhere] * 7,
        out_specs=(anywhere,) * 4,
        scratch_shapes=[
            pltpu.VMEM((ROWS, NP * WIDE), BF),
            pltpu.VMEM((NP, ROWS, WIDE), BF),
            pltpu.VMEM((NY, NP, ROWS, HD), BF),
            pltpu.VMEM((NP, ROWS, HD), BF),
            pltpu.VMEM((2, ROWS, HD), F32),
            pltpu.SMEM(scale_by_head.shape, jnp.int32),
            pltpu.SMEM(scale_table.shape, F32),
            pltpu.VMEM((ROWS, NP * WIDE), BF),
            pltpu.VMEM((ROWS, NP * HD), BF),
            pltpu.VMEM((ROWS, NP * HD), BF),
            dma((3,)),
            dma((NP,)),
            dma((NP,)),
            dma((6,)),
        ],
        compiler_params=pltpu.CompilerParams(vmem_limit_bytes=VMEM_LIMIT),
    )(ao, dqx, k_terms, v_sums, cs, scale_by_head, scale_table)


def solution(mesh):
    rows = P(("ctx", "head"), None)
    in_specs = (rows,) * 4 + (P(),) * 4
    return jax.shard_map(body, mesh=mesh, in_specs=in_specs, out_specs=(rows,) * 4, check_vma=False)
```
